128 devices in a mesh: lat: 16 (over y_lo, z, core), lon: 8 (over x, y_hi).
Axes of the slice: x: 4, y: 4 (y_hi: 2, y_lo: 2; y = y_hi * 2 + y_lo), z: 4, core: 2. Of those that a mesh axis runs over, the one named last changes fastest.
Arguments:
- tokens: bfloat16 [2, 192, 384, 512], P(None, 'lat', 'lon'), may hold values from -6 to 6
- region: int32 [192, 384], P('lat', 'lon'), may hold values from 0 to 3
- w_qkv: bfloat16 [512, 1536], replicated, may hold values from -0.25 to 0.25
- w_proj: bfloat16 [512, 512], replicated, may hold values from -0.25 to 0.25
- w_merge: bfloat16 [2048, 1024], replicated, may hold values from -0.125 to 0.125
- d_merged: bfloat16 [2, 96, 192, 1024], P(None, 'lat', None, 'lon'), may hold values from -6 to 6
Outputs:
- merged: bfloat16 [2, 96, 192, 1024], P(None, 'lat', None, 'lon')
- grad_x: float32 [2, 192, 384, 512], P(None, 'lat', 'lon')
- grad_qkv: float32 [512, 1536], replicated
- grad_proj: float32 [512, 512], replicated
The draws below stay inside these ranges and needn't reach their ends.
All inputs are finite; a program needn't handle non-finite values.
Results may differ from the reference program's by a relative error of at most 0.015.
Values may be sent and summed in bfloat16 or wider, within the bound.
A program may use at most 128 MiB of HBM per device.

```python
import jax
import jax.numpy as jnp
from jax import lax

D = 512
D2 = 1024
HEADS = 8
LEV = 2
WIN_LAT = 6
WIN_LON = 12
H = 192
W = 384
H2 = 96
W2 = 192


def set_ends(array, stream_key, least, high):
    shape = array.shape
    place = [jax.random.randint(jax.random.fold_in(stream_key, axis), (), 0, shape[axis]) for axis in range(len(shape))]
    array = array.at[tuple(place)].set(least)
    longest = shape.index(max(shape))
    place[longest] = (place[longest] + 1) % shape[longest]
    return array.at[tuple(place)].set(high)


def shard_levels(own_key, shape, cuts, smallest, top_value):
    factor_of = 1.0
    for axis_at, blocks in cuts:
        draws = jax.random.uniform(jax.random.fold_in(jax.random.fold_in(own_key, 6), axis_at), (blocks,), jnp.float32, smallest / len(cuts), top_value / len(cuts))
        factor_of = factor_of * jnp.repeat(jnp.exp(draws), shape[axis_at] // blocks).reshape((-1,) + (1,) * (len(shape) - 1 - axis_at))
    return factor_of


def noise(own_key, extent, spread, limit, pieces=(), kind=jnp.bfloat16):
    loudness = shard_levels(own_key, extent, pieces, -0.22, 0.18) if pieces else 1.0
    values = jax.random.normal(own_key, extent, jnp.float32) * spread * loudness
    return jnp.minimum(jnp.maximum(values, -limit), limit).astype(kind)


def setup_inputs(seed: int = 0) -> dict:
    keys = jax.random.split(jax.random.key(seed), 7)
    return {
        "tokens": noise(keys[0], (LEV, H, W, D), 1.0, 6.0, ((1, 16), (2, 8))),
        "region": set_ends(jax.random.randint(keys[1], (H, W), 0, 4), jax.random.fold_in(keys[1], 1), 0, 3).astype(jnp.int32),
        "w_qkv": noise(keys[2], (D, 3 * D), D ** -0.5, 0.25),
        "w_proj": noise(keys[3], (D, D), D ** -0.5, 0.25),
        "w_merge": noise(keys[4], (4 * D, D2), (4 * D) ** -0.5, 0.125),
        "d_merged": noise(keys[5], (LEV, H2, W2, D2), 1.0, 6.0, ((1, 16), (3, 8))),
    }


EPS = 1e-05

def layer_norm(value):
    average = lax.optimization_barrier(jnp.mean(value, -1, keepdims=True))
    centred = value - average
    variance = lax.optimization_barrier(jnp.mean(centred * centred, -1, keepdims=True))
    return centred * lax.rsqrt(variance + EPS)

def norm_back(value, grad):
    average = lax.optimization_barrier(jnp.mean(value, -1, keepdims=True))
    centred = value - average
    variance = lax.optimization_barrier(jnp.mean(centred * centred, -1, keepdims=True))
    inverse = lax.rsqrt(variance + EPS)
    standard = centred * inverse
    return inverse * (grad - lax.optimization_barrier(jnp.mean(grad, -1, keepdims=True)) - standard * lax.optimization_barrier(jnp.mean(grad * standard, -1, keepdims=True)))

def to_windows(field):
    levels, lat_rows, lon_cols, feature = field.shape
    field = field.reshape(levels, lat_rows // WIN_LAT, WIN_LAT, lon_cols // WIN_LON, WIN_LON, feature)
    field = field.transpose(1, 3, 0, 2, 4, 5)
    return field.reshape(-1, levels * WIN_LAT * WIN_LON, feature)

def from_windows(field, lat_rows, lon_cols):
    feature = field.shape[-1]
    field = field.reshape(lat_rows // WIN_LAT, lon_cols // WIN_LON, LEV, WIN_LAT, WIN_LON, feature)
    field = field.transpose(2, 0, 3, 1, 4, 5)
    return field.reshape(LEV, lat_rows, lon_cols, feature)

def split_qkv(qkv):
    win_count, length, _ = qkv.shape
    split_heads = qkv.astype(jnp.float32).reshape(win_count, length, 3, HEADS, D // HEADS)
    return (split_heads[:, :, 0], split_heads[:, :, 1], split_heads[:, :, 2])

def attend(qkv, allowed):
    win_count, length, _ = qkv.shape
    queries, keys_h, values = split_qkv(qkv)
    score_scale = (D // HEADS) ** (-0.5)
    scores = jnp.einsum('wqhd,wkhd->whqk', queries, keys_h) * score_scale
    weights = jnp.where(allowed[:, None], jnp.exp(scores), 0.0)
    soft_weights = weights / lax.optimization_barrier(jnp.sum(weights, -1, keepdims=True))
    soft_bf = lax.optimization_barrier(soft_weights.astype(jnp.bfloat16)).astype(jnp.float32)
    mixed_out = jnp.einsum('whqk,wkhd->wqhd', soft_bf, values)
    return (mixed_out.astype(jnp.bfloat16).reshape(win_count, length, D), soft_weights)

def attend_back(qkv, soft_weights, d_mixed):
    win_count, length, _ = qkv.shape
    queries, keys_h, values = split_qkv(qkv)
    score_scale = (D // HEADS) ** (-0.5)
    grad_heads = d_mixed.astype(jnp.float32).reshape(win_count, length, HEADS, D // HEADS)
    soft_bf = lax.optimization_barrier(soft_weights.astype(jnp.bfloat16)).astype(jnp.float32)
    d_soft = jnp.einsum('wqhd,wkhd->whqk', grad_heads, values)
    d_values = jnp.einsum('whqk,wqhd->wkhd', soft_bf, grad_heads)
    d_scores = soft_weights * (d_soft - lax.optimization_barrier(jnp.sum(soft_weights * d_soft, -1, keepdims=True)))
    d_scores_bf = lax.optimization_barrier(d_scores.astype(jnp.bfloat16)).astype(jnp.float32)
    d_queries = jnp.einsum('whqk,wkhd->wqhd', d_scores_bf, keys_h) * score_scale
    d_keys = jnp.einsum('whqk,wqhd->wkhd', d_scores_bf, queries) * score_scale
    stacked = jnp.stack([d_queries, d_keys, d_values], 2)
    return stacked.astype(jnp.bfloat16).reshape(win_count, length, 3 * D)

def reference(tokens, region, w_qkv, w_proj, w_merge, d_merged):
    height, width = region.shape
    half_lat = WIN_LAT // 2
    half_lon = WIN_LON // 2
    rolled = jnp.roll(tokens, (-half_lat, -half_lon), (1, 2))
    region_rolled = jnp.roll(region, (-half_lat, -half_lon), (0, 1))
    edge_rows = (jnp.arange(height) >= height - half_lat).astype(jnp.int32)
    window_keys = region_rolled + 4 * edge_rows[:, None]
    bands = height // WIN_LAT
    band_tokens = rolled.reshape(LEV, bands, WIN_LAT, width, D).transpose(1, 0, 2, 3, 4)
    band_keys = window_keys.reshape(bands, WIN_LAT, width)

    def band_front(band_x, band_key):
        normed = layer_norm(band_x.astype(jnp.float32)).astype(jnp.bfloat16)
        flat_norm = normed.reshape(-1, D)
        qkv = jnp.dot(flat_norm, w_qkv, preferred_element_type=jnp.float32).astype(jnp.bfloat16)
        qkv = lax.optimization_barrier(qkv)
        qkv_win = to_windows(qkv.reshape(LEV, WIN_LAT, width, 3 * D))
        key_win = to_windows(jnp.broadcast_to(band_key[None, :, :, None], (LEV, WIN_LAT, width, 1)))[:, :, 0]
        allowed = key_win[:, :, None] == key_win[:, None, :]
        return (flat_norm, qkv_win, allowed)

    def band_forward(band_args):
        band_x, band_key = band_args
        flat_norm, qkv_win, allowed = band_front(band_x, band_key)
        mixed_out, soft_weights = attend(qkv_win, allowed)
        branch = jnp.dot(mixed_out.reshape(-1, D), w_proj, preferred_element_type=jnp.float32).astype(jnp.bfloat16)
        return from_windows(branch.reshape(qkv_win.shape[0], -1, D), WIN_LAT, width)
    branches = lax.map(band_forward, (band_tokens, band_keys))
    branch_all = branches.transpose(1, 0, 2, 3, 4).reshape(LEV, height, width, D)
    restored = lax.optimization_barrier(jnp.roll(branch_all, (half_lat, half_lon), (1, 2)))
    stream = (tokens.astype(jnp.float32) + restored.astype(jnp.float32)).astype(jnp.bfloat16)
    stream = lax.optimization_barrier(stream)
    half_h = height // 2
    half_w = width // 2
    grouped = stream.reshape(LEV, half_h, 2, half_w, 2, D).transpose(0, 1, 3, 4, 2, 5).reshape(LEV, half_h, half_w, 4 * D)
    grouped_f = grouped.astype(jnp.float32)
    merge_in = layer_norm(grouped_f).astype(jnp.bfloat16)
    merged = jnp.dot(merge_in.reshape(-1, 4 * D), w_merge, preferred_element_type=jnp.float32).astype(jnp.bfloat16)
    merged = merged.reshape(LEV, half_h, half_w, D2)
    d_in = jnp.dot(d_merged.reshape(-1, D2), w_merge.T, preferred_element_type=jnp.float32).reshape(LEV, half_h, half_w, 4 * D)
    d_grouped = norm_back(grouped_f, d_in)
    d_stream = d_grouped.reshape(LEV, half_h, half_w, 2, 2, D).transpose(0, 1, 4, 2, 3, 5).reshape(LEV, height, width, D)
    d_branch = jnp.roll(d_stream.astype(jnp.bfloat16), (-half_lat, -half_lon), (1, 2))
    band_grads = d_branch.reshape(LEV, bands, WIN_LAT, width, D).transpose(1, 0, 2, 3, 4)

    def band_backward(carry, band_args):
        grad_qkv, grad_proj = carry
        band_x, band_key, band_d = band_args
        flat_norm, qkv_win, allowed = band_front(band_x, band_key)
        mixed_out, soft_weights = attend(qkv_win, allowed)
        d_win = to_windows(band_d).reshape(-1, D)
        grad_proj = grad_proj + jnp.dot(mixed_out.reshape(-1, D).T, d_win, preferred_element_type=jnp.float32)
        d_mixed = jnp.dot(d_win, w_proj.T, preferred_element_type=jnp.float32).astype(jnp.bfloat16)
        d_mixed = lax.optimization_barrier(d_mixed)
        d_qkv = attend_back(qkv_win, soft_weights, d_mixed.reshape(qkv_win.shape[0], -1, D))
        d_flat = from_windows(d_qkv, WIN_LAT, width).reshape(-1, 3 * D)
        grad_qkv = grad_qkv + jnp.dot(flat_norm.T, d_flat, preferred_element_type=jnp.float32)
        d_norm = jnp.dot(d_flat, w_qkv.T, preferred_element_type=jnp.float32).reshape(LEV, WIN_LAT, width, D)
        d_rolled = norm_back(band_x.astype(jnp.float32), d_norm)
        return ((grad_qkv, grad_proj), d_rolled)
    start = (jnp.zeros((D, 3 * D), jnp.float32), jnp.zeros((D, D), jnp.float32))
    sums, d_bands = lax.scan(band_backward, start, (band_tokens, band_keys, band_grads))
    d_rolled = d_bands.transpose(1, 0, 2, 3, 4).reshape(LEV, height, width, D)
    grad_x = d_stream + jnp.roll(d_rolled, (half_lat, half_lon), (1, 2))
    factor = float(LEV * height * width) ** (-0.5)
    return (merged, grad_x, sums[0] * factor, sums[1] * factor)
```

```python
import functools

import jax
import jax.numpy as jnp
import numpy as np
from jax import lax
from jax.experimental import pallas as pl
from jax.experimental.pallas import tpu as pltpu
from jax.sharding import PartitionSpec as P

D = 512
D2 = 1024
HEADS = 8
LEV = 2
WIN_LAT = 6
WIN_LON = 12
EPS = 1e-05

HALF = 288
PACK = 48
EXT = HALF + PACK
WIN = 144
TOK = 1152
CELLS = 288
BF = jnp.bfloat16
F32 = jnp.float32
MESH = pl.DeviceIdType.MESH


def one_hots():
    to_win = np.zeros((HALF, EXT), np.float32)
    pack = np.zeros((PACK, HALF), np.float32)
    for wc in range(4):
        for lr in range(6):
            for cw in range(WIN_LON):
                u = wc * 72 + lr * WIN_LON + cw
                col = WIN_LON * wc + WIN_LON // 2 + cw
                to_win[u, lr * 48 + col if col < 48 else HALF + lr * 6 + col - 48] = 1.0
    for lr in range(6):
        for c in range(6):
            pack[lr * 6 + c, lr * 48 + c] = 1.0
    return to_win, pack


def nn(a, b):
    return lax.dot_general(a, b, (((1,), (0,)), ((), ())), preferred_element_type=F32)


def nt(a, b):
    return lax.dot_general(a, b, (((1,), (1,)), ((), ())), preferred_element_type=F32)


def eye(n, scale=1.0):
    rows = lax.broadcasted_iota(jnp.int32, (n, n), 0)
    cols = lax.broadcasted_iota(jnp.int32, (n, n), 1)
    return jnp.where(rows == cols, scale, 0.0).astype(BF)


def take(ref, rows):
    return jnp.concatenate([ref[c, rows, :] for c in range(4)], 1)


def put(ref, rows, value):
    for c in range(4):
        ref[c, rows, :] = value[:, c * 128:(c + 1) * 128]


def stats(x):
    average = jnp.mean(x, -1, keepdims=True)
    centred = x - average
    variance = jnp.mean(centred * centred, -1, keepdims=True)
    return centred, lax.rsqrt(variance + EPS)


def kernel(
    tokens, region, w_qkv_h, w_proj_h, w_merge_h, d_merged, to_win_h, from_win_h, pack_h, unpack_h,
    m_out, gx_out, gw_out,
    ext, packs, wq, wp, wm, dm_raw, dm_send, dm_recv, to_win, from_win, pack, unpack,
    xw, keyw, normed, q, k, v, soft, mixed_t, mixed, tmp, b_send, b_pack, b_lat, b_packr,
    grid_s, g, d_in, d_str, d_ext, d_packs, d_win, d_qkv, merged,
    r_send, r_pack, r_lat, r_packr,
    grads, core_send, core_recv, send1, recv1, send2, recv2, send3, recv3, total,
    local_sem, halo_send, halo_recv, a2a_send, a2a_recv, ar_send, ar_recv,
):
    lat = lax.axis_index("lat")
    lon = lax.axis_index("lon")
    core = lax.rem(lat, 2)
    z_at = lax.rem(lax.div(lat, 2), 4)
    y_lo = lax.div(lat, 8)
    x_at = lax.div(lon, 2)
    y_at = lax.rem(lon, 2) * 2 + y_lo

    south = lax.rem(lat + 1, 16)
    north = lax.rem(lat + 15, 16)
    east = lax.rem(lon + 1, 8)
    west = lax.rem(lon + 7, 8)

    def on_z(by):
        return (y_lo * 8 + lax.rem(z_at + by, 4) * 2 + core, lon)

    def on_y(by):
        y_new = lax.rem(y_at + by, 4)
        return (lax.rem(y_new, 2) * 8 + z_at * 2 + core, x_at * 2 + lax.div(y_new, 2))

    def on_x(by):
        return (lat, lax.rem(x_at + by, 4) * 2 + lax.rem(lon, 2))

    def local(i, src, dst):
        copy = pltpu.make_async_copy(src, dst, local_sem.at[i])
        copy.start()
        return copy

    def remote(src, dst, sends, recvs, i, to):
        copy = pltpu.make_async_remote_copy(
            src_ref=src, dst_ref=dst, send_sem=sends.at[i], recv_sem=recvs.at[i], device_id=to, device_id_type=MESH
        )
        copy.start()
        return copy

    started = []

    loads = []
    for hb in range(4):
        for lev in range(LEV):
            rows, place = pl.ds(hb * 144, 144), pl.ds(lev * 144, 144)
            loads.append(local(len(loads), tokens.at[lev, rows], ext.at[hb, place, pl.ds(0, D)]))
            loads.append(local(len(loads), region.at[lev, rows], ext.at[hb, place, pl.ds(D, 128)]))
    for src, dst in ((pack_h, pack), (to_win_h, to_win), (d_merged, dm_raw), (w_qkv_h, wq), (w_merge_h, wm),
                     (w_proj_h, wp), (from_win_h, from_win), (unpack_h, unpack)):
        loads.append(local(len(loads), src, dst))
    grid_loads, (l_pack, l_to, l_dm, l_wq, l_wm, l_wp, l_from, l_un) = loads[:16], loads[16:]

    barrier = pltpu.get_barrier_semaphore()
    peers = [(south, lon), (north, lon), (south, east), (north, west)]
    peers += [(lat, lax.rem(lon + by, 8)) for by in range(1, 8)]
    peers += [on_z(by) for by in (1, 2, 3)] + [on_y(by) for by in (1, 3)]
    for peer in peers:
        pl.semaphore_signal(barrier, inc=1, device_id=peer, device_id_type=MESH)

    for copy in grid_loads:
        copy.wait()
    l_pack.wait()
    for hb in range(4):
        packs[hb] = nn(pack[...], ext[hb, 0:HALF, :]).astype(BF)
    pl.semaphore_wait(barrier, len(peers))

    def send_halo(full, small, base):
        out = [remote(full.at[0, pl.ds(0, HALF)], full.at[4, pl.ds(0, HALF)], halo_send, halo_recv, base, (north, lon))]
        for hb in range(4):
            to = (north, west) if hb == 0 else (lat, west)
            out.append(remote(small.at[hb], full.at[hb if hb else 4, pl.ds(HALF, PACK)], halo_send, halo_recv, base + 1 + hb, to))
        started.extend(out)
        return out

    halo = send_halo(ext, packs, 0)

    l_dm.wait()
    for s in range(8):
        part = dm_raw[:, s * 24:(s + 1) * 24, :].astype(F32)
        dm_send[s] = part.reshape(CELLS, 128).astype(BF)
    mine = pl.ds(pl.multiple_of(lon * 128, 128), 128)
    a2a_in = []
    for by in range(1, 8):
        to = lax.rem(lon + by, 8)
        a2a_in.append(remote(dm_send.at[to], dm_recv.at[:, mine], a2a_send, a2a_recv, by - 1, (lat, to)))
    started.extend(a2a_in)
    dm_recv[:, mine] = dm_send[lon]

    l_to.wait()
    l_wq.wait()
    for copy in halo:
        copy.wait_recv()
    for half in range(4):
        moved = nn(to_win[...], ext[half + 1])
        for wc in range(4):
            at = ((half // 2) * 4 + wc) * WIN + (half % 2) * 72
            xw[at:at + 72, :] = moved[wc * 72:(wc + 1) * 72, :D]
            keyw[at:at + 72, :] = moved[wc * 72:(wc + 1) * 72, D:]

    def norm_window(w, _):
        rows = pl.ds(pl.multiple_of(w * WIN, WIN), WIN)
        centred, inverse = stats(xw[rows, :])
        normed[rows, :] = (centred * inverse).astype(BF)
        return 0

    lax.fori_loop(0, 8, norm_window, 0)

    def project_band(band, _):
        rows = pl.ds(pl.multiple_of(band * 576, 576), 576)
        block = normed[rows, :]
        q[rows, :] = (nn(block, wq[:, 0:D]).astype(BF) * 0.125).astype(BF)
        k[rows, :] = nn(block, wq[:, D:2 * D]).astype(BF)
        v[rows, :] = nn(block, wq[:, 2 * D:3 * D]).astype(BF)
        return 0

    lax.fori_loop(0, 2, project_band, 0)

    lane = lax.broadcasted_iota(jnp.int32, (WIN, 128), 1)
    low = lane < 64

    def attend(w, _):
        rows = pl.ds(pl.multiple_of(w * WIN, WIN), WIN)
        hot = jnp.where(keyw[rows, :] == lane.astype(F32), 1.0, 0.0).astype(BF)
        bias = (nt(hot, hot) - 1.0) * 1e30
        v_t = nt(eye(D), v[rows, :]).astype(BF)
        for pair in range(4):
            cols = slice(pair * 128, (pair + 1) * 128)
            q_p, k_p = q[rows, cols], k[rows, cols]
            for side in range(2):
                head = pair * 2 + side
                k_m = jnp.where(low if side == 0 else ~low, k_p, jnp.zeros_like(k_p))
                raw = jnp.exp(nt(k_m, q_p) + bias)
                total_w = jnp.sum(raw, 0, keepdims=True)
                shrink = jnp.where(total_w > 1.0, 2.0 ** -32, 1.0)
                part = (raw * shrink) * (1.0 / (total_w * shrink))
                soft[w, head] = part
                mixed_t[w, head * 64:(head + 1) * 64, :] = nn(v_t[head * 64:(head + 1) * 64, :], part.astype(BF)).astype(BF)
        mixed[rows, :] = nt(eye(WIN), mixed_t[w]).astype(BF)
        return 0

    lax.fori_loop(0, 8, attend, 0)

    l_wp.wait()
    l_from.wait()
    l_un.wait()

    def to_grid(half, base, lat_send, lat_recv, pack_send, pack_recv, keep):
        first = (half // 2) * 4
        block = jnp.concatenate([tmp[(first + wc) * WIN + (half % 2) * 72:(first + wc) * WIN + (half % 2) * 72 + 72, :] for wc in range(4)], 0)
        moved = nn(from_win[...], block.astype(BF))
        pack_send[half] = moved[HALF:, :].astype(BF)
        out = []
        if half == 3:
            lat_send[...] = moved[:HALF, :].astype(BF)
            out.append(remote(lat_send, lat_recv, halo_send, halo_recv, base, (south, lon)))
            out.append(remote(pack_send.at[3], pack_recv.at[0], halo_send, halo_recv, base + 1, (south, east)))
        else:
            put(keep, slice((half + 1) * HALF, (half + 2) * HALF), moved[:HALF, :])
            out.append(remote(pack_send.at[half], pack_recv.at[half + 1], halo_send, halo_recv, base + 2 + half, (lat, east)))
        started.extend(out)
        return out

    def project_branch(i, _):
        rows = pl.ds(pl.multiple_of((1 - i) * 576, 576), 576)
        tmp[rows, :] = nn(mixed[rows, :], wp[...])
        return 0

    lax.fori_loop(0, 2, project_branch, 0)
    branch_halo = []
    for half in (3, 2, 1, 0):
        branch_halo += to_grid(half, 5, b_send, b_lat, b_pack, b_packr, grid_s)

    l_wm.wait()
    for copy in a2a_in:
        copy.wait_recv()

    def d_in_part(p, _):
        d_in[p] = nt(dm_recv[...], wm[pl.ds(pl.multiple_of(p * D, D), D), :])
        return 0

    lax.fori_loop(0, 4, d_in_part, 0)

    for copy in branch_halo:
        copy.wait_recv()
    for hb in range(4):
        at = slice(hb * HALF, (hb + 1) * HALF)
        own = b_lat[...].astype(F32) if hb == 0 else take(grid_s, at)
        full = own + nn(unpack[...], b_packr[hb])
        put(grid_s, at, (ext[hb, 0:HALF, 0:D].astype(F32) + full).astype(BF).astype(F32))

    def cell_rows(p, lev, i):
        row = 2 * i + p % 2
        return ((row // 3 * 2 + lev) * 3 + row % 3) * 48 + p // 2

    for p in range(4):
        for lev in range(LEV):
            for i in range(6):
                at = (lev * 6 + i) * 24
                g[p, at:at + 24, :] = take(grid_s, pl.ds(cell_rows(p, lev, i), 24, stride=2))

    average = sum(jnp.sum(g[p], -1, keepdims=True) for p in range(4)) / (4 * D)
    variance = 0.0
    for p in range(4):
        centred = g[p] - average
        variance = variance + jnp.sum(centred * centred, -1, keepdims=True)
    inverse = lax.rsqrt(variance / (4 * D) + EPS)
    mean_d = sum(jnp.sum(d_in[p], -1, keepdims=True) for p in range(4)) / (4 * D)
    mean_dh = sum(jnp.sum(d_in[p] * ((g[p] - average) * inverse), -1, keepdims=True) for p in range(4)) / (4 * D)
    for p in range(4):
        hat = (g[p] - average) * inverse
        d_part = inverse * (d_in[p] - mean_d - hat * mean_dh)
        g[p] = hat
        for lev in range(LEV):
            for i in range(6):
                at = (lev * 6 + i) * 24
                put(d_str, pl.ds(cell_rows(p, lev, i), 24, stride=2), d_part[at:at + 24, :])

    for hb in range(4):
        d_ext[hb, 0:HALF, :] = take(d_str, slice(hb * HALF, (hb + 1) * HALF)).astype(BF)
    for hb in range(4):
        d_packs[hb] = nn(pack[...], d_ext[hb, 0:HALF, :]).astype(BF)
    d_halo = send_halo(d_ext, d_packs, 10)

    for n in range(2):
        cols = slice(n * 512, (n + 1) * 512)
        sums = nn(g[0].astype(BF), wm[0:D, cols])
        for p in range(1, 4):
            sums = sums + nn(g[p].astype(BF), wm[p * D:(p + 1) * D, cols])
        for s in range(4):
            merged[n * 4 + s] = sums[:, s * 128:(s + 1) * 128].astype(BF)
    for by in range(1, 8):
        to = lax.rem(lon + by, 8)
        started.append(remote(merged.at[to], m_out.at[lon], a2a_send, a2a_recv, 6 + by, (lat, to)))
    merged_out = started[-7:]
    merged_own = local(36, merged.at[lon], m_out.at[lon])

    for copy in d_halo:
        copy.wait_recv()
    for half in range(4):
        moved = nn(to_win[...], d_ext[half + 1])
        for wc in range(4):
            at = ((half // 2) * 4 + wc) * WIN + (half % 2) * 72
            tmp[at:at + 72, :] = moved[wc * 72:(wc + 1) * 72, :]

    d_mix = mixed

    def back_band(band, _):
        rows = pl.ds(pl.multiple_of(band * 576, 576), 576)
        block = tmp[rows, :].astype(BF)
        d_win[rows, :] = block
        d_mix[rows, :] = nt(block, wp[...]).astype(BF)
        return 0

    lax.fori_loop(0, 2, back_band, 0)

    grads[0] = jnp.zeros((D, D), F32)

    def proj_window(w, _):
        rows = pl.ds(pl.multiple_of(w * WIN, WIN), WIN)
        grads[0] = grads[0] + nn(mixed_t[w], d_win[rows, :])
        return 0

    lax.fori_loop(0, 8, proj_window, 0)

    def attend_back(w, _):
        rows = pl.ds(pl.multiple_of(w * WIN, WIN), WIN)
        k_t = nt(eye(D, 0.125), k[rows, :]).astype(BF)
        parts = []
        for pair in range(4):
            cols = slice(pair * 128, (pair + 1) * 128)
            q_p, v_p, dm_p = q[rows, cols], v[rows, cols], d_mix[rows, cols]
            d_v, d_k = [], []
            for side in range(2):
                head = pair * 2 + side
                part = soft[w, head]
                v_m = jnp.where(low if side == 0 else ~low, v_p, jnp.zeros_like(v_p))
                d_soft = nt(v_m, dm_p)
                delta = jnp.sum(part * d_soft, 0, keepdims=True)
                d_s = (part * (d_soft - delta)).astype(BF)
                d_v.append(nn(part.astype(BF), dm_p))
                d_k.append(nn(d_s, q_p))
                parts.append(nn(k_t[head * 64:(head + 1) * 64, :], d_s).astype(BF))
            d_qkv[rows, D + pair * 128:D + (pair + 1) * 128] = jnp.where(low, d_k[0], d_k[1]).astype(BF)
            d_qkv[rows, 2 * D + pair * 128:2 * D + (pair + 1) * 128] = jnp.where(low, d_v[0], d_v[1]).astype(BF)
        d_qkv[rows, 0:D] = nt(eye(WIN), jnp.concatenate(parts, 0)).astype(BF)
        return 0

    lax.fori_loop(0, 8, attend_back, 0)

    def norm_back_band(band, _):
        rows = pl.ds(pl.multiple_of(band * 576, 576), 576)
        d_norm = nt(d_qkv[rows, :], wq[...])
        centred, inverse = stats(xw[rows, :])
        hat = centred * inverse
        tmp[rows, :] = inverse * (
            d_norm - jnp.mean(d_norm, -1, keepdims=True) - hat * jnp.mean(d_norm * hat, -1, keepdims=True)
        )
        return 0

    lax.fori_loop(0, 2, norm_back_band, 0)
    roll_halo = []
    for half in (3, 2, 1, 0):
        roll_halo += to_grid(half, 15, r_send, r_lat, r_pack, r_packr, grid_s)

    normed_t = jnp.concatenate([nt(eye(D), normed[i * 384:(i + 1) * 384, :]).astype(BF) for i in range(3)], 1)
    for m in range(3):
        grads[m + 1] = nn(normed_t, d_qkv[:, m * D:(m + 1) * D])

    orders = (("z", "y", "x"), ("y", "x", "z"), ("x", "z", "y"), ("z", "x", "y"))
    along = {"z": (on_z, z_at), "y": (on_y, y_at), "x": (on_x, x_at)}
    acc1 = d_in
    other = (lat + 1 - 2 * core, lon)
    half_at = pl.multiple_of(core * 256, 256)
    away_at = pl.multiple_of((1 - core) * 256, 256)
    ar = [[None] * 4 for _ in range(4)]
    for m in range(4):
        core_send[m] = grads[m, pl.ds(away_at, 256), :].astype(BF)
        ar[m][0] = [remote(core_send.at[m], core_recv.at[m], ar_send, ar_recv, m * 20, other)]
    for m in range(4):
        move, at = along[orders[m][0]]
        ar[m][0][0].wait_recv()
        acc1[m, 0:256, :] = grads[m, pl.ds(half_at, 256), :] + core_recv[m].astype(F32)
        send1[m] = acc1[m, 0:256, :].astype(BF)
        ar[m][1] = []
        for by in range(1, 4):
            rows = pl.ds(pl.multiple_of(lax.rem(at + by, 4) * 64, 64), 64)
            ar[m][1].append(remote(send1.at[m, rows], recv1.at[m, by - 1], ar_send, ar_recv, m * 20 + by, move(by)))
    places = []
    for m in range(4):
        at = along[orders[m][0]][1]
        for copy in ar[m][1]:
            copy.wait_recv()
        own = acc1[m, pl.ds(pl.multiple_of(at * 64, 64), 64), :]
        for j in range(3):
            own = own + recv1[m, j].astype(F32)
        send2[m] = own.astype(BF)
        acc1[m, 0:64, :] = own
        move, at2 = along[orders[m][1]]
        ar[m][2] = []
        for by in range(1, 4):
            rows = pl.ds(pl.multiple_of(lax.rem(at2 + by, 4) * 16, 16), 16)
            ar[m][2].append(remote(send2.at[m, rows], recv2.at[m, by - 1], ar_send, ar_recv, m * 20 + 3 + by, move(by)))
    for m in range(4):
        at2 = along[orders[m][1]][1]
        for copy in ar[m][2]:
            copy.wait_recv()
        own = acc1[m, pl.ds(pl.multiple_of(at2 * 16, 16), 16), :]
        for j in range(3):
            own = own + recv2[m, j].astype(F32)
        send3[m] = own.astype(BF)
        acc1[m, 0:16, :] = own
        move, at3 = along[orders[m][2]]
        ar[m][3] = []
        for by in range(1, 4):
            cols = pl.ds(pl.multiple_of(lax.rem(at3 + by, 4) * 128, 128), 128)
            ar[m][3].append(remote(send3.at[m, :, cols], recv3.at[m, by - 1], ar_send, ar_recv, m * 20 + 6 + by, move(by)))
    factor = float(LEV * 192 * 384) ** -0.5
    gather = []
    for m in range(4):
        ats = [along[axis][1] for axis in orders[m]]
        for copy in ar[m][3]:
            copy.wait_recv()
        cols = pl.ds(pl.multiple_of(ats[2] * 128, 128), 128)
        own = acc1[m, 0:16, cols]
        for j in range(3):
            own = own + recv3[m, j].astype(F32)
        row1 = core * 256
        row2 = row1 + ats[0] * 64
        row3 = row2 + ats[1] * 16
        rows3 = pl.ds(pl.multiple_of(row3, 16), 16)
        total[m, rows3, cols] = (own * factor).astype(BF)
        move = along[orders[m][2]][0]
        gather.append([
            remote(total.at[m, rows3, cols], total.at[m, rows3, cols], ar_send, ar_recv, m * 20 + 9 + by, move(by))
            for by in range(1, 4)
        ])
        places.append((pl.ds(pl.multiple_of(row1, 256), 256), pl.ds(pl.multiple_of(row2, 64), 64), rows3))
    gather2 = []
    for m in range(4):
        for copy in gather[m]:
            copy.wait_recv()
        move, rows = along[orders[m][1]][0], places[m][2]
        gather2.append([
            remote(total.at[m, rows], total.at[m, rows], ar_send, ar_recv, m * 20 + 12 + by, move(by))
            for by in range(1, 4)
        ])
    gather3 = []
    for m in range(4):
        for copy in gather2[m]:
            copy.wait_recv()
        move, rows = along[orders[m][0]][0], places[m][1]
        gather3.append([
            remote(total.at[m, rows], total.at[m, rows], ar_send, ar_recv, m * 20 + 15 + by, move(by))
            for by in range(1, 4)
        ])

    for copy in roll_halo:
        copy.wait_recv()
    outs = []
    for hb in range(4):
        at = slice(hb * HALF, (hb + 1) * HALF)
        own = r_lat[...].astype(F32) if hb == 0 else take(grid_s, at)
        put(d_str, at, take(d_str, at) + own + nn(unpack[...], r_packr[hb]))
        for lev in range(LEV):
            for c in range(4):
                src = d_str.at[c, pl.ds(hb * HALF + lev * 144, 144)]
                outs.append(local(len(outs), src, gx_out.at[lev, pl.ds(hb * 144, 144), pl.ds(c * 128, 128)]))

    gather4 = []
    for m in range(4):
        for copy in gather3[m]:
            copy.wait_recv()
        rows = places[m][0]
        gather4.append(remote(total.at[m, rows], total.at[m, rows], ar_send, ar_recv, m * 20 + 19, other))
    for m in range(4):
        gather4[m].wait_recv()
        outs.append(local(len(outs), total.at[m], gw_out.at[m]))

    for copy in merged_out:
        copy.wait_recv()
    for copy in started:
        copy.wait_send()
    for m in range(4):
        for stage in ar[m] + [gather[m], gather2[m], gather3[m], [gather4[m]]]:
            for copy in stage:
                copy.wait_send()
    merged_own.wait()
    for copy in outs:
        copy.wait()


def vmem(*shape, dtype=BF):
    return pltpu.VMEM(shape, dtype)


SCRATCH = [
    vmem(5, EXT, 640), vmem(4, PACK, 640), vmem(D, 3 * D), vmem(D, D), vmem(4 * D, D2),
    vmem(12, 192, 128), vmem(8, CELLS, 128), vmem(CELLS, D2), vmem(HALF, EXT), vmem(EXT, HALF), vmem(PACK, HALF), vmem(HALF, PACK),
    vmem(TOK, D, dtype=F32), vmem(TOK, 128, dtype=F32), vmem(TOK, D), vmem(TOK, D), vmem(TOK, D), vmem(TOK, D),
    vmem(8, HEADS, WIN, WIN, dtype=F32), vmem(8, D, WIN), vmem(TOK, D), vmem(TOK, D, dtype=F32),
    vmem(HALF, D), vmem(4, PACK, D), vmem(HALF, D), vmem(4, PACK, D),
    vmem(4, TOK, 128, dtype=F32), vmem(4, CELLS, D, dtype=F32), vmem(4, CELLS, D, dtype=F32), vmem(4, TOK, 128, dtype=F32),
    vmem(5, EXT, D), vmem(4, PACK, D), vmem(TOK, D), vmem(TOK, 3 * D), vmem(8, CELLS, 128),
    vmem(HALF, D), vmem(4, PACK, D), vmem(HALF, D), vmem(4, PACK, D),
    vmem(4, D, D, dtype=F32), vmem(4, 256, D), vmem(4, 256, D), vmem(4, 256, D),
    vmem(4, 3, 64, D), vmem(4, 64, D), vmem(4, 3, 16, D), vmem(4, 16, D), vmem(4, 3, 16, 128), vmem(4, D, D),
    pltpu.SemaphoreType.DMA((37,)), pltpu.SemaphoreType.DMA((20,)), pltpu.SemaphoreType.DMA((20,)),
    pltpu.SemaphoreType.DMA((14,)), pltpu.SemaphoreType.DMA((14,)),
    pltpu.SemaphoreType.DMA((80,)), pltpu.SemaphoreType.DMA((80,)),
]


def per_device(tokens, region, w_qkv, w_proj, w_merge, d_merged):
    levels, lat_rows, lon_cols, feature = tokens.shape
    rows = jnp.arange(lat_rows, dtype=jnp.int32)
    edge = jnp.where((lax.axis_index("lat") == 0) & (rows < WIN_LAT // 2), 4, 0)
    keys = (region + edge[:, None]).astype(BF)
    keys = jnp.broadcast_to(keys[None, :, :, None], (levels, lat_rows, lon_cols, 128))
    to_win, pack = one_hots()
    consts = [jnp.asarray(a, BF) for a in (to_win, to_win.T, pack, pack.T)]
    anywhere = pl.BlockSpec(memory_space=pl.ANY)
    m_out, gx_out, gw_out = pl.pallas_call(
        kernel,
        out_shape=(
            jax.ShapeDtypeStruct((8, CELLS, 128), BF),
            jax.ShapeDtypeStruct((levels, 576, feature), F32),
            jax.ShapeDtypeStruct((4, D, D), BF),
        ),
        in_specs=[anywhere] * 10,
        out_specs=(anywhere,) * 3,
        scratch_shapes=SCRATCH,
        compiler_params=pltpu.CompilerParams(
            collective_id=0, has_side_effects=True, vmem_limit_bytes=64 * 1024 * 1024
        ),
    )(
        tokens.reshape(levels, 576, feature), keys.reshape(levels, 576, 128), w_qkv, w_proj, w_merge,
        d_merged.reshape(12, 192, 128), *consts,
    )
    merged = m_out.reshape(8, levels, 6, 24, 128).transpose(1, 2, 0, 3, 4).reshape(levels, 6, 192, 128)
    grad_x = gx_out.reshape(levels, lat_rows, lon_cols, feature)
    grad_qkv = jnp.concatenate([gw_out[1], gw_out[2], gw_out[3]], 1).astype(F32)
    return (merged, grad_x, grad_qkv, gw_out[0].astype(F32))


def solution(mesh):
    in_specs = (
        P(None, "lat", "lon", None),
        P("lat", "lon"),
        P(),
        P(),
        P(),
        P(None, "lat", None, "lon"),
    )
    out_specs = (P(None, "lat", None, "lon"), P(None, "lat", "lon", None), P(), P())
    return jax.shard_map(
        per_device, mesh=mesh, in_specs=in_specs, out_specs=out_specs, check_vma=False
    )
```

```python
import functools

import jax
import jax.numpy as jnp
import numpy as np
from jax import lax
from jax.experimental import pallas as pl
from jax.experimental.pallas import tpu as pltpu
from jax.sharding import PartitionSpec as P

D = 512
D2 = 1024
HEADS = 8
LEV = 2
WIN_LAT = 6
WIN_LON = 12
EPS = 1e-05

HALF = 288
PACK = 48
EXT = HALF + PACK
WIN = 144
TOK = 1152
CELLS = 288
BF = jnp.bfloat16
F32 = jnp.float32
MESH = pl.DeviceIdType.MESH


CHUNK_LANE = (0, 0, 128, 256, 256)
SEGMENTS = []
for _head in range(HEADS):
    _at = _head * WIN
    while _at < (_head + 1) * WIN:
        _end = min((_at // 256 + 1) * 256, (_head + 1) * WIN)
        SEGMENTS.append((_head, _at, _end))
        _at = _end


def one_hots():
    to_win = np.zeros((HALF, EXT), np.float32)
    pack = np.zeros((PACK, HALF), np.float32)
    for wc in range(4):
        for lr in range(6):
            for cw in range(WIN_LON):
                u = wc * 72 + lr * WIN_LON + cw
                col = WIN_LON * wc + WIN_LON // 2 + cw
                to_win[u, lr * 48 + col if col < 48 else HALF + lr * 6 + col - 48] = 1.0
    for lr in range(6):
        for c in range(6):
            pack[lr * 6 + c, lr * 48 + c] = 1.0
    return to_win, pack


def nn(a, b):
    return lax.dot_general(a, b, (((1,), (0,)), ((), ())), preferred_element_type=F32)


def nt(a, b):
    return lax.dot_general(a, b, (((1,), (1,)), ((), ())), preferred_element_type=F32)


def tn(a, b):
    return lax.dot_general(a, b, (((0,), (0,)), ((), ())), preferred_element_type=F32)


def take(ref, rows):
    return jnp.concatenate([ref[c, rows, :] for c in range(4)], 1)


def put(ref, rows, value):
    for c in range(4):
        ref[c, rows, :] = value[:, c * 128:(c + 1) * 128]


def stats(x):
    average = jnp.mean(x, -1, keepdims=True)
    centred = x - average
    variance = jnp.mean(centred * centred, -1, keepdims=True)
    return centred, lax.rsqrt(variance + EPS)


def kernel(
    tokens, region, w_qkv_h, w_proj_h, w_merge_h, d_merged, to_win_h, from_win_h, pack_h, unpack_h,
    m_out, gx_out, gq_out, gp_out,
    ext, packs, regions, wq, wp, wm, dm_raw, dm_send, dm_recv, to_win, from_win, pack, unpack,
    xw, keyw, normed, q, k, v, block_q, block_d, staged, soft, mixed_t, normed_t, mixed, tmp, b_send, b_pack, b_lat, b_packr,
    grid_s, g, d_in, d_str, d_ext, d_packs, d_win, d_mix, d_qkv, merged, merged_in, merged_all,
    r_send, r_pack, r_lat, r_packr,
    grads, core_send, core_recv, send1, recv1, send2, recv2, send3, recv3, total,
    local_sem, halo_send, halo_recv, a2a_send, a2a_recv, ar_send, ar_recv,
):
    lat = lax.axis_index("lat")
    lon = lax.axis_index("lon")
    core = lax.rem(lat, 2)
    z_at = lax.rem(lax.div(lat, 2), 4)
    y_lo = lax.div(lat, 8)
    x_at = lax.div(lon, 2)
    y_at = lax.rem(lon, 2) * 2 + y_lo

    south = lax.rem(lat + 1, 16)
    north = lax.rem(lat + 15, 16)
    east = lax.rem(lon + 1, 8)
    west = lax.rem(lon + 7, 8)

    def on_z(by):
        return (y_lo * 8 + lax.rem(z_at + by, 4) * 2 + core, lon)

    def on_y(by):
        y_new = lax.rem(y_at + by, 4)
        return (lax.rem(y_new, 2) * 8 + z_at * 2 + core, x_at * 2 + lax.div(y_new, 2))

    def on_x(by):
        return (lat, lax.rem(x_at + by, 4) * 2 + lax.rem(lon, 2))

    def local(i, src, dst):
        copy = pltpu.make_async_copy(src, dst, local_sem.at[i])
        copy.start()
        return copy

    def remote(src, dst, sends, recvs, i, to):
        copy = pltpu.make_async_remote_copy(
            src_ref=src, dst_ref=dst, send_sem=sends.at[i], recv_sem=recvs.at[i], device_id=to, device_id_type=MESH
        )
        copy.start()
        return copy

    started = []

    loads = []
    for hb in range(4):
        for lev in range(LEV):
            rows, place = pl.ds(hb * 144, 144), pl.ds(lev * 144, 144)
            loads.append(local(len(loads), tokens.at[lev, rows], ext.at[hb, place, pl.ds(0, D)]))
    for src, dst in ((region, regions), (pack_h, pack), (to_win_h, to_win), (d_merged, dm_raw), (w_qkv_h, wq), (w_merge_h, wm),
                     (w_proj_h, wp), (from_win_h, from_win), (unpack_h, unpack)):
        loads.append(local(len(loads), src, dst))
    grid_loads, (l_reg, l_pack, l_to, l_dm, l_wq, l_wm, l_wp, l_from, l_un) = loads[:8], loads[8:]

    barrier = pltpu.get_barrier_semaphore()
    peers = [(south, lon), (north, lon), (south, east), (north, west)]
    peers += [(lat, lax.rem(lon + by, 8)) for by in range(1, 8)]
    peers += [on_z(by) for by in (1, 2, 3)] + [on_y(by) for by in (1, 3)]
    for peer in peers:
        pl.semaphore_signal(barrier, inc=1, device_id=peer, device_id_type=MESH)

    for copy in grid_loads:
        copy.wait()
    l_reg.wait()
    corner = lax.broadcasted_iota(jnp.int32, (48, 48), 0) == lax.broadcasted_iota(jnp.int32, (48, 48), 1)
    for row in range(12):
        column = jnp.sum(jnp.where(corner, regions[row:row + 1, :].astype(F32), 0.0), 1, keepdims=True)
        if row < WIN_LAT // 2:
            column = column + jnp.where(lat == 0, 4.0, 0.0)
        for lev in range(LEV):
            at = lev * 144 + row % 3 * 48
            ext[row // 3, at:at + 48, D:] = jnp.broadcast_to(column, (48, 128)).astype(BF)
    l_pack.wait()
    for hb in range(4):
        packs[hb] = nn(pack[...], ext[hb, 0:HALF, :]).astype(BF)
    pl.semaphore_wait(barrier, len(peers))

    def send_halo(full, small, base):
        out = [remote(full.at[0, pl.ds(0, HALF)], full.at[4, pl.ds(0, HALF)], halo_send, halo_recv, base, (north, lon))]
        for hb in range(4):
            to = (north, west) if hb == 0 else (lat, west)
            out.append(remote(small.at[hb], full.at[hb if hb else 4, pl.ds(HALF, PACK)], halo_send, halo_recv, base + 1 + hb, to))
        started.extend(out)
        return out

    halo = send_halo(ext, packs, 0)

    l_dm.wait()
    for s in range(8):
        part = dm_raw[:, s * 24:(s + 1) * 24, :].astype(F32)
        dm_send[s] = part.reshape(CELLS, 128).astype(BF)
    mine = pl.ds(pl.multiple_of(lon * 128, 128), 128)
    a2a_in = []
    for by in range(1, 8):
        to = lax.rem(lon + by, 8)
        a2a_in.append(remote(dm_send.at[to], dm_recv.at[:, mine], a2a_send, a2a_recv, by - 1, (lat, to)))
    started.extend(a2a_in)
    dm_recv[:, mine] = dm_send[lon]

    def window_rows(half, first, moved, wide):
        for i in range(moved.shape[0] // 72):
            at = ((half // 2) * 4 + first + i) * WIN + (half % 2) * 72
            wide[at:at + 72, :] = moved[i * 72:(i + 1) * 72, :D]
            if moved.shape[1] > D:
                keyw[at:at + 72, :] = moved[i * 72:(i + 1) * 72, D:]

    def norm_window(w, _):
        rows = pl.ds(pl.multiple_of(w * WIN, WIN), WIN)
        centred, inverse = stats(xw[rows, :])
        normed[rows, :] = (centred * inverse).astype(BF)
        return 0

    def project_pair(i, _):
        rows = pl.ds(pl.multiple_of(i * 288, 288), 288)
        block = normed[rows, :]
        q[rows, :] = (nn(block, wq[:, 0:D]).astype(BF) * 0.125).astype(BF)
        k[rows, :] = nn(block, wq[:, D:2 * D]).astype(BF)
        v[rows, :] = nn(block, wq[:, 2 * D:3 * D]).astype(BF)
        return 0

    lane = lax.broadcasted_iota(jnp.int32, (WIN, 128), 1)
    low = lane < 64

    def spread(ref, rows, src, filler):
        blank = jnp.zeros((WIN, 128), BF)
        for head, first, last in SEGMENTS:
            chunk, at = first // 256, pl.ds(first, last - first)
            part = slice(first - head * WIN, last - head * WIN)
            own = src[rows, (head // 2) * 128:(head // 2 + 1) * 128]
            own = jnp.where(low if head % 2 == 0 else ~low, own, blank)
            block = head // 2 - CHUNK_LANE[chunk] // 128
            fill = blank if filler is None else filler
            if chunk == 0:
                ref[at, 0:128] = own[part]
                ref[at, 128:256] = fill[part]
            else:
                ref[at, 0:128] = (jnp.where(low, fill, own) if block == 0 else fill)[part]
                ref[at, 128:256] = (own if block == 1 else blank)[part]

    def by_heads(stage, left, right, chunk):
        out = tn(left, right[:, CHUNK_LANE[chunk]:CHUNK_LANE[chunk] + 256])
        for head, first, last in SEGMENTS:
            if first // 256 == chunk:
                block = head // 2 - CHUNK_LANE[chunk] // 128
                rows = slice(first - chunk * 256, last - chunk * 256)
                stage[first:last, :] = out[rows, block * 128:(block + 1) * 128]

    def joined(stage, pair):
        even, odd = 2 * pair * WIN, (2 * pair + 1) * WIN
        return jnp.where(low, stage[even:even + WIN, :], stage[odd:odd + WIN, :])

    def attend(w, q_b, stage):
        rows = pl.ds(pl.multiple_of(w * WIN, WIN), WIN)
        same = keyw[rows, :] == lane.astype(F32)
        differ = jnp.where(same | ~low, 0.0, 1.0).astype(BF)
        forbid = jnp.where(same, -1e30, 0.0).astype(BF)
        spread(q_b, rows, q, differ)
        k_b = [k[rows, i * 128:(i + 1) * 128] for i in range(4)]
        k_x = [jnp.concatenate([k_b[0], jnp.where(low, forbid, k_b[1])], 1)]
        k_x += [jnp.concatenate([jnp.where(low, forbid, k_b[i]), k_b[i + 1]], 1) for i in range(3)]
        values = v[rows, :]
        for chunk in range(5):
            cols = slice(chunk * 256, min(chunk * 256 + 256, 1152))
            raw = jnp.exp(nt(k_x[min(chunk, 3)], q_b[cols, :]))
            total_w = jnp.sum(raw, 0, keepdims=True)
            shrink = jnp.where(total_w > 1.0, 2.0 ** -32, 1.0)
            part = (raw * shrink) * (1.0 / (total_w * shrink))
            soft[w, :, cols] = part
            by_heads(stage, part.astype(BF), values, chunk)
        for pair in range(4):
            mixed[rows, pair * 128:(pair + 1) * 128] = joined(stage, pair).astype(BF)

    def attend_pair(i, _):
        attend(2 * i, block_q.at[0], staged.at[0])
        attend(2 * i + 1, block_q.at[1], staged.at[1])
        return 0

    l_to.wait()
    for half in range(2):
        window_rows(half, 0, nn(to_win[0:WIN, 0:HALF], ext[half + 1, 0:HALF, :]), xw)
    lax.fori_loop(0, 2, norm_window, 0)
    l_wq.wait()
    project_pair(0, 0)
    attend_pair(0, 0)

    for copy in halo:
        copy.wait_recv()
    for half in range(2):
        window_rows(half, 2, nn(to_win[WIN:, :], ext[half + 1]), xw)
    for half in range(2, 4):
        window_rows(half, 0, nn(to_win[...], ext[half + 1]), xw)
    lax.fori_loop(2, 8, norm_window, 0)
    lax.fori_loop(1, 4, project_pair, 0)
    lax.fori_loop(2, 4, attend_pair, 0)

    l_wp.wait()
    l_from.wait()
    l_un.wait()

    def to_grid(half, base, lat_send, lat_recv, pack_send, pack_recv, keep):
        first = (half // 2) * 4
        block = jnp.concatenate([tmp[(first + wc) * WIN + (half % 2) * 72:(first + wc) * WIN + (half % 2) * 72 + 72, :] for wc in range(4)], 0)
        moved = nn(from_win[...], block.astype(BF))
        pack_send[half] = moved[HALF:, :].astype(BF)
        out = []
        if half == 3:
            lat_send[...] = moved[:HALF, :].astype(BF)
            out.append(remote(lat_send, lat_recv, halo_send, halo_recv, base, (south, lon)))
            out.append(remote(pack_send.at[3], pack_recv.at[0], halo_send, halo_recv, base + 1, (south, east)))
        else:
            put(keep, slice((half + 1) * HALF, (half + 2) * HALF), moved[:HALF, :])
            out.append(remote(pack_send.at[half], pack_recv.at[half + 1], halo_send, halo_recv, base + 2 + half, (lat, east)))
        started.extend(out)
        return out

    branch_halo = []
    for band in (1, 0):
        if band == 0:
            attend_pair(1, 0)
        rows = slice(band * 576, (band + 1) * 576)
        tmp[rows, :] = nn(mixed[rows, :], wp[...])
        for half in (band * 2 + 1, band * 2):
            branch_halo += to_grid(half, 5, b_send, b_lat, b_pack, b_packr, grid_s)

    l_wm.wait()
    for copy in a2a_in:
        copy.wait_recv()

    def d_in_part(p, _):
        d_in[p] = nt(dm_recv[...], wm[pl.ds(pl.multiple_of(p * D, D), D), :])
        return 0

    lax.fori_loop(0, 4, d_in_part, 0)
    for i in range(9):
        rows = slice(i * 128, (i + 1) * 128)
        normed_t[:, rows] = normed[rows, :].T
        mixed_t[:, rows] = mixed[rows, :].T

    for copy in branch_halo:
        copy.wait_recv()
    for hb in range(4):
        at = slice(hb * HALF, (hb + 1) * HALF)
        own = b_lat[...].astype(F32) if hb == 0 else take(grid_s, at)
        full = own + nn(unpack[...], b_packr[hb])
        put(grid_s, at, (ext[hb, 0:HALF, 0:D].astype(F32) + full).astype(BF).astype(F32))

    def cell_rows(p, lev, i):
        row = 2 * i + p % 2
        return ((row // 3 * 2 + lev) * 3 + row % 3) * 48 + p // 2

    for p in range(4):
        for lev in range(LEV):
            for i in range(6):
                at = (lev * 6 + i) * 24
                g[p, at:at + 24, :] = take(grid_s, pl.ds(cell_rows(p, lev, i), 24, stride=2))

    average = sum(jnp.sum(g[p], -1, keepdims=True) for p in range(4)) / (4 * D)
    variance = 0.0
    for p in range(4):
        centred = g[p] - average
        variance = variance + jnp.sum(centred * centred, -1, keepdims=True)
    inverse = lax.rsqrt(variance / (4 * D) + EPS)
    mean_d = sum(jnp.sum(d_in[p], -1, keepdims=True) for p in range(4)) / (4 * D)
    mean_dh = sum(jnp.sum(d_in[p] * ((g[p] - average) * inverse), -1, keepdims=True) for p in range(4)) / (4 * D)
    for p in range(4):
        hat = (g[p] - average) * inverse
        d_part = inverse * (d_in[p] - mean_d - hat * mean_dh)
        g[p] = hat
        for lev in range(LEV):
            for i in range(6):
                at = (lev * 6 + i) * 24
                put(d_str, pl.ds(cell_rows(p, lev, i), 24, stride=2), d_part[at:at + 24, :])

    for hb in range(4):
        d_ext[hb, 0:HALF, :] = take(d_str, slice(hb * HALF, (hb + 1) * HALF)).astype(BF)
    for hb in range(4):
        d_packs[hb] = nn(pack[...], d_ext[hb, 0:HALF, :]).astype(BF)
    d_halo = send_halo(d_ext, d_packs, 10)

    for n in range(2):
        cols = slice(n * 512, (n + 1) * 512)
        sums = nn(g[0].astype(BF), wm[0:D, cols])
        for p in range(1, 4):
            sums = sums + nn(g[p].astype(BF), wm[p * D:(p + 1) * D, cols])
        for s in range(4):
            merged[n * 4 + s] = sums[:, s * 128:(s + 1) * 128].astype(BF)
    for by in range(1, 8):
        to = lax.rem(lon + by, 8)
        started.append(remote(merged.at[to], merged_in.at[lon], a2a_send, a2a_recv, 6 + by, (lat, to)))
    merged_out = started[-7:]
    merged_in[lon] = merged[lon]

    def back_pair(i, _):
        rows = pl.ds(pl.multiple_of(i * 288, 288), 288)
        block = tmp[rows, :].astype(BF)
        d_win[rows, :] = block
        d_mix[rows, :] = nt(block, wp[...]).astype(BF)
        return 0

    def attend_back(w, q_b, d_b, stage):
        rows = pl.ds(pl.multiple_of(w * WIN, WIN), WIN)
        spread(q_b, rows, q, None)
        spread(d_b, rows, d_mix, None)
        keys, values = k[rows, :], v[rows, :]
        d_k, d_v = [], []
        for chunk in range(5):
            cols = slice(chunk * 256, min(chunk * 256 + 256, 1152))
            part = soft[w, :, cols]
            d_soft = nt(values[:, CHUNK_LANE[chunk]:CHUNK_LANE[chunk] + 256], d_b[cols, :])
            delta = jnp.sum(part * d_soft, 0, keepdims=True)
            d_s = (part * (d_soft - delta)).astype(BF)
            d_v.append(nn(part.astype(BF), d_b[cols, :]))
            d_k.append(nn(d_s, q_b[cols, :]))
            by_heads(stage, d_s, keys, chunk)
        for which, d in ((1, d_k), (2, d_v)):
            both = [d[0][:, 0:128] + d[1][:, 0:128], d[1][:, 128:256] + d[2][:, 0:128],
                    d[2][:, 128:256] + d[3][:, 0:128] + d[4][:, 0:128], d[3][:, 128:256] + d[4][:, 128:256]]
            for pair in range(4):
                d_qkv[rows, which * D + pair * 128:which * D + (pair + 1) * 128] = both[pair].astype(BF)
        for pair in range(4):
            d_qkv[rows, pair * 128:(pair + 1) * 128] = (joined(stage, pair) * 0.125).astype(BF)

    def attend_back_pair(i, _):
        attend_back(2 * i, block_q.at[0], block_d.at[0], staged.at[0])
        attend_back(2 * i + 1, block_q.at[1], block_d.at[1], staged.at[1])
        return 0

    orders = (("z", "y", "x"), ("y", "x", "z"), ("x", "z", "y"), ("z", "x", "y"))
    along = {"z": (on_z, z_at), "y": (on_y, y_at), "x": (on_x, x_at)}
    acc1 = d_in
    other = (lat + 1 - 2 * core, lon)
    half_at = pl.multiple_of(core * 256, 256)
    away_at = pl.multiple_of((1 - core) * 256, 256)
    factor = float(LEV * 192 * 384) ** -0.5
    outs = []

    def summed(m):
        (move1, at1), (move2, at2), (move3, at3) = [along[axis] for axis in orders[m]]

        def send(i, src, dst, to):
            copy = remote(src, dst, ar_send, ar_recv, m * 20 + i, to)
            started.append(copy)
            return copy

        core_send[m] = grads[m, pl.ds(away_at, 256), :].astype(BF)
        flying = [send(0, core_send.at[m], core_recv.at[m], other)]
        yield
        flying[0].wait_recv()
        acc1[m, 0:256, :] = grads[m, pl.ds(half_at, 256), :] + core_recv[m].astype(F32)
        send1[m] = acc1[m, 0:256, :].astype(BF)
        flying = []
        for by in range(1, 4):
            rows = pl.ds(pl.multiple_of(lax.rem(at1 + by, 4) * 64, 64), 64)
            flying.append(send(by, send1.at[m, rows], recv1.at[m, by - 1], move1(by)))
        yield
        for copy in flying:
            copy.wait_recv()
        own = acc1[m, pl.ds(pl.multiple_of(at1 * 64, 64), 64), :]
        for j in range(3):
            own = own + recv1[m, j].astype(F32)
        send2[m] = own.astype(BF)
        acc1[m, 0:64, :] = own
        flying = []
        for by in range(1, 4):
            rows = pl.ds(pl.multiple_of(lax.rem(at2 + by, 4) * 16, 16), 16)
            flying.append(send(3 + by, send2.at[m, rows], recv2.at[m, by - 1], move2(by)))
        yield
        for copy in flying:
            copy.wait_recv()
        own = acc1[m, pl.ds(pl.multiple_of(at2 * 16, 16), 16), :]
        for j in range(3):
            own = own + recv2[m, j].astype(F32)
        send3[m] = own.astype(BF)
        acc1[m, 0:16, :] = own
        flying = []
        for by in range(1, 4):
            cols = pl.ds(pl.multiple_of(lax.rem(at3 + by, 4) * 128, 128), 128)
            flying.append(send(6 + by, send3.at[m, :, cols], recv3.at[m, by - 1], move3(by)))
        yield
        for copy in flying:
            copy.wait_recv()
        cols = pl.ds(pl.multiple_of(at3 * 128, 128), 128)
        own = acc1[m, 0:16, cols]
        for j in range(3):
            own = own + recv3[m, j].astype(F32)
        row1 = core * 256
        row2 = row1 + at1 * 64
        row3 = row2 + at2 * 16
        rows1, rows2, rows3 = [pl.ds(pl.multiple_of(r, n), n) for r, n in ((row1, 256), (row2, 64), (row3, 16))]
        total[m, rows3, cols] = (own * factor).astype(BF)
        flying = [send(9 + by, total.at[m, rows3, cols], total.at[m, rows3, cols], move3(by)) for by in range(1, 4)]
        yield
        for copy in flying:
            copy.wait_recv()
        flying = [send(12 + by, total.at[m, rows3], total.at[m, rows3], move2(by)) for by in range(1, 4)]
        yield
        for copy in flying:
            copy.wait_recv()
        flying = [send(15 + by, total.at[m, rows2], total.at[m, rows2], move1(by)) for by in range(1, 4)]
        yield
        for copy in flying:
            copy.wait_recv()
        flying = [send(19, total.at[m, rows1], total.at[m, rows1], other)]
        yield
        flying[0].wait_recv()
        outs.append(local(m, total.at[m], gq_out.at[:, pl.ds((m - 1) * D, D)] if m else gp_out))
        yield

    for half in range(2):
        window_rows(half, 0, nn(to_win[0:WIN, 0:HALF], d_ext[half + 1, 0:HALF, :]), tmp)
    back_pair(0, 0)
    attend_back_pair(0, 0)
    for copy in d_halo:
        copy.wait_recv()
    for half in range(2):
        window_rows(half, 2, nn(to_win[WIN:, :], d_ext[half + 1]), tmp)
    for half in range(2, 4):
        window_rows(half, 0, nn(to_win[...], d_ext[half + 1]), tmp)
    lax.fori_loop(1, 4, back_pair, 0)
    grads[0] = nn(mixed_t[...], d_win[...])
    sums = [summed(0)]
    next(sums[0])
    for i in (1, 2, 3):
        attend_back_pair(i, 0)
        next(sums[0])

    for m in range(3):
        grads[m + 1] = nn(normed_t[...], d_qkv[:, m * D:(m + 1) * D])
        sums.append(summed(m + 1))
        next(sums[m + 1])

    def norm_back_band(band, _):
        rows = pl.ds(pl.multiple_of(band * 576, 576), 576)
        d_norm = nt(d_qkv[rows, :], wq[...])
        centred, inverse = stats(xw[rows, :])
        hat = centred * inverse
        tmp[rows, :] = inverse * (
            d_norm - jnp.mean(d_norm, -1, keepdims=True) - hat * jnp.mean(d_norm * hat, -1, keepdims=True)
        )
        return 0

    roll_halo = []
    for band in (1, 0):
        norm_back_band(band, 0)
        for half in (band * 2 + 1, band * 2):
            roll_halo += to_grid(half, 15, r_send, r_lat, r_pack, r_packr, grid_s)
        for step in sums:
            next(step)

    for copy in merged_out:
        copy.wait_recv()
    for s in range(8):
        merged_all[:, s * 24:(s + 1) * 24, :] = merged_in[s].astype(F32).reshape(12, 24, 128)
    dm_raw[...] = merged_all[...].astype(BF)
    outs.append(local(4, dm_raw, m_out))
    for step in sums:
        next(step)

    for copy in roll_halo:
        copy.wait_recv()
    for hb in range(4):
        at = slice(hb * HALF, (hb + 1) * HALF)
        own = r_lat[...].astype(F32) if hb == 0 else take(grid_s, at)
        put(d_str, at, take(d_str, at) + own + nn(unpack[...], r_packr[hb]))
        for lev in range(LEV):
            for c in range(4):
                src = d_str.at[c, pl.ds(hb * HALF + lev * 144, 144)]
                to = gx_out.at[lev, pl.ds(hb * 144, 144), pl.ds(c * 128, 128)]
                outs.append(local(5 + hb * 8 + lev * 4 + c, src, to))
        for step in sums:
            next(step, None)
    for _ in range(8):
        for step in sums:
            next(step, None)

    for copy in started:
        copy.wait_send()
    for copy in outs:
        copy.wait()


def vmem(*shape, dtype=BF):
    return pltpu.VMEM(shape, dtype)


SCRATCH = [
    vmem(5, EXT, 640), vmem(4, PACK, 640), vmem(12, 48, dtype=jnp.int32), vmem(D, 3 * D), vmem(D, D), vmem(4 * D, D2),
    vmem(12, 192, 128), vmem(8, CELLS, 128), vmem(CELLS, D2), vmem(HALF, EXT), vmem(EXT, HALF), vmem(PACK, HALF), vmem(HALF, PACK),
    vmem(TOK, D, dtype=F32), vmem(TOK, 128, dtype=F32), vmem(TOK, D), vmem(TOK, D), vmem(TOK, D), vmem(TOK, D),
    vmem(2, 1152, 256), vmem(2, 1152, 256), vmem(2, 1152, 128, dtype=F32), vmem(8, WIN, 1152, dtype=F32), vmem(D, TOK), vmem(D, TOK), vmem(TOK, D), vmem(TOK, D, dtype=F32),
    vmem(HALF, D), vmem(4, PACK, D), vmem(HALF, D), vmem(4, PACK, D),
    vmem(4, TOK, 128, dtype=F32), vmem(4, CELLS, D, dtype=F32), vmem(4, CELLS, D, dtype=F32), vmem(4, TOK, 128, dtype=F32),
    vmem(5, EXT, D), vmem(4, PACK, D), vmem(TOK, D), vmem(TOK, D), vmem(TOK, 3 * D), vmem(8, CELLS, 128), vmem(8, CELLS, 128), vmem(12, 192, 128, dtype=F32),
    vmem(HALF, D), vmem(4, PACK, D), vmem(HALF, D), vmem(4, PACK, D),
    vmem(4, D, D, dtype=F32), vmem(4, 256, D), vmem(4, 256, D), vmem(4, 256, D),
    vmem(4, 3, 64, D), vmem(4, 64, D), vmem(4, 3, 16, D), vmem(4, 16, D), vmem(4, 3, 16, 128), vmem(4, D, D),
    pltpu.SemaphoreType.DMA((38,)), pltpu.SemaphoreType.DMA((20,)), pltpu.SemaphoreType.DMA((20,)),
    pltpu.SemaphoreType.DMA((14,)), pltpu.SemaphoreType.DMA((14,)),
    pltpu.SemaphoreType.DMA((80,)), pltpu.SemaphoreType.DMA((80,)),
]


def per_device(tokens, region, w_qkv, w_proj, w_merge, d_merged):
    levels, lat_rows, lon_cols, feature = tokens.shape
    to_win, pack = one_hots()
    consts = [jnp.asarray(a, BF) for a in (to_win, to_win.T, pack, pack.T)]
    anywhere = pl.BlockSpec(memory_space=pl.ANY)
    m_out, gx_out, gq_out, gp_out = pl.pallas_call(
        kernel,
        out_shape=(
            jax.ShapeDtypeStruct((12, 192, 128), BF),
            jax.ShapeDtypeStruct((levels, 576, feature), F32),
            jax.ShapeDtypeStruct((D, 3 * D), BF),
            jax.ShapeDtypeStruct((D, D), BF),
        ),
        in_specs=[anywhere] * 10,
        out_specs=(anywhere,) * 4,
        scratch_shapes=SCRATCH,
        compiler_params=pltpu.CompilerParams(
            collective_id=0, has_side_effects=True, vmem_limit_bytes=64 * 1024 * 1024
        ),
    )(
        tokens.reshape(levels, 576, feature), region, w_qkv, w_proj, w_merge,
        d_merged.reshape(12, 192, 128), *consts,
    )
    merged = m_out.reshape(levels, 6, 192, 128)
    grad_x = gx_out.reshape(levels, lat_rows, lon_cols, feature)
    return (merged, grad_x, gq_out.astype(F32), gp_out.astype(F32))


def solution(mesh):
    in_specs = (
        P(None, "lat", "lon", None),
        P("lat", "lon"),
        P(),
        P(),
        P(),
        P(None, "lat", None, "lon"),
    )
    out_specs = (P(None, "lat", None, "lon"), P(None, "lat", "lon", None), P(), P())
    return jax.shard_map(
        per_device, mesh=mesh, in_specs=in_specs, out_specs=out_specs, check_vma=False
    )
```

```python
import functools

import jax
import jax.numpy as jnp
import numpy as np
from jax import lax
from jax.experimental import pallas as pl
from jax.experimental.pallas import tpu as pltpu
from jax.sharding import PartitionSpec as P

D = 512
D2 = 1024
HEADS = 8
LEV = 2
WIN_LAT = 6
WIN_LON = 12
EPS = 1e-05

HALF = 288
PACK = 48
EXT = HALF + PACK
WIN = 144
TOK = 1152
CELLS = 288
BF = jnp.bfloat16
F32 = jnp.float32
MESH = pl.DeviceIdType.MESH


CHUNK_LANE = (0, 0, 128, 256, 256)
SEGMENTS = []
for _head in range(HEADS):
    _at = _head * WIN
    while _at < (_head + 1) * WIN:
        _end = min((_at // 256 + 1) * 256, (_head + 1) * WIN)
        SEGMENTS.append((_head, _at, _end))
        _at = _end


def one_hots():
    to_win = np.zeros((HALF, EXT), np.float32)
    pack = np.zeros((PACK, HALF), np.float32)
    for wc in range(4):
        for lr in range(6):
            for cw in range(WIN_LON):
                u = wc * 72 + lr * WIN_LON + cw
                col = WIN_LON * wc + WIN_LON // 2 + cw
                to_win[u, lr * 48 + col if col < 48 else HALF + lr * 6 + col - 48] = 1.0
    for lr in range(6):
        for c in range(6):
            pack[lr * 6 + c, lr * 48 + c] = 1.0
    return to_win, pack


def nn(a, b):
    return lax.dot_general(a, b, (((1,), (0,)), ((), ())), preferred_element_type=F32)


def nt(a, b):
    return lax.dot_general(a, b, (((1,), (1,)), ((), ())), preferred_element_type=F32)


def tn(a, b):
    return lax.dot_general(a, b, (((0,), (0,)), ((), ())), preferred_element_type=F32)


def take(ref, rows):
    return jnp.concatenate([ref[c, rows, :] for c in range(4)], 1)


def put(ref, rows, value):
    for c in range(4):
        ref[c, rows, :] = value[:, c * 128:(c + 1) * 128]


def stats(x):
    average = jnp.mean(x, -1, keepdims=True)
    centred = x - average
    variance = jnp.mean(centred * centred, -1, keepdims=True)
    return centred, lax.rsqrt(variance + EPS)


def kernel(
    tokens, region, w_qkv_h, w_proj_h, w_merge_h, d_merged, to_win_h, from_win_h, pack_h, unpack_h,
    m_out, gx_out, gq_out, gp_out,
    ext, packs, regions, wq, wp, wm, dm_raw, dm_send, dm_recv, to_win, from_win, pack, unpack,
    xw, keyw, normed, q, k, v, block_q, block_d, staged, soft, mixed_t, normed_t, mixed, tmp, b_send, b_pack, b_lat, b_packr,
    grid_s, g, d_in, d_str, d_ext, d_packs, d_win, d_mix, d_qkv, merged, merged_in, merged_all,
    r_send, r_pack, r_lat, r_packr,
    grads, core_send, core_recv, send1, recv1, send2, recv2, total,
    local_sem, halo_send, halo_recv, a2a_send, a2a_recv, ar_send, ar_recv,
):
    lat = lax.axis_index("lat")
    lon = lax.axis_index("lon")
    core = lax.rem(lat, 2)
    z_at = lax.rem(lax.div(lat, 2), 4)
    y_lo = lax.div(lat, 8)
    x_at = lax.div(lon, 2)
    y_at = lax.rem(lon, 2) * 2 + y_lo

    south = lax.rem(lat + 1, 16)
    north = lax.rem(lat + 15, 16)
    east = lax.rem(lon + 1, 8)
    west = lax.rem(lon + 7, 8)

    places = {"x": x_at, "y": y_at, "z": z_at}

    def moved_by(steps):
        x, y, z = [lax.rem(places[axis] + steps[axis], 4) if steps.get(axis) else places[axis] for axis in "xyz"]
        return (lax.rem(y, 2) * 8 + z * 2 + core, x * 2 + lax.div(y, 2))

    def on_z(by):
        return moved_by({"z": by})

    def on_y(by):
        return moved_by({"y": by})

    def on_x(by):
        return moved_by({"x": by})

    def on_plane(order, b2, b3):
        return moved_by({order[1]: b2, order[2]: b3})

    def local(i, src, dst):
        copy = pltpu.make_async_copy(src, dst, local_sem.at[i])
        copy.start()
        return copy

    def remote(src, dst, sends, recvs, i, to):
        copy = pltpu.make_async_remote_copy(
            src_ref=src, dst_ref=dst, send_sem=sends.at[i], recv_sem=recvs.at[i], device_id=to, device_id_type=MESH
        )
        copy.start()
        return copy

    started = []

    loads = []
    for hb in range(4):
        for lev in range(LEV):
            rows, place = pl.ds(hb * 144, 144), pl.ds(lev * 144, 144)
            loads.append(local(len(loads), tokens.at[lev, rows], ext.at[hb, place, pl.ds(0, D)]))
    for src, dst in ((region, regions), (pack_h, pack), (to_win_h, to_win), (d_merged, dm_raw), (w_qkv_h, wq), (w_merge_h, wm),
                     (w_proj_h, wp), (from_win_h, from_win), (unpack_h, unpack)):
        loads.append(local(len(loads), src, dst))
    grid_loads, (l_reg, l_pack, l_to, l_dm, l_wq, l_wm, l_wp, l_from, l_un) = loads[:8], loads[8:]

    barrier = pltpu.get_barrier_semaphore()
    peers = [(south, lon), (north, lon), (south, east), (north, west)]
    peers += [(lat, lax.rem(lon + by, 8)) for by in range(1, 8)]
    peers += [on_z(by) for by in (1, 2, 3)] + [on_y(by) for by in (1, 3)]
    for first, second in ("xy", "yz", "xz"):
        for b2 in range(1, 4):
            for b3 in range(1, 4):
                if (first, second, b3) != ("x", "y", 2):
                    peers.append(moved_by({first: b2, second: b3}))
    for peer in peers:
        pl.semaphore_signal(barrier, inc=1, device_id=peer, device_id_type=MESH)

    for copy in grid_loads:
        copy.wait()
    l_reg.wait()
    corner = lax.broadcasted_iota(jnp.int32, (48, 48), 0) == lax.broadcasted_iota(jnp.int32, (48, 48), 1)
    for row in range(12):
        column = jnp.sum(jnp.where(corner, regions[row:row + 1, :].astype(F32), 0.0), 1, keepdims=True)
        if row < WIN_LAT // 2:
            column = column + jnp.where(lat == 0, 4.0, 0.0)
        for lev in range(LEV):
            at = lev * 144 + row % 3 * 48
            ext[row // 3, at:at + 48, D:] = jnp.broadcast_to(column, (48, 128)).astype(BF)
    l_pack.wait()
    for hb in range(4):
        packs[hb] = nn(pack[...], ext[hb, 0:HALF, :]).astype(BF)
    pl.semaphore_wait(barrier, len(peers))

    def send_halo(full, small, base):
        out = [remote(full.at[0, pl.ds(0, HALF)], full.at[4, pl.ds(0, HALF)], halo_send, halo_recv, base, (north, lon))]
        for hb in range(4):
            to = (north, west) if hb == 0 else (lat, west)
            out.append(remote(small.at[hb], full.at[hb if hb else 4, pl.ds(HALF, PACK)], halo_send, halo_recv, base + 1 + hb, to))
        started.extend(out)
        return out

    halo = send_halo(ext, packs, 0)

    l_dm.wait()
    for s in range(8):
        part = dm_raw[:, s * 24:(s + 1) * 24, :].astype(F32)
        dm_send[s] = part.reshape(CELLS, 128).astype(BF)
    def window_rows(half, first, moved, wide):
        for i in range(moved.shape[0] // 72):
            at = ((half // 2) * 4 + first + i) * WIN + (half % 2) * 72
            wide[at:at + 72, :] = moved[i * 72:(i + 1) * 72, :D]
            if moved.shape[1] > D:
                keyw[at:at + 72, :] = moved[i * 72:(i + 1) * 72, D:]

    def norm_window(w, _):
        rows = pl.ds(pl.multiple_of(w * WIN, WIN), WIN)
        centred, inverse = stats(xw[rows, :])
        normed[rows, :] = (centred * inverse).astype(BF)
        return 0

    def project_pair(i, _):
        rows = pl.ds(pl.multiple_of(i * 288, 288), 288)
        block = normed[rows, :]
        q[rows, :] = (nn(block, wq[:, 0:D]).astype(BF) * 0.125).astype(BF)
        k[rows, :] = nn(block, wq[:, D:2 * D]).astype(BF)
        v[rows, :] = nn(block, wq[:, 2 * D:3 * D]).astype(BF)
        return 0

    lane = lax.broadcasted_iota(jnp.int32, (WIN, 128), 1)
    low = lane < 64

    def spread(ref, rows, src, filler):
        blank = jnp.zeros((WIN, 128), BF)
        for head, first, last in SEGMENTS:
            chunk, at = first // 256, pl.ds(first, last - first)
            part = slice(first - head * WIN, last - head * WIN)
            own = src[rows, (head // 2) * 128:(head // 2 + 1) * 128]
            own = jnp.where(low if head % 2 == 0 else ~low, own, blank)
            block = head // 2 - CHUNK_LANE[chunk] // 128
            fill = blank if filler is None else filler
            if chunk == 0:
                ref[at, 0:128] = own[part]
                ref[at, 128:256] = fill[part]
            else:
                ref[at, 0:128] = (jnp.where(low, fill, own) if block == 0 else fill)[part]
                ref[at, 128:256] = (own if block == 1 else blank)[part]

    def by_heads(stage, left, right, chunk):
        out = tn(left, right[:, CHUNK_LANE[chunk]:CHUNK_LANE[chunk] + 256])
        for head, first, last in SEGMENTS:
            if first // 256 == chunk:
                block = head // 2 - CHUNK_LANE[chunk] // 128
                rows = slice(first - chunk * 256, last - chunk * 256)
                stage[first:last, :] = out[rows, block * 128:(block + 1) * 128]

    def joined(stage, pair):
        even, odd = 2 * pair * WIN, (2 * pair + 1) * WIN
        return jnp.where(low, stage[even:even + WIN, :], stage[odd:odd + WIN, :])

    def attend(w, q_b, stage):
        rows = pl.ds(pl.multiple_of(w * WIN, WIN), WIN)
        same = keyw[rows, :] == lane.astype(F32)
        differ = jnp.where(same | ~low, 0.0, 1.0).astype(BF)
        forbid = jnp.where(same, -1e30, 0.0).astype(BF)
        spread(q_b, rows, q, differ)
        k_b = [k[rows, i * 128:(i + 1) * 128] for i in range(4)]
        k_x = [jnp.concatenate([k_b[0], jnp.where(low, forbid, k_b[1])], 1)]
        k_x += [jnp.concatenate([jnp.where(low, forbid, k_b[i]), k_b[i + 1]], 1) for i in range(3)]
        values = v[rows, :]
        for chunk in range(5):
            cols = slice(chunk * 256, min(chunk * 256 + 256, 1152))
            raw = jnp.exp(nt(k_x[min(chunk, 3)], q_b[cols, :]))
            total_w = jnp.sum(raw, 0, keepdims=True)
            shrink = jnp.where(total_w > 1.0, 2.0 ** -32, 1.0)
            part = (raw * shrink) * (1.0 / (total_w * shrink))
            soft[w, :, cols] = part
            by_heads(stage, part.astype(BF), values, chunk)
        for pair in range(4):
            mixed[rows, pair * 128:(pair + 1) * 128] = joined(stage, pair).astype(BF)

    def attend_pair(i, _):
        attend(2 * i, block_q.at[0], staged.at[0])
        attend(2 * i + 1, block_q.at[1], staged.at[1])
        return 0

    l_to.wait()
    for half in range(2):
        window_rows(half, 0, nn(to_win[0:WIN, 0:HALF], ext[half + 1, 0:HALF, :]), xw)
    lax.fori_loop(0, 2, norm_window, 0)
    l_wq.wait()
    project_pair(0, 0)
    attend_pair(0, 0)

    for copy in halo:
        copy.wait_recv()
    mine = pl.ds(pl.multiple_of(lon * 128, 128), 128)
    a2a_in = []
    for by in range(1, 8):
        to = lax.rem(lon + by, 8)
        a2a_in.append(remote(dm_send.at[to], dm_recv.at[:, mine], a2a_send, a2a_recv, by - 1, (lat, to)))
    started.extend(a2a_in)
    dm_recv[:, mine] = dm_send[lon]
    for half in range(2):
        window_rows(half, 2, nn(to_win[WIN:, :], ext[half + 1]), xw)
    for half in range(2, 4):
        window_rows(half, 0, nn(to_win[...], ext[half + 1]), xw)
    lax.fori_loop(2, 8, norm_window, 0)
    lax.fori_loop(1, 4, project_pair, 0)
    lax.fori_loop(2, 4, attend_pair, 0)

    l_wp.wait()
    l_from.wait()
    l_un.wait()

    def to_grid(half, base, lat_send, lat_recv, pack_send, pack_recv, keep):
        first = (half // 2) * 4
        block = jnp.concatenate([tmp[(first + wc) * WIN + (half % 2) * 72:(first + wc) * WIN + (half % 2) * 72 + 72, :] for wc in range(4)], 0)
        moved = nn(from_win[...], block.astype(BF))
        pack_send[half] = moved[HALF:, :].astype(BF)
        out = []
        if half == 3:
            lat_send[...] = moved[:HALF, :].astype(BF)
            out.append(remote(lat_send, lat_recv, halo_send, halo_recv, base, (south, lon)))
            out.append(remote(pack_send.at[3], pack_recv.at[0], halo_send, halo_recv, base + 1, (south, east)))
        else:
            put(keep, slice((half + 1) * HALF, (half + 2) * HALF), moved[:HALF, :])
            out.append(remote(pack_send.at[half], pack_recv.at[half + 1], halo_send, halo_recv, base + 2 + half, (lat, east)))
        started.extend(out)
        return out

    branch_halo = []
    for band in (1, 0):
        if band == 0:
            attend_pair(1, 0)
        rows = slice(band * 576, (band + 1) * 576)
        tmp[rows, :] = nn(mixed[rows, :], wp[...])
        for half in (band * 2 + 1, band * 2):
            branch_halo += to_grid(half, 5, b_send, b_lat, b_pack, b_packr, grid_s)

    l_wm.wait()
    for copy in a2a_in:
        copy.wait_recv()

    def d_in_part(p, _):
        d_in[p] = nt(dm_recv[...], wm[pl.ds(pl.multiple_of(p * D, D), D), :])
        return 0

    lax.fori_loop(0, 4, d_in_part, 0)
    for i in range(9):
        rows = slice(i * 128, (i + 1) * 128)
        normed_t[:, rows] = normed[rows, :].T
        mixed_t[:, rows] = mixed[rows, :].T

    for copy in branch_halo:
        copy.wait_recv()
    for hb in range(4):
        at = slice(hb * HALF, (hb + 1) * HALF)
        own = b_lat[...].astype(F32) if hb == 0 else take(grid_s, at)
        full = own + nn(unpack[...], b_packr[hb])
        put(grid_s, at, (ext[hb, 0:HALF, 0:D].astype(F32) + full).astype(BF).astype(F32))

    def cell_rows(p, lev, i):
        row = 2 * i + p % 2
        return ((row // 3 * 2 + lev) * 3 + row % 3) * 48 + p // 2

    for p in range(4):
        for lev in range(LEV):
            for i in range(6):
                at = (lev * 6 + i) * 24
                g[p, at:at + 24, :] = take(grid_s, pl.ds(cell_rows(p, lev, i), 24, stride=2))

    average = sum(jnp.sum(g[p], -1, keepdims=True) for p in range(4)) / (4 * D)
    variance = 0.0
    for p in range(4):
        centred = g[p] - average
        variance = variance + jnp.sum(centred * centred, -1, keepdims=True)
    inverse = lax.rsqrt(variance / (4 * D) + EPS)
    mean_d = sum(jnp.sum(d_in[p], -1, keepdims=True) for p in range(4)) / (4 * D)
    mean_dh = sum(jnp.sum(d_in[p] * ((g[p] - average) * inverse), -1, keepdims=True) for p in range(4)) / (4 * D)
    for p in range(4):
        hat = (g[p] - average) * inverse
        d_part = inverse * (d_in[p] - mean_d - hat * mean_dh)
        g[p] = hat
        for lev in range(LEV):
            for i in range(6):
                at = (lev * 6 + i) * 24
                put(d_str, pl.ds(cell_rows(p, lev, i), 24, stride=2), d_part[at:at + 24, :])

    for hb in range(4):
        d_ext[hb, 0:HALF, :] = take(d_str, slice(hb * HALF, (hb + 1) * HALF)).astype(BF)
    for hb in range(4):
        d_packs[hb] = nn(pack[...], d_ext[hb, 0:HALF, :]).astype(BF)
    d_halo = send_halo(d_ext, d_packs, 10)

    for n in range(2):
        cols = slice(n * 512, (n + 1) * 512)
        sums = nn(g[0].astype(BF), wm[0:D, cols])
        for p in range(1, 4):
            sums = sums + nn(g[p].astype(BF), wm[p * D:(p + 1) * D, cols])
        for s in range(4):
            merged[n * 4 + s] = sums[:, s * 128:(s + 1) * 128].astype(BF)
    def back_pair(i, _):
        rows = pl.ds(pl.multiple_of(i * 288, 288), 288)
        block = tmp[rows, :].astype(BF)
        d_win[rows, :] = block
        d_mix[rows, :] = nt(block, wp[...]).astype(BF)
        return 0

    def attend_back(w, q_b, d_b, stage):
        rows = pl.ds(pl.multiple_of(w * WIN, WIN), WIN)
        spread(q_b, rows, q, None)
        spread(d_b, rows, d_mix, None)
        keys, values = k[rows, :], v[rows, :]
        d_k, d_v = [], []
        for chunk in range(5):
            cols = slice(chunk * 256, min(chunk * 256 + 256, 1152))
            part = soft[w, :, cols]
            d_soft = nt(values[:, CHUNK_LANE[chunk]:CHUNK_LANE[chunk] + 256], d_b[cols, :])
            delta = jnp.sum(part * d_soft, 0, keepdims=True)
            d_s = (part * (d_soft - delta)).astype(BF)
            d_v.append(nn(part.astype(BF), d_b[cols, :]))
            d_k.append(nn(d_s, q_b[cols, :]))
            by_heads(stage, d_s, keys, chunk)
        for which, d in ((1, d_k), (2, d_v)):
            both = [d[0][:, 0:128] + d[1][:, 0:128], d[1][:, 128:256] + d[2][:, 0:128],
                    d[2][:, 128:256] + d[3][:, 0:128] + d[4][:, 0:128], d[3][:, 128:256] + d[4][:, 128:256]]
            for pair in range(4):
                d_qkv[rows, which * D + pair * 128:which * D + (pair + 1) * 128] = both[pair].astype(BF)
        for pair in range(4):
            d_qkv[rows, pair * 128:(pair + 1) * 128] = (joined(stage, pair) * 0.125).astype(BF)

    def attend_back_pair(i, _):
        attend_back(2 * i, block_q.at[0], block_d.at[0], staged.at[0])
        attend_back(2 * i + 1, block_q.at[1], block_d.at[1], staged.at[1])
        return 0

    orders = (("z", "y", "x"), ("y", "x", "z"), ("x", "z", "y"), ("z", "x", "y"))
    along = {"z": (on_z, z_at), "y": (on_y, y_at), "x": (on_x, x_at)}
    acc1 = d_in
    other = (lat + 1 - 2 * core, lon)
    half_at = pl.multiple_of(core * 256, 256)
    away_at = pl.multiple_of((1 - core) * 256, 256)
    factor = float(LEV * 192 * 384) ** -0.5
    outs = []

    def summed(m):
        (move1, at1), (_, at2), (_, at3) = [along[axis] for axis in orders[m]]

        def send(i, src, dst, to):
            copy = remote(src, dst, ar_send, ar_recv, m * 38 + i, to)
            started.append(copy)
            return copy

        core_send[m] = grads[m, pl.ds(away_at, 256), :].astype(BF)
        flying = [send(0, core_send.at[m], core_recv.at[m], other)]
        yield
        flying[0].wait_recv()
        acc1[m, 0:256, :] = grads[m, pl.ds(half_at, 256), :] + core_recv[m].astype(F32)
        send1[m] = acc1[m, 0:256, :].astype(BF)
        flying = []
        for by in range(1, 4):
            rows = pl.ds(pl.multiple_of(lax.rem(at1 + by, 4) * 64, 64), 64)
            flying.append(send(by, send1.at[m, rows], recv1.at[m, by - 1], move1(by)))
        yield
        for copy in flying:
            copy.wait_recv()
        own = acc1[m, pl.ds(pl.multiple_of(at1 * 64, 64), 64), :]
        for j in range(3):
            own = own + recv1[m, j].astype(F32)
        send2[m] = own.astype(BF)
        acc1[m, 0:64, :] = own
        rest = [(b2, b3) for b2 in range(4) for b3 in range(4) if (b2, b3) != (0, 0)]
        flying = []
        for i, (b2, b3) in enumerate(rest):
            rows = pl.ds(pl.multiple_of(lax.rem(at2 + b2, 4) * 16, 16), 16)
            cols = pl.ds(pl.multiple_of(lax.rem(at3 + b3, 4) * 128, 128), 128)
            flying.append(send(4 + i, send2.at[m, rows, cols], recv2.at[m, i], on_plane(orders[m], b2, b3)))
        yield
        for copy in flying:
            copy.wait_recv()
        row1 = core * 256
        row2 = row1 + at1 * 64
        row3 = row2 + at2 * 16
        rows1, rows2, rows3 = [pl.ds(pl.multiple_of(r, n), n) for r, n in ((row1, 256), (row2, 64), (row3, 16))]
        cols = pl.ds(pl.multiple_of(at3 * 128, 128), 128)
        own = acc1[m, pl.ds(pl.multiple_of(at2 * 16, 16), 16), cols]
        for j in range(15):
            own = own + recv2[m, j].astype(F32)
        total[m, rows3, cols] = (own * factor).astype(BF)
        piece = total.at[m, rows3, cols]
        flying = [send(19 + i, piece, piece, on_plane(orders[m], b2, b3)) for i, (b2, b3) in enumerate(rest)]
        yield
        for copy in flying:
            copy.wait_recv()
        flying = [send(33 + by, total.at[m, rows2], total.at[m, rows2], move1(by)) for by in range(1, 4)]
        yield
        for copy in flying:
            copy.wait_recv()
        flying = [send(37, total.at[m, rows1], total.at[m, rows1], other)]
        yield
        flying[0].wait_recv()
        grads[m] = total[m].astype(F32)
        outs.append(local(m, grads.at[m], gq_out.at[:, pl.ds((m - 1) * D, D)] if m else gp_out))
        yield

    for half in range(2):
        window_rows(half, 0, nn(to_win[0:WIN, 0:HALF], d_ext[half + 1, 0:HALF, :]), tmp)
    back_pair(0, 0)
    attend_back_pair(0, 0)
    for copy in d_halo:
        copy.wait_recv()
    for by in range(1, 8):
        to = lax.rem(lon + by, 8)
        started.append(remote(merged.at[to], merged_in.at[lon], a2a_send, a2a_recv, 6 + by, (lat, to)))
    merged_out = started[-7:]
    merged_in[lon] = merged[lon]
    for half in range(2):
        window_rows(half, 2, nn(to_win[WIN:, :], d_ext[half + 1]), tmp)
    for half in range(2, 4):
        window_rows(half, 0, nn(to_win[...], d_ext[half + 1]), tmp)
    lax.fori_loop(1, 4, back_pair, 0)
    grads[0] = nn(mixed_t[...], d_win[...])
    sums = [summed(0)]
    next(sums[0])
    for i in (1, 2, 3):
        attend_back_pair(i, 0)
        if i != 2:
            next(sums[0])

    for m in range(3):
        grads[m + 1] = nn(normed_t[...], d_qkv[:, m * D:(m + 1) * D])
        sums.append(summed(m + 1))
        next(sums[m + 1])

    def norm_back_band(band, _):
        rows = pl.ds(pl.multiple_of(band * 576, 576), 576)
        d_norm = nt(d_qkv[rows, :], wq[...])
        centred, inverse = stats(xw[rows, :])
        hat = centred * inverse
        tmp[rows, :] = inverse * (
            d_norm - jnp.mean(d_norm, -1, keepdims=True) - hat * jnp.mean(d_norm * hat, -1, keepdims=True)
        )
        return 0

    roll_halo = []
    for band in (1, 0):
        norm_back_band(band, 0)
        for half in (band * 2 + 1, band * 2):
            roll_halo += to_grid(half, 15, r_send, r_lat, r_pack, r_packr, grid_s)
        for step in sums:
            next(step)

    for copy in merged_out:
        copy.wait_recv()
    for s in range(8):
        merged_all[:, s * 24:(s + 1) * 24, :] = merged_in[s].astype(F32).reshape(12, 24, 128)
    dm_raw[...] = merged_all[...].astype(BF)
    outs.append(local(4, dm_raw, m_out))
    for step in sums:
        next(step)

    for copy in roll_halo:
        copy.wait_recv()
    for hb in range(4):
        at = slice(hb * HALF, (hb + 1) * HALF)
        own = r_lat[...].astype(F32) if hb == 0 else take(grid_s, at)
        put(d_str, at, take(d_str, at) + own + nn(unpack[...], r_packr[hb]))
        for lev in range(LEV):
            for c in range(4):
                src = d_str.at[c, pl.ds(hb * HALF + lev * 144, 144)]
                to = gx_out.at[lev, pl.ds(hb * 144, 144), pl.ds(c * 128, 128)]
                outs.append(local(5 + hb * 8 + lev * 4 + c, src, to))
        for step in sums:
            next(step, None)
    for _ in range(8):
        for step in sums:
            next(step, None)

    for copy in started:
        copy.wait_send()
    for copy in outs:
        copy.wait()


def vmem(*shape, dtype=BF):
    return pltpu.VMEM(shape, dtype)


SCRATCH = [
    vmem(5, EXT, 640), vmem(4, PACK, 640), vmem(12, 48, dtype=jnp.int32), vmem(D, 3 * D), vmem(D, D), vmem(4 * D, D2),
    vmem(12, 192, 128), vmem(8, CELLS, 128), vmem(CELLS, D2), vmem(HALF, EXT), vmem(EXT, HALF), vmem(PACK, HALF), vmem(HALF, PACK),
    vmem(TOK, D, dtype=F32), vmem(TOK, 128, dtype=F32), vmem(TOK, D), vmem(TOK, D), vmem(TOK, D), vmem(TOK, D),
    vmem(2, 1152, 256), vmem(2, 1152, 256), vmem(2, 1152, 128, dtype=F32), vmem(8, WIN, 1152, dtype=F32), vmem(D, TOK), vmem(D, TOK), vmem(TOK, D), vmem(TOK, D, dtype=F32),
    vmem(HALF, D), vmem(4, PACK, D), vmem(HALF, D), vmem(4, PACK, D),
    vmem(4, TOK, 128, dtype=F32), vmem(4, CELLS, D, dtype=F32), vmem(4, CELLS, D, dtype=F32), vmem(4, TOK, 128, dtype=F32),
    vmem(5, EXT, D), vmem(4, PACK, D), vmem(TOK, D), vmem(TOK, D), vmem(TOK, 3 * D), vmem(8, CELLS, 128), vmem(8, CELLS, 128), vmem(12, 192, 128, dtype=F32),
    vmem(HALF, D), vmem(4, PACK, D), vmem(HALF, D), vmem(4, PACK, D),
    vmem(4, D, D, dtype=F32), vmem(4, 256, D), vmem(4, 256, D), vmem(4, 256, D),
    vmem(4, 3, 64, D), vmem(4, 64, D), vmem(4, 15, 16, 128), vmem(4, D, D),
    pltpu.SemaphoreType.DMA((38,)), pltpu.SemaphoreType.DMA((20,)), pltpu.SemaphoreType.DMA((20,)),
    pltpu.SemaphoreType.DMA((14,)), pltpu.SemaphoreType.DMA((14,)),
    pltpu.SemaphoreType.DMA((152,)), pltpu.SemaphoreType.DMA((152,)),
]


def per_device(tokens, region, w_qkv, w_proj, w_merge, d_merged):
    levels, lat_rows, lon_cols, feature = tokens.shape
    to_win, pack = one_hots()
    consts = [jnp.asarray(a, BF) for a in (to_win, to_win.T, pack, pack.T)]
    anywhere = pl.BlockSpec(memory_space=pl.ANY)
    m_out, gx_out, gq_out, gp_out = pl.pallas_call(
        kernel,
        out_shape=(
            jax.ShapeDtypeStruct((12, 192, 128), BF),
            jax.ShapeDtypeStruct((levels, 576, feature), F32),
            jax.ShapeDtypeStruct((D, 3 * D), F32),
            jax.ShapeDtypeStruct((D, D), F32),
        ),
        in_specs=[anywhere] * 10,
        out_specs=(anywhere,) * 4,
        scratch_shapes=SCRATCH,
        compiler_params=pltpu.CompilerParams(
            collective_id=0, has_side_effects=True, vmem_limit_bytes=64 * 1024 * 1024
        ),
    )(
        tokens.reshape(levels, 576, feature), region, w_qkv, w_proj, w_merge,
        d_merged.reshape(12, 192, 128), *consts,
    )
    merged = m_out.reshape(levels, 6, 192, 128)
    grad_x = gx_out.reshape(levels, lat_rows, lon_cols, feature)
    return (merged, grad_x, gq_out, gp_out)


def solution(mesh):
    in_specs = (
        P(None, "lat", "lon", None),
        P("lat", "lon"),
        P(),
        P(),
        P(),
        P(None, "lat", None, "lon"),
    )
    out_specs = (P(None, "lat", None, "lon"), P(None, "lat", "lon", None), P(), P())
    return jax.shard_map(
        per_device, mesh=mesh, in_specs=in_specs, out_specs=out_specs, check_vma=False
    )
```

```python
import functools

import jax
import jax.numpy as jnp
import numpy as np
from jax import lax
from jax.experimental import pallas as pl
from jax.experimental.pallas import tpu as pltpu
from jax.sharding import PartitionSpec as P

D = 512
D2 = 1024
HEADS = 8
LEV = 2
WIN_LAT = 6
WIN_LON = 12
EPS = 1e-05

HALF = 288
EDGE = 36
PACK = 48
SIDE = 112
WIN = 144
TOK = 1152
CELLS = 288
BF = jnp.bfloat16
F32 = jnp.float32
MESH = pl.DeviceIdType.MESH


CHUNK_LANE = (0, 0, 128, 256, 256)
SEGMENTS = []
for _head in range(HEADS):
    _at = _head * WIN
    while _at < (_head + 1) * WIN:
        _end = min((_at // 256 + 1) * 256, (_head + 1) * WIN)
        SEGMENTS.append((_head, _at, _end))
        _at = _end


def one_hots():
    to_win = np.zeros((HALF, HALF), np.float32)
    from_win = np.zeros((HALF + PACK, HALF), np.float32)
    edge_in = np.zeros((4, 80, SIDE), np.float32)
    pack = np.zeros((PACK, HALF), np.float32)
    unpack = np.zeros((3, HALF, SIDE), np.float32)
    for lr in range(6):
        for wc in range(4):
            for cw in range(WIN_LON):
                u = wc * 72 + lr * WIN_LON + cw
                col = WIN_LON * wc + WIN_LON // 2 + cw
                if col < 48:
                    to_win[u, lr * 48 + col] = from_win[lr * 48 + col, u] = 1.0
                else:
                    at = lr * 6 + col - 48
                    from_win[HALF + at, u] = 1.0
                    for half in range(4):
                        edge_in[half, u - 216, half * EDGE + at if half < 3 else 12 + at] = 1.0
        for c in range(6):
            pack[lr * 6 + c, lr * 48 + c] = 1.0
            for half in range(3):
                unpack[half, lr * 48 + c, half * EDGE + lr * 6 + c] = 1.0
    return to_win, from_win, edge_in, pack, unpack, pack.T


def nn(a, b):
    return lax.dot_general(a, b, (((1,), (0,)), ((), ())), preferred_element_type=F32)


def nt(a, b):
    return lax.dot_general(a, b, (((1,), (1,)), ((), ())), preferred_element_type=F32)


def tn(a, b):
    return lax.dot_general(a, b, (((0,), (0,)), ((), ())), preferred_element_type=F32)


def take(ref, rows):
    return jnp.concatenate([ref[c, rows, :] for c in range(4)], 1)


def put(ref, rows, value):
    for c in range(4):
        ref[c, rows, :] = value[:, c * 128:(c + 1) * 128]


def stats(x):
    average = jnp.mean(x, -1, keepdims=True)
    centred = x - average
    variance = jnp.mean(centred * centred, -1, keepdims=True)
    return centred, lax.rsqrt(variance + EPS)


def kernel(
    tokens, region, w_qkv_h, w_proj_h, w_merge_h, d_merged, to_win_h, from_win_h, edge_in_h, pack_h, unpack_h, corner_h,
    m_out, gx_out, gw_out,
    ext, side, corner, regions, wq, wp, wm, dm_raw, dm_send, dm_recv, to_win, from_win, edge_in, pack, unpack, uncorner, loose, packed,
    xw, keyw, normed, q, k, v, block_q, block_d, staged, soft, mixed_t, normed_t, mixed, tmp, b_send, b_diag, b_lat, b_side, b_corner,
    grid_s, g, d_in, d_str, d_ext, d_side, d_corner, d_win, d_mix, d_qkv, merged, merged_in, merged_all,
    r_send, r_diag, r_lat, r_side, r_corner,
    grads, core_send, core_recv, send1, recv1, send2, recv2, total,
    local_sem, halo_send, halo_recv, a2a_send, a2a_recv, ar_send, ar_recv,
):
    lat = lax.axis_index("lat")
    lon = lax.axis_index("lon")
    core = lax.rem(lat, 2)
    z_at = lax.rem(lax.div(lat, 2), 4)
    y_lo = lax.div(lat, 8)
    x_at = lax.div(lon, 2)
    y_at = lax.rem(lon, 2) * 2 + y_lo

    south = lax.rem(lat + 1, 16)
    north = lax.rem(lat + 15, 16)
    east = lax.rem(lon + 1, 8)
    west = lax.rem(lon + 7, 8)

    places = {"x": x_at, "y": y_at, "z": z_at}

    def moved_by(steps):
        x, y, z = [lax.rem(places[axis] + steps[axis], 4) if steps.get(axis) else places[axis] for axis in "xyz"]
        return (lax.rem(y, 2) * 8 + z * 2 + core, x * 2 + lax.div(y, 2))

    def on_z(by):
        return moved_by({"z": by})

    def on_y(by):
        return moved_by({"y": by})

    def on_x(by):
        return moved_by({"x": by})

    def on_plane(order, b2, b3):
        return moved_by({order[1]: b2, order[2]: b3})

    def local(i, src, dst):
        copy = pltpu.make_async_copy(src, dst, local_sem.at[i])
        copy.start()
        return copy

    def remote(src, dst, sends, recvs, i, to):
        copy = pltpu.make_async_remote_copy(
            src_ref=src, dst_ref=dst, send_sem=sends.at[i], recv_sem=recvs.at[i], device_id=to, device_id_type=MESH
        )
        copy.start()
        return copy

    started = []

    loads = []
    for hb in range(4):
        for lev in range(LEV):
            rows, place = pl.ds(hb * 144, 144), pl.ds(lev * 144, 144)
            loads.append(local(len(loads), tokens.at[lev, rows], ext.at[hb, place, pl.ds(0, D)]))
    for src, dst in ((region, regions), (pack_h, pack), (to_win_h, to_win), (d_merged, dm_raw), (w_qkv_h, wq), (w_merge_h, wm),
                     (w_proj_h, wp), (from_win_h, from_win), (unpack_h, unpack), (edge_in_h, edge_in), (corner_h, uncorner)):
        loads.append(local(len(loads), src, dst))
    grid_loads, (l_reg, l_pack, l_to, l_dm, l_wq, l_wm, l_wp, l_from, l_un, l_edge, l_corner) = loads[:8], loads[8:]

    barrier = pltpu.get_barrier_semaphore()
    peers = [(south, lon), (north, lon), (south, east), (north, west)]
    peers += [(lat, lax.rem(lon + by, 8)) for by in range(1, 8)]
    peers += [on_z(by) for by in (1, 2, 3)] + [on_y(by) for by in (1, 3)]
    for first, second in ("xy", "yz", "xz"):
        for b2 in range(1, 4):
            for b3 in range(1, 4):
                if (first, second, b3) != ("x", "y", 2):
                    peers.append(moved_by({first: b2, second: b3}))
    for peer in peers:
        pl.semaphore_signal(barrier, inc=1, device_id=peer, device_id_type=MESH)

    for copy in grid_loads:
        copy.wait()
    l_reg.wait()
    diagonal = lax.broadcasted_iota(jnp.int32, (48, 48), 0) == lax.broadcasted_iota(jnp.int32, (48, 48), 1)
    for row in range(12):
        column = jnp.sum(jnp.where(diagonal, regions[row:row + 1, :].astype(F32), 0.0), 1, keepdims=True)
        if row < WIN_LAT // 2:
            column = column + jnp.where(lat == 0, 4.0, 0.0)
        for lev in range(LEV):
            at = lev * 144 + row % 3 * 48
            ext[row // 3, at:at + 48, D:] = jnp.broadcast_to(column, (48, 128)).astype(BF)
    l_pack.wait()
    def gather_edges(number, full, width):
        for i, hb in enumerate((1, 2, 3, 0)):
            loose[i * EDGE:(i + 1) * EDGE, 0:width] = nn(pack[...], full[hb])[0:EDGE]
        packed[number, :, 0:width] = loose[:, 0:width].astype(BF)

    def send_halo(number, full, to_side, to_corner, width):
        lanes = pl.ds(0, width)
        out = [
            remote(full.at[0], full.at[4], halo_send, halo_recv, number * 3, (north, lon)),
            remote(packed.at[number, pl.ds(0, SIDE), lanes], to_side, halo_send, halo_recv, number * 3 + 1, (lat, west)),
            remote(packed.at[number, pl.ds(96, PACK), lanes], to_corner, halo_send, halo_recv, number * 3 + 2, (north, west)),
        ]
        started.extend(out)
        return out

    gather_edges(0, ext, 640)
    pl.semaphore_wait(barrier, len(peers))
    halo = send_halo(0, ext, side, corner, 640)

    l_dm.wait()
    for s in range(8):
        part = dm_raw[:, s * 24:(s + 1) * 24, :].astype(F32)
        dm_send[s] = part.reshape(CELLS, 128).astype(BF)
    def window_rows(half, first, last, full, to_side, to_corner, wide):
        moved = nn(to_win[first * 72:last * 72, :], full[half + 1])
        for wc in range(first, last):
            at = ((half // 2) * 4 + wc) * WIN + (half % 2) * 72
            part = moved[(wc - first) * 72:(wc - first + 1) * 72, :]
            if wc == 3:
                if half == 3:
                    part = part + nn(edge_in[3, :, 0:PACK], to_corner[...])[0:72]
                else:
                    part = part + nn(edge_in[half], to_side[...])[0:72]
            wide[at:at + 72, :] = part[:, :D]
            if part.shape[1] > D:
                keyw[at:at + 72, :] = part[:, D:]

    def norm_window(w, _):
        rows = pl.ds(pl.multiple_of(w * WIN, WIN), WIN)
        centred, inverse = stats(xw[rows, :])
        normed[rows, :] = (centred * inverse).astype(BF)
        return 0

    def project_pair(i, _):
        rows = pl.ds(pl.multiple_of(i * 288, 288), 288)
        block = normed[rows, :]
        q[rows, :] = (nn(block, wq[:, 0:D]).astype(BF) * 0.125).astype(BF)
        k[rows, :] = nn(block, wq[:, D:2 * D]).astype(BF)
        v[rows, :] = nn(block, wq[:, 2 * D:3 * D]).astype(BF)
        return 0

    lane = lax.broadcasted_iota(jnp.int32, (WIN, 128), 1)
    low = lane < 64

    def spread(ref, rows, src, filler):
        blank = jnp.zeros((WIN, 128), BF)
        for head, first, last in SEGMENTS:
            chunk, at = first // 256, pl.ds(first, last - first)
            part = slice(first - head * WIN, last - head * WIN)
            own = src[rows, (head // 2) * 128:(head // 2 + 1) * 128]
            own = jnp.where(low if head % 2 == 0 else ~low, own, blank)
            block = head // 2 - CHUNK_LANE[chunk] // 128
            fill = blank if filler is None else filler
            if chunk == 0:
                ref[at, 0:128] = own[part]
                ref[at, 128:256] = fill[part]
            else:
                ref[at, 0:128] = (jnp.where(low, fill, own) if block == 0 else fill)[part]
                ref[at, 128:256] = (own if block == 1 else blank)[part]

    def by_heads(stage, left, right, chunk):
        out = tn(left, right[:, CHUNK_LANE[chunk]:CHUNK_LANE[chunk] + 256])
        for head, first, last in SEGMENTS:
            if first // 256 == chunk:
                block = head // 2 - CHUNK_LANE[chunk] // 128
                rows = slice(first - chunk * 256, last - chunk * 256)
                stage[first:last, :] = out[rows, block * 128:(block + 1) * 128]

    def joined(stage, pair):
        even, odd = 2 * pair * WIN, (2 * pair + 1) * WIN
        return jnp.where(low, stage[even:even + WIN, :], stage[odd:odd + WIN, :])

    def attend(w, q_b, stage):
        rows = pl.ds(pl.multiple_of(w * WIN, WIN), WIN)
        same = keyw[rows, :] == lane.astype(F32)
        differ = jnp.where(same | ~low, 0.0, 1.0).astype(BF)
        forbid = jnp.where(same, -1e30, 0.0).astype(BF)
        spread(q_b, rows, q, differ)
        k_b = [k[rows, i * 128:(i + 1) * 128] for i in range(4)]
        k_x = [jnp.concatenate([k_b[0], jnp.where(low, forbid, k_b[1])], 1)]
        k_x += [jnp.concatenate([jnp.where(low, forbid, k_b[i]), k_b[i + 1]], 1) for i in range(3)]
        values = v[rows, :]
        for chunk in range(5):
            cols = slice(chunk * 256, min(chunk * 256 + 256, 1152))
            raw = jnp.exp(nt(k_x[min(chunk, 3)], q_b[cols, :]))
            total_w = jnp.sum(raw, 0, keepdims=True)
            shrink = jnp.where(total_w > 1.0, 2.0 ** -32, 1.0)
            part = (raw * shrink) * (1.0 / (total_w * shrink))
            soft[w, :, cols] = part
            by_heads(stage, part.astype(BF), values, chunk)
        for pair in range(4):
            mixed[rows, pair * 128:(pair + 1) * 128] = joined(stage, pair).astype(BF)

    def attend_pair(i, _):
        attend(2 * i, block_q.at[0], staged.at[0])
        attend(2 * i + 1, block_q.at[1], staged.at[1])
        return 0

    l_to.wait()
    for half in range(2):
        window_rows(half, 0, 2, ext, side, corner, xw)
    lax.fori_loop(0, 2, norm_window, 0)
    l_wq.wait()
    project_pair(0, 0)
    mine = pl.ds(pl.multiple_of(lon * 128, 128), 128)
    a2a_in = []
    for by in range(1, 8):
        to = lax.rem(lon + by, 8)
        a2a_in.append(remote(dm_send.at[to], dm_recv.at[:, mine], a2a_send, a2a_recv, by - 1, (lat, to)))
    started.extend(a2a_in)
    dm_recv[:, mine] = dm_send[lon]
    attend_pair(0, 0)

    for copy in halo:
        copy.wait_recv()
    l_edge.wait()
    for half in range(2):
        window_rows(half, 2, 4, ext, side, corner, xw)
    for half in range(2, 4):
        window_rows(half, 0, 4, ext, side, corner, xw)
    lax.fori_loop(2, 8, norm_window, 0)
    lax.fori_loop(1, 4, project_pair, 0)
    lax.fori_loop(2, 4, attend_pair, 0)

    l_wp.wait()
    l_from.wait()
    l_un.wait()
    l_corner.wait()

    def to_grid(half, number, lat_send, lat_recv, diag_send, to_side, to_corner, keep):
        first = (half // 2) * 4
        block = jnp.concatenate([tmp[(first + wc) * WIN + (half % 2) * 72:(first + wc) * WIN + (half % 2) * 72 + 72, :] for wc in range(4)], 0)
        moved = nn(from_win[...], block.astype(BF))
        out = []
        if half == 3:
            loose[3 * EDGE:, 0:D] = jnp.zeros((EDGE, D), F32)
            diag_send[...] = moved[HALF:, :].astype(BF)
            lat_send[...] = moved[:HALF, :].astype(BF)
            out.append(remote(lat_send, lat_recv, halo_send, halo_recv, number * 3, (south, lon)))
            out.append(remote(diag_send, to_corner, halo_send, halo_recv, number * 3 + 2, (south, east)))
        else:
            put(keep, slice((half + 1) * HALF, (half + 2) * HALF), moved[:HALF, :])
            loose[half * EDGE:(half + 1) * EDGE, 0:D] = moved[HALF:HALF + EDGE, :]
        if half == 0:
            packed[number, :, 0:D] = loose[:, 0:D].astype(BF)
            sides = packed.at[number, pl.ds(0, SIDE), pl.ds(0, D)]
            out.append(remote(sides, to_side, halo_send, halo_recv, number * 3 + 1, (lat, east)))
        started.extend(out)
        return out

    def from_edges(hb, to_side, to_corner):
        return nn(uncorner[...], to_corner[...]) if hb == 0 else nn(unpack[hb - 1], to_side[...])

    branch_halo = []
    for band in (1, 0):
        if band == 0:
            attend_pair(1, 0)
        rows = slice(band * 576, (band + 1) * 576)
        tmp[rows, :] = nn(mixed[rows, :], wp[...])
        for half in (band * 2 + 1, band * 2):
            branch_halo += to_grid(half, 1, b_send, b_lat, b_diag, b_side, b_corner, grid_s)

    l_wm.wait()
    for copy in a2a_in:
        copy.wait_recv()

    def d_in_part(p, _):
        d_in[p] = nt(dm_recv[...], wm[pl.ds(pl.multiple_of(p * D, D), D), :])
        return 0

    lax.fori_loop(0, 4, d_in_part, 0)
    for i in range(9):
        rows = slice(i * 128, (i + 1) * 128)
        normed_t[:, rows] = normed[rows, :].T
        mixed_t[:, rows] = mixed[rows, :].T

    for copy in branch_halo:
        copy.wait_recv()
    for hb in range(4):
        at = slice(hb * HALF, (hb + 1) * HALF)
        own = b_lat[...].astype(F32) if hb == 0 else take(grid_s, at)
        full = own + from_edges(hb, b_side, b_corner)
        put(grid_s, at, (ext[hb, 0:HALF, 0:D].astype(F32) + full).astype(BF).astype(F32))

    def cell_rows(p, lev, i):
        row = 2 * i + p % 2
        return ((row // 3 * 2 + lev) * 3 + row % 3) * 48 + p // 2

    for p in range(4):
        for lev in range(LEV):
            for i in range(6):
                at = (lev * 6 + i) * 24
                g[p, at:at + 24, :] = take(grid_s, pl.ds(cell_rows(p, lev, i), 24, stride=2))

    average = sum(jnp.sum(g[p], -1, keepdims=True) for p in range(4)) / (4 * D)
    variance = 0.0
    for p in range(4):
        centred = g[p] - average
        variance = variance + jnp.sum(centred * centred, -1, keepdims=True)
    inverse = lax.rsqrt(variance / (4 * D) + EPS)
    mean_d = sum(jnp.sum(d_in[p], -1, keepdims=True) for p in range(4)) / (4 * D)
    mean_dh = sum(jnp.sum(d_in[p] * ((g[p] - average) * inverse), -1, keepdims=True) for p in range(4)) / (4 * D)
    for p in range(4):
        hat = (g[p] - average) * inverse
        d_part = inverse * (d_in[p] - mean_d - hat * mean_dh)
        g[p] = hat
        for lev in range(LEV):
            for i in range(6):
                at = (lev * 6 + i) * 24
                put(d_str, pl.ds(cell_rows(p, lev, i), 24, stride=2), d_part[at:at + 24, :])

    for hb in range(4):
        d_ext[hb] = take(d_str, slice(hb * HALF, (hb + 1) * HALF)).astype(BF)
    gather_edges(2, d_ext, D)
    d_halo = send_halo(2, d_ext, d_side, d_corner, D)

    for n in range(2):
        cols = slice(n * 512, (n + 1) * 512)
        sums = nn(g[0].astype(BF), wm[0:D, cols])
        for p in range(1, 4):
            sums = sums + nn(g[p].astype(BF), wm[p * D:(p + 1) * D, cols])
        for s in range(4):
            merged[n * 4 + s] = sums[:, s * 128:(s + 1) * 128].astype(BF)
    def back_pair(i, _):
        rows = pl.ds(pl.multiple_of(i * 288, 288), 288)
        block = tmp[rows, :].astype(BF)
        d_win[rows, :] = block
        d_mix[rows, :] = nt(block, wp[...]).astype(BF)
        return 0

    def attend_back(w, q_b, d_b, stage):
        rows = pl.ds(pl.multiple_of(w * WIN, WIN), WIN)
        spread(q_b, rows, q, None)
        spread(d_b, rows, d_mix, None)
        keys, values = k[rows, :], v[rows, :]
        d_k, d_v = [], []
        for chunk in range(5):
            cols = slice(chunk * 256, min(chunk * 256 + 256, 1152))
            part = soft[w, :, cols]
            d_soft = nt(values[:, CHUNK_LANE[chunk]:CHUNK_LANE[chunk] + 256], d_b[cols, :])
            delta = jnp.sum(part * d_soft, 0, keepdims=True)
            d_s = (part * (d_soft - delta)).astype(BF)
            d_v.append(nn(part.astype(BF), d_b[cols, :]))
            d_k.append(nn(d_s, q_b[cols, :]))
            by_heads(stage, d_s, keys, chunk)
        for which, d in ((1, d_k), (2, d_v)):
            both = [d[0][:, 0:128] + d[1][:, 0:128], d[1][:, 128:256] + d[2][:, 0:128],
                    d[2][:, 128:256] + d[3][:, 0:128] + d[4][:, 0:128], d[3][:, 128:256] + d[4][:, 128:256]]
            for pair in range(4):
                d_qkv[rows, which * D + pair * 128:which * D + (pair + 1) * 128] = both[pair].astype(BF)
        for pair in range(4):
            d_qkv[rows, pair * 128:(pair + 1) * 128] = (joined(stage, pair) * 0.125).astype(BF)

    def attend_back_pair(i, _):
        attend_back(2 * i, block_q.at[0], block_d.at[0], staged.at[0])
        attend_back(2 * i + 1, block_q.at[1], block_d.at[1], staged.at[1])
        return 0

    orders = (("z", "y", "x"), ("y", "x", "z"), ("x", "z", "y"), ("z", "x", "y"))
    along = {"z": (on_z, z_at), "y": (on_y, y_at), "x": (on_x, x_at)}
    acc1 = d_in
    other = (lat + 1 - 2 * core, lon)
    half_at = pl.multiple_of(core * 256, 256)
    away_at = pl.multiple_of((1 - core) * 256, 256)
    factor = float(LEV * 192 * 384) ** -0.5
    outs = []

    def summed(m):
        (move1, at1), (_, at2), (_, at3) = [along[axis] for axis in orders[m]]

        def send(i, src, dst, to):
            copy = remote(src, dst, ar_send, ar_recv, m * 38 + i, to)
            started.append(copy)
            return copy

        core_send[m] = grads[m, pl.ds(away_at, 256), :].astype(BF)
        flying = [send(0, core_send.at[m], core_recv.at[m], other)]
        yield
        flying[0].wait_recv()
        acc1[m, 0:256, :] = grads[m, pl.ds(half_at, 256), :] + core_recv[m].astype(F32)
        send1[m] = acc1[m, 0:256, :].astype(BF)
        flying = []
        for by in range(1, 4):
            rows = pl.ds(pl.multiple_of(lax.rem(at1 + by, 4) * 64, 64), 64)
            flying.append(send(by, send1.at[m, rows], recv1.at[m, by - 1], move1(by)))
        yield
        for copy in flying:
            copy.wait_recv()
        own = acc1[m, pl.ds(pl.multiple_of(at1 * 64, 64), 64), :]
        for j in range(3):
            own = own + recv1[m, j].astype(F32)
        send2[m] = own.astype(BF)
        acc1[m, 0:64, :] = own
        rest = [(b2, b3) for b2 in range(4) for b3 in range(4) if (b2, b3) != (0, 0)]
        flying = []
        for i, (b2, b3) in enumerate(rest):
            rows = pl.ds(pl.multiple_of(lax.rem(at2 + b2, 4) * 16, 16), 16)
            cols = pl.ds(pl.multiple_of(lax.rem(at3 + b3, 4) * 128, 128), 128)
            flying.append(send(4 + i, send2.at[m, rows, cols], recv2.at[m, i], on_plane(orders[m], b2, b3)))
        yield
        for copy in flying:
            copy.wait_recv()
        row1 = core * 256
        row2 = row1 + at1 * 64
        row3 = row2 + at2 * 16
        rows1, rows2, rows3 = [pl.ds(pl.multiple_of(r, n), n) for r, n in ((row1, 256), (row2, 64), (row3, 16))]
        cols = pl.ds(pl.multiple_of(at3 * 128, 128), 128)
        own = acc1[m, pl.ds(pl.multiple_of(at2 * 16, 16), 16), cols]
        for j in range(15):
            own = own + recv2[m, j].astype(F32)
        total[m, rows3, cols] = (own * factor).astype(BF)
        piece = total.at[m, rows3, cols]
        flying = [send(19 + i, piece, piece, on_plane(orders[m], b2, b3)) for i, (b2, b3) in enumerate(rest)]
        yield
        for copy in flying:
            copy.wait_recv()
        flying = [send(33 + by, total.at[m, rows2], total.at[m, rows2], move1(by)) for by in range(1, 4)]
        yield
        for copy in flying:
            copy.wait_recv()
        flying = [send(37, total.at[m, rows1], total.at[m, rows1], other)]
        yield
        flying[0].wait_recv()
        outs.append(local(m, total.at[m], gw_out.at[:, pl.ds(m * D, D)]))
        yield

    for half in range(2):
        window_rows(half, 0, 2, d_ext, d_side, d_corner, tmp)
    back_pair(0, 0)
    attend_back_pair(0, 0)
    for copy in d_halo:
        copy.wait_recv()
    for by in range(1, 8):
        to = lax.rem(lon + by, 8)
        started.append(remote(merged.at[to], merged_in.at[lon], a2a_send, a2a_recv, 6 + by, (lat, to)))
    merged_out = started[-7:]
    merged_in[lon] = merged[lon]
    for half in range(2):
        window_rows(half, 2, 4, d_ext, d_side, d_corner, tmp)
    for half in range(2, 4):
        window_rows(half, 0, 4, d_ext, d_side, d_corner, tmp)
    lax.fori_loop(1, 4, back_pair, 0)
    grads[0] = nn(mixed_t[...], d_win[...])
    sums = [summed(0)]
    next(sums[0])
    for i in (1, 2, 3):
        attend_back_pair(i, 0)
        if i == 1:
            next(sums[0])

    for m in range(3):
        grads[m + 1] = nn(normed_t[...], d_qkv[:, m * D:(m + 1) * D])
        sums.append(summed(m + 1))
        next(sums[m + 1])

    def norm_back_band(band, _):
        rows = pl.ds(pl.multiple_of(band * 576, 576), 576)
        d_norm = nt(d_qkv[rows, :], wq[...])
        centred, inverse = stats(xw[rows, :])
        hat = centred * inverse
        tmp[rows, :] = inverse * (
            d_norm - jnp.mean(d_norm, -1, keepdims=True) - hat * jnp.mean(d_norm * hat, -1, keepdims=True)
        )
        return 0

    roll_halo = []
    for band in (1, 0):
        norm_back_band(band, 0)
        for half in (band * 2 + 1, band * 2):
            roll_halo += to_grid(half, 3, r_send, r_lat, r_diag, r_side, r_corner, grid_s)
        for step in sums:
            next(step)

    for copy in merged_out:
        copy.wait_recv()
    for s in range(8):
        merged_all[:, s * 24:(s + 1) * 24, :] = merged_in[s].astype(F32).reshape(12, 24, 128)
    dm_raw[...] = merged_all[...].astype(BF)
    outs.append(local(4, dm_raw, m_out))
    for step in sums:
        next(step)

    for copy in roll_halo:
        copy.wait_recv()
    for hb in range(4):
        at = slice(hb * HALF, (hb + 1) * HALF)
        own = r_lat[...].astype(F32) if hb == 0 else take(grid_s, at)
        put(d_str, at, take(d_str, at) + own + from_edges(hb, r_side, r_corner))
        for lev in range(LEV):
            for c in range(4):
                src = d_str.at[c, pl.ds(hb * HALF + lev * 144, 144)]
                to = gx_out.at[lev, pl.ds(hb * 144, 144), pl.ds(c * 128, 128)]
                outs.append(local(5 + hb * 8 + lev * 4 + c, src, to))
        for step in sums:
            next(step, None)
    for _ in range(8):
        for step in sums:
            next(step, None)

    for copy in started:
        copy.wait_send()
    for copy in outs:
        copy.wait()


def finish(m_in, gx_in, gw_in, m_out, gx_out, gq_out, gp_out, m_v, gx_v, gw_v, wide, in_sem, out_sem):
    ins, outs = [], []

    def start(sems, held, src, dst):
        copy = pltpu.make_async_copy(src, dst, sems.at[len(held)])
        copy.start()
        held.append(copy)

    quarters = [pl.ds(i * 128, 128) for i in range(4)]
    halves = [(lev, pl.ds(i * 288, 288)) for lev in range(LEV) for i in range(2)]
    for rows in quarters:
        start(in_sem, ins, gw_in.at[rows], gw_v.at[rows])
    for at in halves:
        start(in_sem, ins, gx_in.at[at], gx_v.at[at])
    start(in_sem, ins, m_in, m_v)
    for i, rows in enumerate(quarters):
        ins[i].wait()
        wide[rows, :] = gw_v[rows, :].astype(F32)
        start(out_sem, outs, wide.at[rows, pl.ds(D, 3 * D)], gq_out.at[rows])
        start(out_sem, outs, wide.at[rows, pl.ds(0, D)], gp_out.at[rows])
    for i, at in enumerate(halves):
        ins[4 + i].wait()
        start(out_sem, outs, gx_v.at[at], gx_out.at[at])
    ins[8].wait()
    start(out_sem, outs, m_v, m_out)
    for copy in outs:
        copy.wait()


def vmem(*shape, dtype=BF):
    return pltpu.VMEM(shape, dtype)


SCRATCH = [
    vmem(5, HALF, 640), vmem(SIDE, 640), vmem(PACK, 640), vmem(12, 48, dtype=jnp.int32), vmem(D, 3 * D), vmem(D, D), vmem(4 * D, D2),
    vmem(12, 192, 128), vmem(8, CELLS, 128), vmem(CELLS, D2), vmem(HALF, HALF), vmem(HALF + PACK, HALF), vmem(4, 80, SIDE),
    vmem(PACK, HALF), vmem(3, HALF, SIDE), vmem(HALF, PACK), vmem(4 * EDGE, 640, dtype=F32), vmem(4, 4 * EDGE, 640),
    vmem(TOK, D, dtype=F32), vmem(TOK, 128, dtype=F32), vmem(TOK, D), vmem(TOK, D), vmem(TOK, D), vmem(TOK, D),
    vmem(2, 1152, 256), vmem(2, 1152, 256), vmem(2, 1152, 128, dtype=F32), vmem(8, WIN, 1152, dtype=F32), vmem(D, TOK), vmem(D, TOK), vmem(TOK, D), vmem(TOK, D, dtype=F32),
    vmem(HALF, D), vmem(PACK, D), vmem(HALF, D), vmem(SIDE, D), vmem(PACK, D),
    vmem(4, TOK, 128, dtype=F32), vmem(4, CELLS, D, dtype=F32), vmem(4, CELLS, D, dtype=F32), vmem(4, TOK, 128, dtype=F32),
    vmem(5, HALF, D), vmem(SIDE, D), vmem(PACK, D), vmem(TOK, D), vmem(TOK, D), vmem(TOK, 3 * D), vmem(8, CELLS, 128), vmem(8, CELLS, 128), vmem(12, 192, 128, dtype=F32),
    vmem(HALF, D), vmem(PACK, D), vmem(HALF, D), vmem(SIDE, D), vmem(PACK, D),
    vmem(4, D, D, dtype=F32), vmem(4, 256, D), vmem(4, 256, D), vmem(4, 256, D),
    vmem(4, 3, 64, D), vmem(4, 64, D), vmem(4, 15, 16, 128), vmem(4, D, D),
    pltpu.SemaphoreType.DMA((38,)), pltpu.SemaphoreType.DMA((12,)), pltpu.SemaphoreType.DMA((12,)),
    pltpu.SemaphoreType.DMA((14,)), pltpu.SemaphoreType.DMA((14,)),
    pltpu.SemaphoreType.DMA((152,)), pltpu.SemaphoreType.DMA((152,)),
]


def per_device(tokens, region, w_qkv, w_proj, w_merge, d_merged):
    levels, lat_rows, lon_cols, feature = tokens.shape
    consts = [jnp.asarray(a, BF) for a in one_hots()]
    anywhere = pl.BlockSpec(memory_space=pl.ANY)
    m_out, gx_out, gw_out = pl.pallas_call(
        kernel,
        out_shape=(
            jax.ShapeDtypeStruct((12, 192, 128), BF),
            jax.ShapeDtypeStruct((levels, 576, feature), F32),
            jax.ShapeDtypeStruct((D, 4 * D), BF),
        ),
        in_specs=[anywhere] * 12,
        out_specs=(anywhere,) * 3,
        scratch_shapes=SCRATCH,
        compiler_params=pltpu.CompilerParams(
            collective_id=0, has_side_effects=True, vmem_limit_bytes=64 * 1024 * 1024
        ),
    )(
        tokens.reshape(levels, 576, feature), region, w_qkv, w_proj, w_merge,
        d_merged.reshape(12, 192, 128), *consts,
    )
    merged, grad_x, grad_qkv, grad_proj = pl.pallas_call(
        finish,
        out_shape=(
            jax.ShapeDtypeStruct((12, 192, 128), BF),
            jax.ShapeDtypeStruct((levels, 576, feature), F32),
            jax.ShapeDtypeStruct((D, 3 * D), F32),
            jax.ShapeDtypeStruct((D, D), F32),
        ),
        in_specs=[anywhere] * 3,
        out_specs=(anywhere,) * 4,
        scratch_shapes=[
            vmem(12, 192, 128), vmem(LEV, 576, D, dtype=F32), vmem(D, 4 * D), vmem(D, 4 * D, dtype=F32),
            pltpu.SemaphoreType.DMA((9,)), pltpu.SemaphoreType.DMA((13,)),
        ],
        compiler_params=pltpu.CompilerParams(vmem_limit_bytes=32 * 1024 * 1024),
    )(m_out, gx_out, gw_out)
    return (
        merged.reshape(levels, 6, 192, 128), grad_x.reshape(levels, lat_rows, lon_cols, feature), grad_qkv, grad_proj
    )


def solution(mesh):
    in_specs = (
        P(None, "lat", "lon", None),
        P("lat", "lon"),
        P(),
        P(),
        P(),
        P(None, "lat", None, "lon"),
    )
    out_specs = (P(None, "lat", None, "lon"), P(None, "lat", "lon", None), P(), P())
    return jax.shard_map(
        per_device, mesh=mesh, in_specs=in_specs, out_specs=out_specs, check_vma=False
    )
```

```python
import functools

import jax
import jax.numpy as jnp
import numpy as np
from jax import lax
from jax.experimental import pallas as pl
from jax.experimental.pallas import tpu as pltpu
from jax.sharding import PartitionSpec as P

D = 512
D2 = 1024
HEADS = 8
LEV = 2
WIN_LAT = 6
WIN_LON = 12
EPS = 1e-05

HALF = 288
EDGE = 36
PACK = 48
SIDE = 112
WIN = 144
TOK = 1152
CELLS = 288
BF = jnp.bfloat16
F32 = jnp.float32
MESH = pl.DeviceIdType.MESH


CHUNK_LANE = (0, 0, 128, 256, 256)
SEGMENTS = []
for _head in range(HEADS):
    _at = _head * WIN
    while _at < (_head + 1) * WIN:
        _end = min((_at // 256 + 1) * 256, (_head + 1) * WIN)
        SEGMENTS.append((_head, _at, _end))
        _at = _end


def one_hots():
    to_win = np.zeros((HALF, HALF), np.float32)
    from_win = np.zeros((HALF + PACK, HALF), np.float32)
    edge_in = np.zeros((4, 80, SIDE), np.float32)
    pack = np.zeros((PACK, HALF), np.float32)
    unpack = np.zeros((3, HALF, SIDE), np.float32)
    for lr in range(6):
        for wc in range(4):
            for cw in range(WIN_LON):
                u = wc * 72 + lr * WIN_LON + cw
                col = WIN_LON * wc + WIN_LON // 2 + cw
                if col < 48:
                    to_win[u, lr * 48 + col] = from_win[lr * 48 + col, u] = 1.0
                else:
                    at = lr * 6 + col - 48
                    from_win[HALF + at, u] = 1.0
                    for half in range(4):
                        edge_in[half, u - 216, half * EDGE + at if half < 3 else 12 + at] = 1.0
        for c in range(6):
            pack[lr * 6 + c, lr * 48 + c] = 1.0
            for half in range(3):
                unpack[half, lr * 48 + c, half * EDGE + lr * 6 + c] = 1.0
    return to_win, from_win, edge_in, pack, unpack, pack.T


def nn(a, b):
    return lax.dot_general(a, b, (((1,), (0,)), ((), ())), preferred_element_type=F32)


def nt(a, b):
    return lax.dot_general(a, b, (((1,), (1,)), ((), ())), preferred_element_type=F32)


def tn(a, b):
    return lax.dot_general(a, b, (((0,), (0,)), ((), ())), preferred_element_type=F32)


def take(ref, rows):
    return jnp.concatenate([ref[c, rows, :] for c in range(4)], 1)


def put(ref, rows, value):
    for c in range(4):
        ref[c, rows, :] = value[:, c * 128:(c + 1) * 128]


def stats(x):
    average = jnp.mean(x, -1, keepdims=True)
    centred = x - average
    variance = jnp.mean(centred * centred, -1, keepdims=True)
    return centred, lax.rsqrt(variance + EPS)


def kernel(
    tokens, region, w_qkv_h, w_proj_h, w_merge_h, d_merged, to_win_h, from_win_h, edge_in_h, pack_h, unpack_h, corner_h,
    m_out, gx_out, gw_out,
    ext, side, corner, regions, wq, wp, wm, dm_raw, dm_send, dm_recv, to_win, from_win, edge_in, pack, unpack, uncorner, loose, packed,
    xw, keyw, normed, q, k, v, block_q, block_d, staged, soft, mixed_t, normed_t, mixed, tmp, b_send, b_diag, b_lat, b_side, b_corner,
    grid_s, g, d_in, d_str, d_ext, d_side, d_corner, d_win, d_mix, d_qkv, merged, merged_in, merged_all,
    r_send, r_diag, r_lat, r_side, r_corner,
    grads, core_send, core_recv, send1, recv1, send2, recv2, total,
    local_sem, halo_send, halo_recv, a2a_send, a2a_recv, ar_send, ar_recv,
):
    lat = lax.axis_index("lat")
    lon = lax.axis_index("lon")
    core = lax.rem(lat, 2)
    z_at = lax.rem(lax.div(lat, 2), 4)
    y_lo = lax.div(lat, 8)
    x_at = lax.div(lon, 2)
    y_at = lax.rem(lon, 2) * 2 + y_lo

    south = lax.rem(lat + 1, 16)
    north = lax.rem(lat + 15, 16)
    east = lax.rem(lon + 1, 8)
    west = lax.rem(lon + 7, 8)

    places = {"x": x_at, "y": y_at, "z": z_at}

    def moved_by(steps):
        x, y, z = [lax.rem(places[axis] + steps[axis], 4) if steps.get(axis) else places[axis] for axis in "xyz"]
        return (lax.rem(y, 2) * 8 + z * 2 + core, x * 2 + lax.div(y, 2))

    def on_z(by):
        return moved_by({"z": by})

    def on_y(by):
        return moved_by({"y": by})

    def on_x(by):
        return moved_by({"x": by})

    def on_plane(order, b2, b3):
        return moved_by({order[1]: b2, order[2]: b3})

    def local(i, src, dst):
        copy = pltpu.make_async_copy(src, dst, local_sem.at[i])
        copy.start()
        return copy

    def remote(src, dst, sends, recvs, i, to):
        copy = pltpu.make_async_remote_copy(
            src_ref=src, dst_ref=dst, send_sem=sends.at[i], recv_sem=recvs.at[i], device_id=to, device_id_type=MESH
        )
        copy.start()
        return copy

    started = []

    loads = []
    for hb in range(4):
        for lev in range(LEV):
            rows, place = pl.ds(hb * 144, 144), pl.ds(lev * 144, 144)
            loads.append(local(len(loads), tokens.at[lev, rows], ext.at[hb, place, pl.ds(0, D)]))
    for src, dst in ((region, regions), (pack_h, pack), (to_win_h, to_win), (d_merged, dm_raw), (w_qkv_h, wq), (w_merge_h, wm),
                     (w_proj_h, wp), (from_win_h, from_win), (unpack_h, unpack), (edge_in_h, edge_in), (corner_h, uncorner)):
        loads.append(local(len(loads), src, dst))
    grid_loads, (l_reg, l_pack, l_to, l_dm, l_wq, l_wm, l_wp, l_from, l_un, l_edge, l_corner) = loads[:8], loads[8:]

    barrier = pltpu.get_barrier_semaphore()
    peers = [(south, lon), (north, lon), (south, east), (north, west)]
    peers += [(lat, lax.rem(lon + by, 8)) for by in range(1, 8)]
    peers += [on_z(by) for by in (1, 2, 3)] + [on_y(by) for by in (1, 3)]
    for first, second in ("xy", "yz", "xz"):
        for b2 in range(1, 4):
            for b3 in range(1, 4):
                if (first, second, b3) != ("x", "y", 2):
                    peers.append(moved_by({first: b2, second: b3}))
    for peer in peers:
        pl.semaphore_signal(barrier, inc=1, device_id=peer, device_id_type=MESH)

    for copy in grid_loads:
        copy.wait()
    l_reg.wait()
    diagonal = lax.broadcasted_iota(jnp.int32, (48, 48), 0) == lax.broadcasted_iota(jnp.int32, (48, 48), 1)
    for row in range(12):
        column = jnp.sum(jnp.where(diagonal, regions[row:row + 1, :].astype(F32), 0.0), 1, keepdims=True)
        if row < WIN_LAT // 2:
            column = column + jnp.where(lat == 0, 4.0, 0.0)
        for lev in range(LEV):
            at = lev * 144 + row % 3 * 48
            ext[row // 3, at:at + 48, D:] = jnp.broadcast_to(column, (48, 128)).astype(BF)
    l_pack.wait()
    def gather_edges(number, full, width):
        for i, hb in enumerate((1, 2, 3, 0)):
            loose[i * EDGE:(i + 1) * EDGE, 0:width] = nn(pack[...], full[hb])[0:EDGE]
        packed[number, :, 0:width] = loose[:, 0:width].astype(BF)

    def send_halo(number, full, to_side, to_corner, width):
        lanes = pl.ds(0, width)
        out = [
            remote(full.at[0], full.at[4], halo_send, halo_recv, number * 3, (north, lon)),
            remote(packed.at[number, pl.ds(0, SIDE), lanes], to_side, halo_send, halo_recv, number * 3 + 1, (lat, west)),
            remote(packed.at[number, pl.ds(96, PACK), lanes], to_corner, halo_send, halo_recv, number * 3 + 2, (north, west)),
        ]
        started.extend(out)
        return out

    gather_edges(0, ext, 640)
    pl.semaphore_wait(barrier, len(peers))
    halo = send_halo(0, ext, side, corner, 640)

    l_dm.wait()
    for s in range(8):
        part = dm_raw[:, s * 24:(s + 1) * 24, :].astype(F32)
        dm_send[s] = part.reshape(CELLS, 128).astype(BF)
    def window_rows(half, first, last, full, to_side, to_corner, wide):
        moved = nn(to_win[first * 72:last * 72, :], full[half + 1])
        for wc in range(first, last):
            at = ((half // 2) * 4 + wc) * WIN + (half % 2) * 72
            part = moved[(wc - first) * 72:(wc - first + 1) * 72, :]
            if wc == 3:
                if half == 3:
                    part = part + nn(edge_in[3, :, 0:PACK], to_corner[...])[0:72]
                else:
                    part = part + nn(edge_in[half], to_side[...])[0:72]
            wide[at:at + 72, :] = part[:, :D]
            if part.shape[1] > D:
                keyw[at:at + 72, :] = part[:, D:]

    def norm_window(w, _):
        rows = pl.ds(pl.multiple_of(w * WIN, WIN), WIN)
        centred, inverse = stats(xw[rows, :])
        normed[rows, :] = (centred * inverse).astype(BF)
        return 0

    def project_pair(i, _):
        rows = pl.ds(pl.multiple_of(i * 288, 288), 288)
        block = normed[rows, :]
        q[rows, :] = (nn(block, wq[:, 0:D]).astype(BF) * 0.125).astype(BF)
        k[rows, :] = nn(block, wq[:, D:2 * D]).astype(BF)
        v[rows, :] = nn(block, wq[:, 2 * D:3 * D]).astype(BF)
        return 0

    lane = lax.broadcasted_iota(jnp.int32, (WIN, 128), 1)
    low = lane < 64

    def spread(ref, rows, src, filler):
        blank = jnp.zeros((WIN, 128), BF)
        for head, first, last in SEGMENTS:
            chunk, at = first // 256, pl.ds(first, last - first)
            part = slice(first - head * WIN, last - head * WIN)
            own = src[rows, (head // 2) * 128:(head // 2 + 1) * 128]
            own = jnp.where(low if head % 2 == 0 else ~low, own, blank)
            block = head // 2 - CHUNK_LANE[chunk] // 128
            fill = blank if filler is None else filler
            if chunk == 0:
                ref[at, 0:128] = own[part]
                ref[at, 128:256] = fill[part]
            else:
                ref[at, 0:128] = (jnp.where(low, fill, own) if block == 0 else fill)[part]
                ref[at, 128:256] = (own if block == 1 else blank)[part]

    def by_heads(stage, left, right, chunk):
        out = tn(left, right[:, CHUNK_LANE[chunk]:CHUNK_LANE[chunk] + 256])
        for head, first, last in SEGMENTS:
            if first // 256 == chunk:
                block = head // 2 - CHUNK_LANE[chunk] // 128
                rows = slice(first - chunk * 256, last - chunk * 256)
                stage[first:last, :] = out[rows, block * 128:(block + 1) * 128]

    def joined(stage, pair):
        even, odd = 2 * pair * WIN, (2 * pair + 1) * WIN
        return jnp.where(low, stage[even:even + WIN, :], stage[odd:odd + WIN, :])

    def attend(w, q_b, stage):
        rows = pl.ds(pl.multiple_of(w * WIN, WIN), WIN)
        same = keyw[rows, :] == lane.astype(F32)
        differ = jnp.where(same | ~low, 0.0, 1.0).astype(BF)
        forbid = jnp.where(same, -1e30, 0.0).astype(BF)
        spread(q_b, rows, q, differ)
        k_b = [k[rows, i * 128:(i + 1) * 128] for i in range(4)]
        k_x = [jnp.concatenate([k_b[0], jnp.where(low, forbid, k_b[1])], 1)]
        k_x += [jnp.concatenate([jnp.where(low, forbid, k_b[i]), k_b[i + 1]], 1) for i in range(3)]
        values = v[rows, :]
        for chunk in range(5):
            cols = slice(chunk * 256, min(chunk * 256 + 256, 1152))
            raw = jnp.exp(nt(k_x[min(chunk, 3)], q_b[cols, :]))
            total_w = jnp.sum(raw, 0, keepdims=True)
            shrink = jnp.where(total_w > 1.0, 2.0 ** -32, 1.0)
            part = (raw * shrink) * (1.0 / (total_w * shrink))
            soft[w, :, cols] = part
            by_heads(stage, part.astype(BF), values, chunk)
        for pair in range(4):
            mixed[rows, pair * 128:(pair + 1) * 128] = joined(stage, pair).astype(BF)

    def attend_pair(i, _):
        attend(2 * i, block_q.at[0], staged.at[0])
        attend(2 * i + 1, block_q.at[1], staged.at[1])
        return 0

    l_to.wait()
    for half in range(2):
        window_rows(half, 0, 2, ext, side, corner, xw)
    lax.fori_loop(0, 2, norm_window, 0)
    l_wq.wait()
    project_pair(0, 0)
    mine = pl.ds(pl.multiple_of(lon * 128, 128), 128)
    a2a_in = []

    def send_cotangents(steps):
        for by in steps:
            to = lax.rem(lon + by, 8)
            copy = remote(dm_send.at[to], dm_recv.at[:, mine], a2a_send, a2a_recv, by - 1, (lat, to))
            a2a_in.append(copy)
            started.append(copy)

    send_cotangents((2, 4, 6))
    dm_recv[:, mine] = dm_send[lon]
    attend_pair(0, 0)

    for copy in halo:
        copy.wait_recv()
    send_cotangents((1, 3, 5, 7))
    l_edge.wait()
    for half in range(2):
        window_rows(half, 2, 4, ext, side, corner, xw)
    for half in range(2, 4):
        window_rows(half, 0, 4, ext, side, corner, xw)
    lax.fori_loop(2, 8, norm_window, 0)
    lax.fori_loop(1, 4, project_pair, 0)
    lax.fori_loop(2, 4, attend_pair, 0)

    l_wp.wait()
    l_from.wait()
    l_un.wait()
    l_corner.wait()

    def to_grid(half, number, lat_send, lat_recv, diag_send, to_side, to_corner, keep):
        first = (half // 2) * 4
        block = jnp.concatenate([tmp[(first + wc) * WIN + (half % 2) * 72:(first + wc) * WIN + (half % 2) * 72 + 72, :] for wc in range(4)], 0)
        moved = nn(from_win[...], block.astype(BF))
        out = []
        if half == 3:
            loose[3 * EDGE:, 0:D] = jnp.zeros((EDGE, D), F32)
            diag_send[...] = moved[HALF:, :].astype(BF)
            lat_send[...] = moved[:HALF, :].astype(BF)
            out.append((lat_send, lat_recv, number * 3, (south, lon)))
            out.append((diag_send, to_corner, number * 3 + 2, (south, east)))
        else:
            put(keep, slice((half + 1) * HALF, (half + 2) * HALF), moved[:HALF, :])
            loose[half * EDGE:(half + 1) * EDGE, 0:D] = moved[HALF:HALF + EDGE, :]
        if half == 0:
            packed[number, :, 0:D] = loose[:, 0:D].astype(BF)
            sides = packed.at[number, pl.ds(0, SIDE), pl.ds(0, D)]
            out.append((sides, to_side, number * 3 + 1, (lat, east)))
        return out

    def launch(parts):
        out = [remote(src, dst, halo_send, halo_recv, i, to) for src, dst, i, to in parts]
        started.extend(out)
        return out

    def from_edges(hb, to_side, to_corner):
        return nn(uncorner[...], to_corner[...]) if hb == 0 else nn(unpack[hb - 1], to_side[...])

    branch_halo = []
    for band in (1, 0):
        if band == 0:
            attend_pair(1, 0)
        rows = slice(band * 576, (band + 1) * 576)
        tmp[rows, :] = nn(mixed[rows, :], wp[...])
        for half in (band * 2 + 1, band * 2):
            branch_halo += launch(to_grid(half, 1, b_send, b_lat, b_diag, b_side, b_corner, grid_s))

    l_wm.wait()
    for copy in a2a_in:
        copy.wait_recv()

    def d_in_part(p, _):
        d_in[p] = nt(dm_recv[...], wm[pl.ds(pl.multiple_of(p * D, D), D), :])
        return 0

    lax.fori_loop(0, 4, d_in_part, 0)
    for i in range(9):
        rows = slice(i * 128, (i + 1) * 128)
        normed_t[:, rows] = normed[rows, :].T
        mixed_t[:, rows] = mixed[rows, :].T

    for copy in branch_halo:
        copy.wait_recv()
    for hb in range(4):
        at = slice(hb * HALF, (hb + 1) * HALF)
        own = b_lat[...].astype(F32) if hb == 0 else take(grid_s, at)
        full = own + from_edges(hb, b_side, b_corner)
        put(grid_s, at, (ext[hb, 0:HALF, 0:D].astype(F32) + full).astype(BF).astype(F32))

    def cell_rows(p, lev, i):
        row = 2 * i + p % 2
        return ((row // 3 * 2 + lev) * 3 + row % 3) * 48 + p // 2

    for p in range(4):
        for lev in range(LEV):
            for i in range(6):
                at = (lev * 6 + i) * 24
                g[p, at:at + 24, :] = take(grid_s, pl.ds(cell_rows(p, lev, i), 24, stride=2))

    average = sum(jnp.sum(g[p], -1, keepdims=True) for p in range(4)) / (4 * D)
    variance = 0.0
    for p in range(4):
        centred = g[p] - average
        variance = variance + jnp.sum(centred * centred, -1, keepdims=True)
    inverse = lax.rsqrt(variance / (4 * D) + EPS)
    mean_d = sum(jnp.sum(d_in[p], -1, keepdims=True) for p in range(4)) / (4 * D)
    mean_dh = sum(jnp.sum(d_in[p] * ((g[p] - average) * inverse), -1, keepdims=True) for p in range(4)) / (4 * D)
    for p in range(4):
        hat = (g[p] - average) * inverse
        d_part = inverse * (d_in[p] - mean_d - hat * mean_dh)
        g[p] = hat
        for lev in range(LEV):
            for i in range(6):
                at = (lev * 6 + i) * 24
                put(d_str, pl.ds(cell_rows(p, lev, i), 24, stride=2), d_part[at:at + 24, :])

    for hb in range(4):
        d_ext[hb] = take(d_str, slice(hb * HALF, (hb + 1) * HALF)).astype(BF)
    gather_edges(2, d_ext, D)
    d_halo = send_halo(2, d_ext, d_side, d_corner, D)

    for n in range(2):
        cols = slice(n * 512, (n + 1) * 512)
        sums = nn(g[0].astype(BF), wm[0:D, cols])
        for p in range(1, 4):
            sums = sums + nn(g[p].astype(BF), wm[p * D:(p + 1) * D, cols])
        for s in range(4):
            merged[n * 4 + s] = sums[:, s * 128:(s + 1) * 128].astype(BF)
    def back_pair(i, _):
        rows = pl.ds(pl.multiple_of(i * 288, 288), 288)
        block = tmp[rows, :].astype(BF)
        d_win[rows, :] = block
        d_mix[rows, :] = nt(block, wp[...]).astype(BF)
        return 0

    def attend_back(w, q_b, d_b, stage):
        rows = pl.ds(pl.multiple_of(w * WIN, WIN), WIN)
        spread(q_b, rows, q, None)
        spread(d_b, rows, d_mix, None)
        keys, values = k[rows, :], v[rows, :]
        d_k, d_v = [], []
        for chunk in range(5):
            cols = slice(chunk * 256, min(chunk * 256 + 256, 1152))
            part = soft[w, :, cols]
            d_soft = nt(values[:, CHUNK_LANE[chunk]:CHUNK_LANE[chunk] + 256], d_b[cols, :])
            delta = jnp.sum(part * d_soft, 0, keepdims=True)
            d_s = (part * (d_soft - delta)).astype(BF)
            d_v.append(nn(part.astype(BF), d_b[cols, :]))
            d_k.append(nn(d_s, q_b[cols, :]))
            by_heads(stage, d_s, keys, chunk)
        for which, d in ((1, d_k), (2, d_v)):
            both = [d[0][:, 0:128] + d[1][:, 0:128], d[1][:, 128:256] + d[2][:, 0:128],
                    d[2][:, 128:256] + d[3][:, 0:128] + d[4][:, 0:128], d[3][:, 128:256] + d[4][:, 128:256]]
            for pair in range(4):
                d_qkv[rows, which * D + pair * 128:which * D + (pair + 1) * 128] = both[pair].astype(BF)
        for pair in range(4):
            d_qkv[rows, pair * 128:(pair + 1) * 128] = (joined(stage, pair) * 0.125).astype(BF)

    def attend_back_pair(i, _):
        attend_back(2 * i, block_q.at[0], block_d.at[0], staged.at[0])
        attend_back(2 * i + 1, block_q.at[1], block_d.at[1], staged.at[1])
        return 0

    orders = (("z", "y", "x"), ("y", "x", "z"), ("x", "z", "y"), ("z", "x", "y"))
    along = {"z": (on_z, z_at), "y": (on_y, y_at), "x": (on_x, x_at)}
    acc1 = d_in
    other = (lat + 1 - 2 * core, lon)
    half_at = pl.multiple_of(core * 256, 256)
    away_at = pl.multiple_of((1 - core) * 256, 256)
    factor = float(LEV * 192 * 384) ** -0.5
    outs = []

    def summed(m):
        (move1, at1), (_, at2), (_, at3) = [along[axis] for axis in orders[m]]

        def send(i, src, dst, to):
            copy = remote(src, dst, ar_send, ar_recv, m * 38 + i, to)
            started.append(copy)
            return copy

        core_send[m] = grads[m, pl.ds(away_at, 256), :].astype(BF)
        flying = [send(0, core_send.at[m], core_recv.at[m], other)]
        yield
        flying[0].wait_recv()
        acc1[m, 0:256, :] = grads[m, pl.ds(half_at, 256), :] + core_recv[m].astype(F32)
        send1[m] = acc1[m, 0:256, :].astype(BF)
        flying = []
        for by in range(1, 4):
            rows = pl.ds(pl.multiple_of(lax.rem(at1 + by, 4) * 64, 64), 64)
            flying.append(send(by, send1.at[m, rows], recv1.at[m, by - 1], move1(by)))
        yield
        for copy in flying:
            copy.wait_recv()
        own = acc1[m, pl.ds(pl.multiple_of(at1 * 64, 64), 64), :]
        for j in range(3):
            own = own + recv1[m, j].astype(F32)
        send2[m] = own.astype(BF)
        acc1[m, 0:64, :] = own
        rest = [(b2, b3) for b2 in range(4) for b3 in range(4) if (b2, b3) != (0, 0)]
        flying = []
        for i, (b2, b3) in enumerate(rest):
            rows = pl.ds(pl.multiple_of(lax.rem(at2 + b2, 4) * 16, 16), 16)
            cols = pl.ds(pl.multiple_of(lax.rem(at3 + b3, 4) * 128, 128), 128)
            flying.append(send(4 + i, send2.at[m, rows, cols], recv2.at[m, i], on_plane(orders[m], b2, b3)))
        yield
        for copy in flying:
            copy.wait_recv()
        row1 = core * 256
        row2 = row1 + at1 * 64
        row3 = row2 + at2 * 16
        rows1, rows2, rows3 = [pl.ds(pl.multiple_of(r, n), n) for r, n in ((row1, 256), (row2, 64), (row3, 16))]
        cols = pl.ds(pl.multiple_of(at3 * 128, 128), 128)
        own = acc1[m, pl.ds(pl.multiple_of(at2 * 16, 16), 16), cols]
        for j in range(15):
            own = own + recv2[m, j].astype(F32)
        total[m, rows3, cols] = (own * factor).astype(BF)
        piece = total.at[m, rows3, cols]
        flying = [send(19 + i, piece, piece, on_plane(orders[m], b2, b3)) for i, (b2, b3) in enumerate(rest)]
        yield
        for copy in flying:
            copy.wait_recv()
        flying = [send(33 + by, total.at[m, rows2], total.at[m, rows2], move1(by)) for by in range(1, 4)]
        yield
        for copy in flying:
            copy.wait_recv()
        flying = [send(37, total.at[m, rows1], total.at[m, rows1], other)]
        yield
        flying[0].wait_recv()
        outs.append(local(m, total.at[m], gw_out.at[:, pl.ds(m * D, D)]))
        yield

    for half in range(2):
        window_rows(half, 0, 2, d_ext, d_side, d_corner, tmp)
    back_pair(0, 0)
    attend_back_pair(0, 0)
    for copy in d_halo:
        copy.wait_recv()
    for by in range(1, 8):
        to = lax.rem(lon + by, 8)
        started.append(remote(merged.at[to], merged_in.at[lon], a2a_send, a2a_recv, 6 + by, (lat, to)))
    merged_out = started[-7:]
    merged_in[lon] = merged[lon]
    for half in range(2):
        window_rows(half, 2, 4, d_ext, d_side, d_corner, tmp)
    for half in range(2, 4):
        window_rows(half, 0, 4, d_ext, d_side, d_corner, tmp)
    lax.fori_loop(1, 4, back_pair, 0)
    grads[0] = nn(mixed_t[...], d_win[...])
    sums = [summed(0)]
    next(sums[0])
    for i in (1, 2, 3):
        attend_back_pair(i, 0)
        if i == 1:
            next(sums[0])

    for m in range(3):
        grads[m + 1] = nn(normed_t[...], d_qkv[:, m * D:(m + 1) * D])
        sums.append(summed(m + 1))
        next(sums[m + 1])

    def norm_back_band(band, _):
        rows = pl.ds(pl.multiple_of(band * 576, 576), 576)
        d_norm = nt(d_qkv[rows, :], wq[...])
        centred, inverse = stats(xw[rows, :])
        hat = centred * inverse
        tmp[rows, :] = inverse * (
            d_norm - jnp.mean(d_norm, -1, keepdims=True) - hat * jnp.mean(d_norm * hat, -1, keepdims=True)
        )
        return 0

    roll_parts = []
    for band in (1, 0):
        norm_back_band(band, 0)
        if band == 1:
            for step in sums:
                next(step)
        for half in (band * 2 + 1, band * 2):
            roll_parts += to_grid(half, 3, r_send, r_lat, r_diag, r_side, r_corner, grid_s)
    for step in sums:
        next(step)
    roll_halo = launch(roll_parts)

    for copy in merged_out:
        copy.wait_recv()
    for s in range(8):
        merged_all[:, s * 24:(s + 1) * 24, :] = merged_in[s].astype(F32).reshape(12, 24, 128)
    dm_raw[...] = merged_all[...].astype(BF)
    outs.append(local(4, dm_raw, m_out))
    for _ in range(2):
        for step in sums:
            next(step)

    for copy in roll_halo:
        copy.wait_recv()
    for hb in range(4):
        at = slice(hb * HALF, (hb + 1) * HALF)
        own = r_lat[...].astype(F32) if hb == 0 else take(grid_s, at)
        put(d_str, at, take(d_str, at) + own + from_edges(hb, r_side, r_corner))
        for lev in range(LEV):
            for c in range(4):
                src = d_str.at[c, pl.ds(hb * HALF + lev * 144, 144)]
                to = gx_out.at[lev, pl.ds(hb * 144, 144), pl.ds(c * 128, 128)]
                outs.append(local(5 + hb * 8 + lev * 4 + c, src, to))
    for _ in range(8):
        for step in sums:
            next(step, None)

    for copy in started:
        copy.wait_send()
    for copy in outs:
        copy.wait()


def finish(m_in, gx_in, gw_in, m_out, gx_out, gq_out, gp_out, m_v, gx_v, gw_v, wide, in_sem, out_sem):
    ins, outs = [], []

    def start(sems, held, src, dst):
        copy = pltpu.make_async_copy(src, dst, sems.at[len(held)])
        copy.start()
        held.append(copy)

    quarters = [pl.ds(i * 128, 128) for i in range(4)]
    halves = [(lev, pl.ds(i * 288, 288)) for lev in range(LEV) for i in range(2)]
    for rows in quarters:
        start(in_sem, ins, gw_in.at[rows], gw_v.at[rows])
    for at in halves:
        start(in_sem, ins, gx_in.at[at], gx_v.at[at])
    start(in_sem, ins, m_in, m_v)
    for i, rows in enumerate(quarters):
        ins[i].wait()
        wide[rows, :] = gw_v[rows, :].astype(F32)
        start(out_sem, outs, wide.at[rows, pl.ds(D, 3 * D)], gq_out.at[rows])
        start(out_sem, outs, wide.at[rows, pl.ds(0, D)], gp_out.at[rows])
    for i, at in enumerate(halves):
        ins[4 + i].wait()
        start(out_sem, outs, gx_v.at[at], gx_out.at[at])
    ins[8].wait()
    start(out_sem, outs, m_v, m_out)
    for copy in outs:
        copy.wait()


def vmem(*shape, dtype=BF):
    return pltpu.VMEM(shape, dtype)


SCRATCH = [
    vmem(5, HALF, 640), vmem(SIDE, 640), vmem(PACK, 640), vmem(12, 48, dtype=jnp.int32), vmem(D, 3 * D), vmem(D, D), vmem(4 * D, D2),
    vmem(12, 192, 128), vmem(8, CELLS, 128), vmem(CELLS, D2), vmem(HALF, HALF), vmem(HALF + PACK, HALF), vmem(4, 80, SIDE),
    vmem(PACK, HALF), vmem(3, HALF, SIDE), vmem(HALF, PACK), vmem(4 * EDGE, 640, dtype=F32), vmem(4, 4 * EDGE, 640),
    vmem(TOK, D, dtype=F32), vmem(TOK, 128, dtype=F32), vmem(TOK, D), vmem(TOK, D), vmem(TOK, D), vmem(TOK, D),
    vmem(2, 1152, 256), vmem(2, 1152, 256), vmem(2, 1152, 128, dtype=F32), vmem(8, WIN, 1152, dtype=F32), vmem(D, TOK), vmem(D, TOK), vmem(TOK, D), vmem(TOK, D, dtype=F32),
    vmem(HALF, D), vmem(PACK, D), vmem(HALF, D), vmem(SIDE, D), vmem(PACK, D),
    vmem(4, TOK, 128, dtype=F32), vmem(4, CELLS, D, dtype=F32), vmem(4, CELLS, D, dtype=F32), vmem(4, TOK, 128, dtype=F32),
    vmem(5, HALF, D), vmem(SIDE, D), vmem(PACK, D), vmem(TOK, D), vmem(TOK, D), vmem(TOK, 3 * D), vmem(8, CELLS, 128), vmem(8, CELLS, 128), vmem(12, 192, 128, dtype=F32),
    vmem(HALF, D), vmem(PACK, D), vmem(HALF, D), vmem(SIDE, D), vmem(PACK, D),
    vmem(4, D, D, dtype=F32), vmem(4, 256, D), vmem(4, 256, D), vmem(4, 256, D),
    vmem(4, 3, 64, D), vmem(4, 64, D), vmem(4, 15, 16, 128), vmem(4, D, D),
    pltpu.SemaphoreType.DMA((38,)), pltpu.SemaphoreType.DMA((12,)), pltpu.SemaphoreType.DMA((12,)),
    pltpu.SemaphoreType.DMA((14,)), pltpu.SemaphoreType.DMA((14,)),
    pltpu.SemaphoreType.DMA((152,)), pltpu.SemaphoreType.DMA((152,)),
]


def per_device(tokens, region, w_qkv, w_proj, w_merge, d_merged):
    levels, lat_rows, lon_cols, feature = tokens.shape
    consts = [jnp.asarray(a, BF) for a in one_hots()]
    anywhere = pl.BlockSpec(memory_space=pl.ANY)
    m_out, gx_out, gw_out = pl.pallas_call(
        kernel,
        out_shape=(
            jax.ShapeDtypeStruct((12, 192, 128), BF),
            jax.ShapeDtypeStruct((levels, 576, feature), F32),
            jax.ShapeDtypeStruct((D, 4 * D), BF),
        ),
        in_specs=[anywhere] * 12,
        out_specs=(anywhere,) * 3,
        scratch_shapes=SCRATCH,
        compiler_params=pltpu.CompilerParams(
            collective_id=0, has_side_effects=True, vmem_limit_bytes=64 * 1024 * 1024
        ),
    )(
        tokens.reshape(levels, 576, feature), region, w_qkv, w_proj, w_merge,
        d_merged.reshape(12, 192, 128), *consts,
    )
    merged, grad_x, grad_qkv, grad_proj = pl.pallas_call(
        finish,
        out_shape=(
            jax.ShapeDtypeStruct((12, 192, 128), BF),
            jax.ShapeDtypeStruct((levels, 576, feature), F32),
            jax.ShapeDtypeStruct((D, 3 * D), F32),
            jax.ShapeDtypeStruct((D, D), F32),
        ),
        in_specs=[anywhere] * 3,
        out_specs=(anywhere,) * 4,
        scratch_shapes=[
            vmem(12, 192, 128), vmem(LEV, 576, D, dtype=F32), vmem(D, 4 * D), vmem(D, 4 * D, dtype=F32),
            pltpu.SemaphoreType.DMA((9,)), pltpu.SemaphoreType.DMA((13,)),
        ],
        compiler_params=pltpu.CompilerParams(vmem_limit_bytes=64 * 1024 * 1024),
    )(m_out, gx_out, gw_out)
    return (
        merged.reshape(levels, 6, 192, 128), grad_x.reshape(levels, lat_rows, lon_cols, feature), grad_qkv, grad_proj
    )


def solution(mesh):
    in_specs = (
        P(None, "lat", "lon", None),
        P("lat", "lon"),
        P(),
        P(),
        P(),
        P(None, "lat", None, "lon"),
    )
    out_specs = (P(None, "lat", None, "lon"), P(None, "lat", "lon", None), P(), P())
    return jax.shard_map(
        per_device, mesh=mesh, in_specs=in_specs, out_specs=out_specs, check_vma=False
    )
```

```python
import functools

import jax
import jax.numpy as jnp
import numpy as np
from jax import lax
from jax.experimental import pallas as pl
from jax.experimental.pallas import tpu as pltpu
from jax.sharding import PartitionSpec as P

D = 512
D2 = 1024
HEADS = 8
LEV = 2
WIN_LAT = 6
WIN_LON = 12
EPS = 1e-05

HALF = 288
EDGE = 36
PACK = 48
SIDE = 112
WIN = 144
TOK = 1152
CELLS = 288
BF = jnp.bfloat16
F32 = jnp.float32
MESH = pl.DeviceIdType.MESH


CHUNK_LANE = (0, 0, 128, 256, 256)
SEGMENTS = []
for _head in range(HEADS):
    _at = _head * WIN
    while _at < (_head + 1) * WIN:
        _end = min((_at // 256 + 1) * 256, (_head + 1) * WIN)
        SEGMENTS.append((_head, _at, _end))
        _at = _end


def one_hots():
    to_win = np.zeros((HALF, HALF), np.float32)
    from_win = np.zeros((HALF + PACK, HALF), np.float32)
    edge_in = np.zeros((4, 80, SIDE), np.float32)
    pack = np.zeros((PACK, HALF), np.float32)
    unpack = np.zeros((3, HALF, SIDE), np.float32)
    for lr in range(6):
        for wc in range(4):
            for cw in range(WIN_LON):
                u = wc * 72 + lr * WIN_LON + cw
                col = WIN_LON * wc + WIN_LON // 2 + cw
                if col < 48:
                    to_win[u, lr * 48 + col] = from_win[lr * 48 + col, u] = 1.0
                else:
                    at = lr * 6 + col - 48
                    from_win[HALF + at, u] = 1.0
                    for half in range(4):
                        edge_in[half, u - 216, half * EDGE + at if half < 3 else 12 + at] = 1.0
        for c in range(6):
            pack[lr * 6 + c, lr * 48 + c] = 1.0
            for half in range(3):
                unpack[half, lr * 48 + c, half * EDGE + lr * 6 + c] = 1.0
    return to_win, from_win, edge_in, pack, unpack, pack.T


def nn(a, b):
    return lax.dot_general(a, b, (((1,), (0,)), ((), ())), preferred_element_type=F32)


def nt(a, b):
    return lax.dot_general(a, b, (((1,), (1,)), ((), ())), preferred_element_type=F32)


def tn(a, b):
    return lax.dot_general(a, b, (((0,), (0,)), ((), ())), preferred_element_type=F32)


def take(ref, rows):
    return jnp.concatenate([ref[c, rows, :] for c in range(4)], 1)


def put(ref, rows, value):
    for c in range(4):
        ref[c, rows, :] = value[:, c * 128:(c + 1) * 128]


def stats(x):
    average = jnp.mean(x, -1, keepdims=True)
    centred = x - average
    variance = jnp.mean(centred * centred, -1, keepdims=True)
    return centred, lax.rsqrt(variance + EPS)


def kernel(
    tokens, region, w_qkv_h, w_proj_h, w_merge_h, d_merged, to_win_h, from_win_h, edge_in_h, pack_h, unpack_h, corner_h,
    m_out, gx_out, gw_out,
    ext, side, corner, regions, region_s, region_e, region_se, keys, key_side, key_corner, key_loose, wq, wp, wm, dm_raw, dm_send, dm_recv, to_win, from_win, edge_in, pack, unpack, uncorner, loose, packed,
    xw, keyw, normed, q, k, v, block_q, block_d, staged, soft, mixed_t, normed_t, mixed, tmp, b_send, b_diag, b_lat, b_side, b_corner,
    grid_s, g, d_in, d_str, d_ext, d_side, d_corner, d_win, d_mix, d_qkv, merged, merged_in, merged_all,
    r_send, r_diag, r_lat, r_side, r_corner,
    grads, core_send, core_recv, send1, recv1, send2, recv2, total,
    local_sem, halo_send, halo_recv, a2a_send, a2a_recv, ar_send, ar_recv,
):
    lat = lax.axis_index("lat")
    lon = lax.axis_index("lon")
    core = lax.rem(lat, 2)
    z_at = lax.rem(lax.div(lat, 2), 4)
    y_lo = lax.div(lat, 8)
    x_at = lax.div(lon, 2)
    y_at = lax.rem(lon, 2) * 2 + y_lo

    south = lax.rem(lat + 1, 16)
    north = lax.rem(lat + 15, 16)
    east = lax.rem(lon + 1, 8)
    west = lax.rem(lon + 7, 8)

    places = {"x": x_at, "y": y_at, "z": z_at}

    def moved_by(steps):
        x, y, z = [lax.rem(places[axis] + steps[axis], 4) if steps.get(axis) else places[axis] for axis in "xyz"]
        return (lax.rem(y, 2) * 8 + z * 2 + core, x * 2 + lax.div(y, 2))

    def on_z(by):
        return moved_by({"z": by})

    def on_y(by):
        return moved_by({"y": by})

    def on_x(by):
        return moved_by({"x": by})

    def on_plane(order, b2, b3):
        return moved_by({order[1]: b2, order[2]: b3})

    def local(i, src, dst):
        copy = pltpu.make_async_copy(src, dst, local_sem.at[i])
        copy.start()
        return copy

    def remote(src, dst, sends, recvs, i, to):
        copy = pltpu.make_async_remote_copy(
            src_ref=src, dst_ref=dst, send_sem=sends.at[i], recv_sem=recvs.at[i], device_id=to, device_id_type=MESH
        )
        copy.start()
        return copy

    started = []

    loads = []
    for hb in range(4):
        for lev in range(LEV):
            rows, place = pl.ds(hb * 144, 144), pl.ds(lev * 144, 144)
            loads.append(local(len(loads), tokens.at[lev, rows], ext.at[hb, place]))
    for src, dst in ((region, regions), (pack_h, pack), (to_win_h, to_win), (d_merged, dm_raw), (w_qkv_h, wq), (w_merge_h, wm),
                     (w_proj_h, wp), (from_win_h, from_win), (unpack_h, unpack), (edge_in_h, edge_in), (corner_h, uncorner)):
        loads.append(local(len(loads), src, dst))
    grid_loads, (l_reg, l_pack, l_to, l_dm, l_wq, l_wm, l_wp, l_from, l_un, l_edge, l_corner) = loads[:8], loads[8:]

    barrier = pltpu.get_barrier_semaphore()
    peers = [(south, lon), (north, lon), (south, east), (north, west)]
    peers += [(lat, lax.rem(lon + by, 8)) for by in range(1, 8)]
    peers += [on_z(by) for by in (1, 2, 3)] + [on_y(by) for by in (1, 3)]
    for first, second in ("xy", "yz", "xz"):
        for b2 in range(1, 4):
            for b3 in range(1, 4):
                if (first, second, b3) != ("x", "y", 2):
                    peers.append(moved_by({first: b2, second: b3}))
    for peer in peers:
        pl.semaphore_signal(barrier, inc=1, device_id=peer, device_id_type=MESH)

    for copy in grid_loads:
        copy.wait()
    l_reg.wait()
    l_pack.wait()

    def gather_edges(number, full):
        for i, hb in enumerate((1, 2, 3, 0)):
            loose[i * EDGE:(i + 1) * EDGE, :] = nn(pack[...], full[hb])[0:EDGE]
        packed[number] = loose[...].astype(BF)

    def send_halo(number, full, to_side, to_corner):
        out = [
            remote(full.at[0], full.at[4], halo_send, halo_recv, number * 3, (north, lon)),
            remote(packed.at[number, pl.ds(0, SIDE)], to_side, halo_send, halo_recv, number * 3 + 1, (lat, west)),
            remote(packed.at[number, pl.ds(96, PACK)], to_corner, halo_send, halo_recv, number * 3 + 2, (north, west)),
        ]
        started.extend(out)
        return out

    gather_edges(0, ext)
    pl.semaphore_wait(barrier, len(peers))
    halo = send_halo(0, ext, side, corner)
    for i, (there, to) in enumerate(((region_s, (north, lon)), (region_e, (lat, west)), (region_se, (north, west)))):
        halo.append(remote(regions, there, halo_send, halo_recv, 12 + i, to))
    started.extend(halo[3:])

    l_dm.wait()
    for s in range(8):
        part = dm_raw[:, s * 24:(s + 1) * 24, :].astype(F32)
        dm_send[s] = part.reshape(CELLS, 128).astype(BF)
    def window_rows(half, first, last, full, to_side, to_corner, wide):
        low_row, high_row = first * 72 // 16 * 16, -(-last * 72 // 16) * 16
        moved = nn(to_win[low_row:high_row, :], full[half + 1])
        for wc in range(first, last):
            at = ((half // 2) * 4 + wc) * WIN + (half % 2) * 72
            part = moved[wc * 72 - low_row:(wc + 1) * 72 - low_row, :]
            if wc == 3:
                if half == 3:
                    part = part + nn(edge_in[3, :, 0:PACK], to_corner[...])[0:72]
                else:
                    part = part + nn(edge_in[half], to_side[...])[0:72]
            wide[at:at + 72, :] = part

    diagonal = lax.broadcasted_iota(jnp.int32, (48, 48), 0) == lax.broadcasted_iota(jnp.int32, (48, 48), 1)

    def key_rows(source, first, extra):
        rows = []
        for row in range(first, first + 3):
            column = jnp.sum(jnp.where(diagonal, source[row:row + 1, :].astype(F32), 0.0), 1, keepdims=True)
            rows.append(jnp.broadcast_to(column + extra, (48, 128)))
        return jnp.concatenate(rows * LEV, 0).astype(BF)

    def norm_window(w, _):
        rows = pl.ds(pl.multiple_of(w * WIN, WIN), WIN)
        centred, inverse = stats(xw[rows, :])
        normed[rows, :] = (centred * inverse).astype(BF)
        return 0

    def project(rows):
        block = normed[rows, :]
        q[rows, :] = (nn(block, wq[:, 0:D]).astype(BF) * 0.125).astype(BF)
        k[rows, :] = nn(block, wq[:, D:2 * D]).astype(BF)
        v[rows, :] = nn(block, wq[:, 2 * D:3 * D]).astype(BF)

    def later_rows(i):
        return pl.ds(pl.multiple_of(3 * WIN + i * 240, 16), 240)

    def project_later(i, _):
        project(later_rows(i))
        return 0

    lane = lax.broadcasted_iota(jnp.int32, (WIN, 128), 1)
    low = lane < 64

    def spread(ref, rows, src, filler):
        blank = jnp.zeros((WIN, 128), BF)
        for head, first, last in SEGMENTS:
            chunk, at = first // 256, pl.ds(first, last - first)
            part = slice(first - head * WIN, last - head * WIN)
            own = src[rows, (head // 2) * 128:(head // 2 + 1) * 128]
            own = jnp.where(low if head % 2 == 0 else ~low, own, blank)
            block = head // 2 - CHUNK_LANE[chunk] // 128
            fill = blank if filler is None else filler
            if chunk == 0:
                ref[at, 0:128] = own[part]
                ref[at, 128:256] = fill[part]
            else:
                ref[at, 0:128] = (jnp.where(low, fill, own) if block == 0 else fill)[part]
                ref[at, 128:256] = (own if block == 1 else blank)[part]

    def by_heads(stage, left, right, chunk):
        out = tn(left, right[:, CHUNK_LANE[chunk]:CHUNK_LANE[chunk] + 256])
        for head, first, last in SEGMENTS:
            if first // 256 == chunk:
                block = head // 2 - CHUNK_LANE[chunk] // 128
                rows = slice(first - chunk * 256, last - chunk * 256)
                stage[first:last, :] = out[rows, block * 128:(block + 1) * 128]

    def joined(stage, pair):
        even, odd = 2 * pair * WIN, (2 * pair + 1) * WIN
        return jnp.where(low, stage[even:even + WIN, :], stage[odd:odd + WIN, :])

    def attend(w, q_b, stage):
        rows = pl.ds(pl.multiple_of(w * WIN, WIN), WIN)
        same = keyw[rows, :] == lane.astype(F32)
        differ = jnp.where(same | ~low, 0.0, 1.0).astype(BF)
        forbid = jnp.where(same, -1e30, 0.0).astype(BF)
        spread(q_b, rows, q, differ)
        k_b = [k[rows, i * 128:(i + 1) * 128] for i in range(4)]
        k_x = [jnp.concatenate([k_b[0], jnp.where(low, forbid, k_b[1])], 1)]
        k_x += [jnp.concatenate([jnp.where(low, forbid, k_b[i]), k_b[i + 1]], 1) for i in range(3)]
        values = v[rows, :]
        for chunk in range(5):
            cols = slice(chunk * 256, min(chunk * 256 + 256, 1152))
            raw = jnp.exp(nt(k_x[min(chunk, 3)], q_b[cols, :]))
            total_w = jnp.sum(raw, 0, keepdims=True)
            shrink = jnp.where(total_w > 1.0, 2.0 ** -32, 1.0)
            part = (raw * shrink) * (1.0 / (total_w * shrink))
            soft[w, :, cols] = part
            by_heads(stage, part.astype(BF), values, chunk)
        for pair in range(4):
            mixed[rows, pair * 128:(pair + 1) * 128] = joined(stage, pair).astype(BF)

    def attend_pair(i, _):
        attend(2 * i, block_q.at[0], staged.at[0])
        attend(2 * i + 1, block_q.at[1], staged.at[1])
        return 0

    l_to.wait()
    for half in range(2):
        window_rows(half, 0, 3, ext, side, corner, xw)
    lax.fori_loop(0, 3, norm_window, 0)
    for half in range(3):
        keys[half + 1] = key_rows(regions, 3 * half + 3, 0.0)
    for half in range(2):
        window_rows(half, 0, 3, keys, key_side, key_corner, keyw)
    l_wq.wait()
    project(slice(0, 3 * WIN))
    mine = pl.ds(pl.multiple_of(lon * 128, 128), 128)
    a2a_in = []

    def send_cotangents(steps):
        for by in steps:
            to = lax.rem(lon + by, 8)
            copy = remote(dm_send.at[to], dm_recv.at[:, mine], a2a_send, a2a_recv, by - 1, (lat, to))
            a2a_in.append(copy)
            started.append(copy)

    send_cotangents((2, 4, 6))
    dm_recv[:, mine] = dm_send[lon]
    attend_pair(0, 0)
    attend(2, block_q.at[0], staged.at[0])

    for copy in halo:
        copy.wait_recv()
    send_cotangents((1, 3, 5, 7))
    l_edge.wait()
    edge_key = jnp.where(lat == 15, 4.0, 0.0)
    keys[4] = key_rows(region_s, 0, edge_key)
    for half in range(4):
        near = key_rows(region_e, 3 * half + 3, 0.0) if half < 3 else key_rows(region_se, 0, edge_key)
        key_loose[half * EDGE:(half + 1) * EDGE, :] = nn(pack[...], near)[0:EDGE]
    key_side[...] = key_loose[0:SIDE, :].astype(BF)
    key_corner[...] = key_loose[96:, :].astype(BF)
    for half in range(4):
        first = 3 if half < 2 else 0
        window_rows(half, first, 4, ext, side, corner, xw)
        window_rows(half, first, 4, keys, key_side, key_corner, keyw)
    lax.fori_loop(3, 8, norm_window, 0)
    lax.fori_loop(0, 3, project_later, 0)
    lax.fori_loop(2, 4, attend_pair, 0)

    l_wp.wait()
    l_from.wait()
    l_un.wait()
    l_corner.wait()

    def to_grid(half, number, lat_send, lat_recv, diag_send, to_side, to_corner, keep):
        first = (half // 2) * 4
        block = jnp.concatenate([tmp[(first + wc) * WIN + (half % 2) * 72:(first + wc) * WIN + (half % 2) * 72 + 72, :] for wc in range(4)], 0)
        moved = nn(from_win[...], block.astype(BF))
        out = []
        if half == 3:
            loose[3 * EDGE:, :] = jnp.zeros((EDGE, D), F32)
            diag_send[...] = moved[HALF:, :].astype(BF)
            lat_send[...] = moved[:HALF, :].astype(BF)
            out.append((lat_send, lat_recv, number * 3, (south, lon)))
            out.append((diag_send, to_corner, number * 3 + 2, (south, east)))
        else:
            put(keep, slice((half + 1) * HALF, (half + 2) * HALF), moved[:HALF, :])
            loose[half * EDGE:(half + 1) * EDGE, :] = moved[HALF:HALF + EDGE, :]
        if half == 0:
            packed[number] = loose[...].astype(BF)
            sides = packed.at[number, pl.ds(0, SIDE)]
            out.append((sides, to_side, number * 3 + 1, (lat, east)))
        return out

    def launch(parts):
        out = [remote(src, dst, halo_send, halo_recv, i, to) for src, dst, i, to in parts]
        started.extend(out)
        return out

    def from_edges(hb, to_side, to_corner):
        return nn(uncorner[...], to_corner[...]) if hb == 0 else nn(unpack[hb - 1], to_side[...])

    branch_halo = []
    for band in (1, 0):
        if band == 0:
            attend(3, block_q.at[0], staged.at[0])
        rows = slice(band * 576, (band + 1) * 576)
        tmp[rows, :] = nn(mixed[rows, :], wp[...])
        for half in (band * 2 + 1, band * 2):
            branch_halo += launch(to_grid(half, 1, b_send, b_lat, b_diag, b_side, b_corner, grid_s))

    l_wm.wait()
    for copy in a2a_in:
        copy.wait_recv()

    def d_in_part(p, _):
        d_in[p] = nt(dm_recv[...], wm[pl.ds(pl.multiple_of(p * D, D), D), :])
        return 0

    lax.fori_loop(0, 4, d_in_part, 0)
    for i in range(9):
        rows = slice(i * 128, (i + 1) * 128)
        normed_t[:, rows] = normed[rows, :].T
        mixed_t[:, rows] = mixed[rows, :].T

    for copy in branch_halo:
        copy.wait_recv()
    for hb in range(4):
        at = slice(hb * HALF, (hb + 1) * HALF)
        own = b_lat[...].astype(F32) if hb == 0 else take(grid_s, at)
        full = own + from_edges(hb, b_side, b_corner)
        put(grid_s, at, (ext[hb].astype(F32) + full).astype(BF).astype(F32))

    def cell_rows(p, lev, i):
        row = 2 * i + p % 2
        return ((row // 3 * 2 + lev) * 3 + row % 3) * 48 + p // 2

    for p in range(4):
        for lev in range(LEV):
            for i in range(6):
                at = (lev * 6 + i) * 24
                g[p, at:at + 24, :] = take(grid_s, pl.ds(cell_rows(p, lev, i), 24, stride=2))

    average = sum(jnp.sum(g[p], -1, keepdims=True) for p in range(4)) / (4 * D)
    variance = 0.0
    for p in range(4):
        centred = g[p] - average
        variance = variance + jnp.sum(centred * centred, -1, keepdims=True)
    inverse = lax.rsqrt(variance / (4 * D) + EPS)
    mean_d = sum(jnp.sum(d_in[p], -1, keepdims=True) for p in range(4)) / (4 * D)
    mean_dh = sum(jnp.sum(d_in[p] * ((g[p] - average) * inverse), -1, keepdims=True) for p in range(4)) / (4 * D)
    for p in range(4):
        hat = (g[p] - average) * inverse
        d_part = inverse * (d_in[p] - mean_d - hat * mean_dh)
        g[p] = hat
        for lev in range(LEV):
            for i in range(6):
                at = (lev * 6 + i) * 24
                put(d_str, pl.ds(cell_rows(p, lev, i), 24, stride=2), d_part[at:at + 24, :])

    for hb in range(4):
        d_ext[hb] = take(d_str, slice(hb * HALF, (hb + 1) * HALF)).astype(BF)
    gather_edges(2, d_ext)
    d_halo = send_halo(2, d_ext, d_side, d_corner)

    for n in range(2):
        cols = slice(n * 512, (n + 1) * 512)
        sums = nn(g[0].astype(BF), wm[0:D, cols])
        for p in range(1, 4):
            sums = sums + nn(g[p].astype(BF), wm[p * D:(p + 1) * D, cols])
        for s in range(4):
            merged[n * 4 + s] = sums[:, s * 128:(s + 1) * 128].astype(BF)
    def back(rows):
        block = tmp[rows, :].astype(BF)
        d_win[rows, :] = block
        d_mix[rows, :] = nt(block, wp[...]).astype(BF)

    def back_later(i, _):
        back(later_rows(i))
        return 0

    def attend_back(w, q_b, d_b, stage):
        rows = pl.ds(pl.multiple_of(w * WIN, WIN), WIN)
        spread(q_b, rows, q, None)
        spread(d_b, rows, d_mix, None)
        keys, values = k[rows, :], v[rows, :]
        d_k, d_v = [], []
        for chunk in range(5):
            cols = slice(chunk * 256, min(chunk * 256 + 256, 1152))
            part = soft[w, :, cols]
            d_soft = nt(values[:, CHUNK_LANE[chunk]:CHUNK_LANE[chunk] + 256], d_b[cols, :])
            delta = jnp.sum(part * d_soft, 0, keepdims=True)
            d_s = (part * (d_soft - delta)).astype(BF)
            d_v.append(nn(part.astype(BF), d_b[cols, :]))
            d_k.append(nn(d_s, q_b[cols, :]))
            by_heads(stage, d_s, keys, chunk)
        for which, d in ((1, d_k), (2, d_v)):
            both = [d[0][:, 0:128] + d[1][:, 0:128], d[1][:, 128:256] + d[2][:, 0:128],
                    d[2][:, 128:256] + d[3][:, 0:128] + d[4][:, 0:128], d[3][:, 128:256] + d[4][:, 128:256]]
            for pair in range(4):
                d_qkv[rows, which * D + pair * 128:which * D + (pair + 1) * 128] = both[pair].astype(BF)
        for pair in range(4):
            d_qkv[rows, pair * 128:(pair + 1) * 128] = (joined(stage, pair) * 0.125).astype(BF)

    def attend_back_pair(i, _):
        attend_back(2 * i, block_q.at[0], block_d.at[0], staged.at[0])
        attend_back(2 * i + 1, block_q.at[1], block_d.at[1], staged.at[1])
        return 0

    orders = (("z", "y", "x"), ("y", "x", "z"), ("x", "z", "y"), ("z", "x", "y"))
    along = {"z": (on_z, z_at), "y": (on_y, y_at), "x": (on_x, x_at)}
    acc1 = d_in
    other = (lat + 1 - 2 * core, lon)
    half_at = pl.multiple_of(core * 256, 256)
    away_at = pl.multiple_of((1 - core) * 256, 256)
    factor = float(LEV * 192 * 384) ** -0.5
    outs = []

    def summed(m):
        (move1, at1), (_, at2), (_, at3) = [along[axis] for axis in orders[m]]

        def send(i, src, dst, to):
            copy = remote(src, dst, ar_send, ar_recv, m * 38 + i, to)
            started.append(copy)
            return copy

        core_send[m] = grads[m, pl.ds(away_at, 256), :].astype(BF)
        flying = [send(0, core_send.at[m], core_recv.at[m], other)]
        yield
        flying[0].wait_recv()
        acc1[m, 0:256, :] = grads[m, pl.ds(half_at, 256), :] + core_recv[m].astype(F32)
        send1[m] = acc1[m, 0:256, :].astype(BF)
        flying = []
        for by in range(1, 4):
            rows = pl.ds(pl.multiple_of(lax.rem(at1 + by, 4) * 64, 64), 64)
            flying.append(send(by, send1.at[m, rows], recv1.at[m, by - 1], move1(by)))
        yield
        for copy in flying:
            copy.wait_recv()
        own = acc1[m, pl.ds(pl.multiple_of(at1 * 64, 64), 64), :]
        for j in range(3):
            own = own + recv1[m, j].astype(F32)
        send2[m] = own.astype(BF)
        acc1[m, 0:64, :] = own
        rest = [(b2, b3) for b2 in range(4) for b3 in range(4) if (b2, b3) != (0, 0)]
        flying = []
        for i, (b2, b3) in enumerate(rest):
            rows = pl.ds(pl.multiple_of(lax.rem(at2 + b2, 4) * 16, 16), 16)
            cols = pl.ds(pl.multiple_of(lax.rem(at3 + b3, 4) * 128, 128), 128)
            flying.append(send(4 + i, send2.at[m, rows, cols], recv2.at[m, i], on_plane(orders[m], b2, b3)))
        yield
        for copy in flying:
            copy.wait_recv()
        row1 = core * 256
        row2 = row1 + at1 * 64
        row3 = row2 + at2 * 16
        rows1, rows2, rows3 = [pl.ds(pl.multiple_of(r, n), n) for r, n in ((row1, 256), (row2, 64), (row3, 16))]
        cols = pl.ds(pl.multiple_of(at3 * 128, 128), 128)
        own = acc1[m, pl.ds(pl.multiple_of(at2 * 16, 16), 16), cols]
        for j in range(15):
            own = own + recv2[m, j].astype(F32)
        total[m, rows3, cols] = (own * factor).astype(BF)
        piece = total.at[m, rows3, cols]
        flying = [send(19 + i, piece, piece, on_plane(orders[m], b2, b3)) for i, (b2, b3) in enumerate(rest)]
        yield
        for copy in flying:
            copy.wait_recv()
        flying = [send(33 + by, total.at[m, rows2], total.at[m, rows2], move1(by)) for by in range(1, 4)]
        yield
        for copy in flying:
            copy.wait_recv()
        flying = [send(37, total.at[m, rows1], total.at[m, rows1], other)]
        yield
        flying[0].wait_recv()
        outs.append(local(m, total.at[m], gw_out.at[:, pl.ds(m * D, D)]))
        yield

    for half in range(2):
        window_rows(half, 0, 3, d_ext, d_side, d_corner, tmp)
    back(slice(0, 3 * WIN))
    attend_back_pair(0, 0)
    attend_back(2, block_q.at[0], block_d.at[0], staged.at[0])
    for copy in d_halo:
        copy.wait_recv()
    for by in range(1, 8):
        to = lax.rem(lon + by, 8)
        started.append(remote(merged.at[to], merged_in.at[lon], a2a_send, a2a_recv, 6 + by, (lat, to)))
    merged_out = started[-7:]
    merged_in[lon] = merged[lon]
    for half in range(4):
        window_rows(half, 3 if half < 2 else 0, 4, d_ext, d_side, d_corner, tmp)
    lax.fori_loop(0, 3, back_later, 0)
    grads[0] = nn(mixed_t[...], d_win[...])
    sums = [summed(0)]
    next(sums[0])
    attend_back_pair(2, 0)
    next(sums[0])
    attend_back_pair(3, 0)
    attend_back(3, block_q.at[0], block_d.at[0], staged.at[0])

    for m in range(3):
        grads[m + 1] = nn(normed_t[...], d_qkv[:, m * D:(m + 1) * D])
        sums.append(summed(m + 1))
        next(sums[m + 1])

    def norm_back_band(band, _):
        rows = pl.ds(pl.multiple_of(band * 576, 576), 576)
        d_norm = nt(d_qkv[rows, :], wq[...])
        centred, inverse = stats(xw[rows, :])
        hat = centred * inverse
        tmp[rows, :] = inverse * (
            d_norm - jnp.mean(d_norm, -1, keepdims=True) - hat * jnp.mean(d_norm * hat, -1, keepdims=True)
        )
        return 0

    roll_parts = []
    for band in (1, 0):
        norm_back_band(band, 0)
        if band == 1:
            for step in sums:
                next(step)
        for half in (band * 2 + 1, band * 2):
            roll_parts += to_grid(half, 3, r_send, r_lat, r_diag, r_side, r_corner, grid_s)
    for step in sums:
        next(step)
    roll_halo = launch(roll_parts)

    for copy in merged_out:
        copy.wait_recv()
    for s in range(8):
        merged_all[:, s * 24:(s + 1) * 24, :] = merged_in[s].astype(F32).reshape(12, 24, 128)
    dm_raw[...] = merged_all[...].astype(BF)
    outs.append(local(4, dm_raw, m_out))
    for _ in range(2):
        for step in sums:
            next(step)

    for copy in roll_halo:
        copy.wait_recv()
    for hb in range(4):
        at = slice(hb * HALF, (hb + 1) * HALF)
        own = r_lat[...].astype(F32) if hb == 0 else take(grid_s, at)
        put(d_str, at, take(d_str, at) + own + from_edges(hb, r_side, r_corner))
        for lev in range(LEV):
            for c in range(4):
                src = d_str.at[c, pl.ds(hb * HALF + lev * 144, 144)]
                to = gx_out.at[lev, pl.ds(hb * 144, 144), pl.ds(c * 128, 128)]
                outs.append(local(5 + hb * 8 + lev * 4 + c, src, to))
    for _ in range(8):
        for step in sums:
            next(step, None)

    for copy in started:
        copy.wait_send()
    for copy in outs:
        copy.wait()


def finish(m_in, gx_in, gw_in, m_out, gx_out, gq_out, gp_out, m_v, gx_v, gw_v, wide, in_sem, out_sem):
    ins, outs = [], []

    def start(sems, held, src, dst):
        copy = pltpu.make_async_copy(src, dst, sems.at[len(held)])
        copy.start()
        held.append(copy)

    quarters = [pl.ds(i * 128, 128) for i in range(4)]
    halves = [(lev, pl.ds(i * 288, 288)) for lev in range(LEV) for i in range(2)]
    for rows in quarters:
        start(in_sem, ins, gw_in.at[rows], gw_v.at[rows])
    for at in halves:
        start(in_sem, ins, gx_in.at[at], gx_v.at[at])
    start(in_sem, ins, m_in, m_v)
    for i, rows in enumerate(quarters):
        ins[i].wait()
        wide[rows, :] = gw_v[rows, :].astype(F32)
        start(out_sem, outs, wide.at[rows, pl.ds(D, 3 * D)], gq_out.at[rows])
        start(out_sem, outs, wide.at[rows, pl.ds(0, D)], gp_out.at[rows])
    for i, at in enumerate(halves):
        ins[4 + i].wait()
        start(out_sem, outs, gx_v.at[at], gx_out.at[at])
    ins[8].wait()
    start(out_sem, outs, m_v, m_out)
    for copy in outs:
        copy.wait()


def vmem(*shape, dtype=BF):
    return pltpu.VMEM(shape, dtype)


SCRATCH = [
    vmem(5, HALF, D), vmem(SIDE, D), vmem(PACK, D)] + [vmem(12, 48, dtype=jnp.int32)] * 4 + [
    vmem(5, HALF, 128), vmem(SIDE, 128), vmem(PACK, 128), vmem(4 * EDGE, 128, dtype=F32), vmem(D, 3 * D), vmem(D, D), vmem(4 * D, D2),
    vmem(12, 192, 128), vmem(8, CELLS, 128), vmem(CELLS, D2), vmem(HALF, HALF), vmem(HALF + PACK, HALF), vmem(4, 80, SIDE),
    vmem(PACK, HALF), vmem(3, HALF, SIDE), vmem(HALF, PACK), vmem(4 * EDGE, D, dtype=F32), vmem(4, 4 * EDGE, D),
    vmem(TOK, D, dtype=F32), vmem(TOK, 128, dtype=F32), vmem(TOK, D), vmem(TOK, D), vmem(TOK, D), vmem(TOK, D),
    vmem(2, 1152, 256), vmem(2, 1152, 256), vmem(2, 1152, 128, dtype=F32), vmem(8, WIN, 1152, dtype=F32), vmem(D, TOK), vmem(D, TOK), vmem(TOK, D), vmem(TOK, D, dtype=F32),
    vmem(HALF, D), vmem(PACK, D), vmem(HALF, D), vmem(SIDE, D), vmem(PACK, D),
    vmem(4, TOK, 128, dtype=F32), vmem(4, CELLS, D, dtype=F32), vmem(4, CELLS, D, dtype=F32), vmem(4, TOK, 128, dtype=F32),
    vmem(5, HALF, D), vmem(SIDE, D), vmem(PACK, D), vmem(TOK, D), vmem(TOK, D), vmem(TOK, 3 * D), vmem(8, CELLS, 128), vmem(8, CELLS, 128), vmem(12, 192, 128, dtype=F32),
    vmem(HALF, D), vmem(PACK, D), vmem(HALF, D), vmem(SIDE, D), vmem(PACK, D),
    vmem(4, D, D, dtype=F32), vmem(4, 256, D), vmem(4, 256, D), vmem(4, 256, D),
    vmem(4, 3, 64, D), vmem(4, 64, D), vmem(4, 15, 16, 128), vmem(4, D, D),
    pltpu.SemaphoreType.DMA((38,)), pltpu.SemaphoreType.DMA((15,)), pltpu.SemaphoreType.DMA((15,)),
    pltpu.SemaphoreType.DMA((14,)), pltpu.SemaphoreType.DMA((14,)),
    pltpu.SemaphoreType.DMA((152,)), pltpu.SemaphoreType.DMA((152,)),
]


def per_device(tokens, region, w_qkv, w_proj, w_merge, d_merged):
    levels, lat_rows, lon_cols, feature = tokens.shape
    consts = [jnp.asarray(a, BF) for a in one_hots()]
    anywhere = pl.BlockSpec(memory_space=pl.ANY)
    m_out, gx_out, gw_out = pl.pallas_call(
        kernel,
        out_shape=(
            jax.ShapeDtypeStruct((12, 192, 128), BF),
            jax.ShapeDtypeStruct((levels, 576, feature), F32),
            jax.ShapeDtypeStruct((D, 4 * D), BF),
        ),
        in_specs=[anywhere] * 12,
        out_specs=(anywhere,) * 3,
        scratch_shapes=SCRATCH,
        compiler_params=pltpu.CompilerParams(
            collective_id=0, has_side_effects=True, vmem_limit_bytes=64 * 1024 * 1024
        ),
    )(
        tokens.reshape(levels, 576, feature), region, w_qkv, w_proj, w_merge,
        d_merged.reshape(12, 192, 128), *consts,
    )
    merged, grad_x, grad_qkv, grad_proj = pl.pallas_call(
        finish,
        out_shape=(
            jax.ShapeDtypeStruct((12, 192, 128), BF),
            jax.ShapeDtypeStruct((levels, 576, feature), F32),
            jax.ShapeDtypeStruct((D, 3 * D), F32),
            jax.ShapeDtypeStruct((D, D), F32),
        ),
        in_specs=[anywhere] * 3,
        out_specs=(anywhere,) * 4,
        scratch_shapes=[
            vmem(12, 192, 128), vmem(LEV, 576, D, dtype=F32), vmem(D, 4 * D), vmem(D, 4 * D, dtype=F32),
            pltpu.SemaphoreType.DMA((9,)), pltpu.SemaphoreType.DMA((13,)),
        ],
        compiler_params=pltpu.CompilerParams(vmem_limit_bytes=64 * 1024 * 1024),
    )(m_out, gx_out, gw_out)
    return (
        merged.reshape(levels, 6, 192, 128), grad_x.reshape(levels, lat_rows, lon_cols, feature), grad_qkv, grad_proj
    )


def solution(mesh):
    in_specs = (
        P(None, "lat", "lon", None),
        P("lat", "lon"),
        P(),
        P(),
        P(),
        P(None, "lat", None, "lon"),
    )
    out_specs = (P(None, "lat", None, "lon"), P(None, "lat", "lon", None), P(), P())
    return jax.shard_map(
        per_device, mesh=mesh, in_specs=in_specs, out_specs=out_specs, check_vma=False
    )
```

```python
import functools

import jax
import jax.numpy as jnp
import numpy as np
from jax import lax
from jax.experimental import pallas as pl
from jax.experimental.pallas import tpu as pltpu
from jax.sharding import PartitionSpec as P

D = 512
D2 = 1024
HEADS = 8
LEV = 2
WIN_LAT = 6
WIN_LON = 12
EPS = 1e-05

HALF = 288
EDGE = 36
PACK = 48
SIDE = 112
WIN = 144
TOK = 1152
CELLS = 288
BF = jnp.bfloat16
F32 = jnp.float32
MESH = pl.DeviceIdType.MESH


CHUNK_LANE = (0, 0, 128, 256, 256)
SEGMENTS = []
for _head in range(HEADS):
    _at = _head * WIN
    while _at < (_head + 1) * WIN:
        _end = min((_at // 256 + 1) * 256, (_head + 1) * WIN)
        SEGMENTS.append((_head, _at, _end))
        _at = _end


def one_hots():
    to_win = np.zeros((HALF, HALF), np.float32)
    from_win = np.zeros((HALF + PACK, HALF), np.float32)
    edge_in = np.zeros((4, 80, SIDE), np.float32)
    pack = np.zeros((PACK, HALF), np.float32)
    unpack = np.zeros((3, HALF, SIDE), np.float32)
    for lr in range(6):
        for wc in range(4):
            for cw in range(WIN_LON):
                u = wc * 72 + lr * WIN_LON + cw
                col = WIN_LON * wc + WIN_LON // 2 + cw
                if col < 48:
                    to_win[u, lr * 48 + col] = from_win[lr * 48 + col, u] = 1.0
                else:
                    at = lr * 6 + col - 48
                    from_win[HALF + at, u] = 1.0
                    for half in range(4):
                        edge_in[half, u - 216, half * EDGE + at if half < 3 else 12 + at] = 1.0
        for c in range(6):
            pack[lr * 6 + c, lr * 48 + c] = 1.0
            for half in range(3):
                unpack[half, lr * 48 + c, half * EDGE + lr * 6 + c] = 1.0
    return to_win, from_win, edge_in, pack, unpack, pack.T


def nn(a, b):
    return lax.dot_general(a, b, (((1,), (0,)), ((), ())), preferred_element_type=F32)


def nt(a, b):
    return lax.dot_general(a, b, (((1,), (1,)), ((), ())), preferred_element_type=F32)


def tn(a, b):
    return lax.dot_general(a, b, (((0,), (0,)), ((), ())), preferred_element_type=F32)


def take(ref, rows):
    return jnp.concatenate([ref[c, rows, :] for c in range(4)], 1)


def put(ref, rows, value):
    for c in range(4):
        ref[c, rows, :] = value[:, c * 128:(c + 1) * 128]


def stats(x):
    average = jnp.mean(x, -1, keepdims=True)
    centred = x - average
    variance = jnp.mean(centred * centred, -1, keepdims=True)
    return centred, lax.rsqrt(variance + EPS)


def kernel(
    tokens, region, w_qkv_h, w_proj_h, w_merge_h, d_merged, to_win_h, from_win_h, edge_in_h, pack_h, unpack_h, corner_h,
    m_out, gx_out, gw_out,
    ext, side, corner, regions, region_s, region_e, region_se, keys, key_side, key_corner, key_loose, wq, wp, wm, dm_raw, dm_send, dm_recv, to_win, from_win, edge_in, pack, unpack, uncorner, loose, packed,
    xw, keyw, normed, q, k, v, block_q, block_d, staged, soft, mixed_t, normed_t, mixed, tmp, b_send, b_diag, b_lat, b_side, b_corner,
    grid_s, g, d_in, d_str, d_ext, d_side, d_corner, d_win, d_mix, d_qkv, merged, merged_in, merged_all,
    r_send, r_diag, r_lat, r_side, r_corner, gx_all,
    grads, core_send, core_recv, send1, recv1, send2, recv2, total,
    local_sem, halo_send, halo_recv, a2a_send, a2a_recv, ar_send, ar_recv,
):
    lat = lax.axis_index("lat")
    lon = lax.axis_index("lon")
    core = lax.rem(lat, 2)
    z_at = lax.rem(lax.div(lat, 2), 4)
    y_lo = lax.div(lat, 8)
    x_at = lax.div(lon, 2)
    y_at = lax.rem(lon, 2) * 2 + y_lo

    south = lax.rem(lat + 1, 16)
    north = lax.rem(lat + 15, 16)
    east = lax.rem(lon + 1, 8)
    west = lax.rem(lon + 7, 8)

    places = {"x": x_at, "y": y_at, "z": z_at}

    def moved_by(steps):
        x, y, z = [lax.rem(places[axis] + steps[axis], 4) if steps.get(axis) else places[axis] for axis in "xyz"]
        return (lax.rem(y, 2) * 8 + z * 2 + core, x * 2 + lax.div(y, 2))

    def on_z(by):
        return moved_by({"z": by})

    def on_y(by):
        return moved_by({"y": by})

    def on_x(by):
        return moved_by({"x": by})

    def on_plane(order, b2, b3):
        return moved_by({order[1]: b2, order[2]: b3})

    def local(i, src, dst):
        copy = pltpu.make_async_copy(src, dst, local_sem.at[i])
        copy.start()
        return copy

    def remote(src, dst, sends, recvs, i, to):
        copy = pltpu.make_async_remote_copy(
            src_ref=src, dst_ref=dst, send_sem=sends.at[i], recv_sem=recvs.at[i], device_id=to, device_id_type=MESH
        )
        copy.start()
        return copy

    started = []

    loads = []
    for hb in range(4):
        for lev in range(LEV):
            rows, place = pl.ds(hb * 144, 144), pl.ds(lev * 144, 144)
            loads.append(local(len(loads), tokens.at[lev, rows], ext.at[hb, place]))
    l_reg = local(8, region, regions)
    l_pack = local(9, pack_h, pack)

    barrier = pltpu.get_barrier_semaphore()
    peers = [(south, lon), (north, lon), (south, east), (north, west)]
    peers += [(lat, lax.rem(lon + by, 8)) for by in range(1, 8)]
    peers += [on_z(by) for by in (1, 2, 3)] + [on_y(by) for by in (1, 3)]
    for first, second in ("xy", "yz", "xz"):
        for b2 in range(1, 4):
            for b3 in range(1, 4):
                if (first, second, b3) != ("x", "y", 2):
                    peers.append(moved_by({first: b2, second: b3}))
    for peer in peers:
        pl.semaphore_signal(barrier, inc=1, device_id=peer, device_id_type=MESH)

    for copy in loads:
        copy.wait()
    later = ((to_win_h, to_win), (w_qkv_h, wq), (d_merged, dm_raw), (edge_in_h, edge_in), (w_proj_h, wp),
             (from_win_h, from_win), (unpack_h, unpack), (corner_h, uncorner), (w_merge_h, wm))
    l_to, l_wq, l_dm, l_edge, l_wp, l_from, l_un, l_corner, l_wm = [
        local(10 + i, src, dst) for i, (src, dst) in enumerate(later)
    ]
    l_reg.wait()
    l_pack.wait()

    def gather_edges(number, full):
        for i, hb in enumerate((1, 2, 3, 0)):
            loose[i * EDGE:(i + 1) * EDGE, :] = nn(pack[...], full[hb])[0:EDGE]
        packed[number] = loose[...].astype(BF)

    def send_halo(number, full, to_side, to_corner):
        out = [
            remote(full.at[0], full.at[4], halo_send, halo_recv, number * 3, (north, lon)),
            remote(packed.at[number, pl.ds(0, SIDE)], to_side, halo_send, halo_recv, number * 3 + 1, (lat, west)),
            remote(packed.at[number, pl.ds(96, PACK)], to_corner, halo_send, halo_recv, number * 3 + 2, (north, west)),
        ]
        started.extend(out)
        return out

    gather_edges(0, ext)
    pl.semaphore_wait(barrier, len(peers))
    halo = send_halo(0, ext, side, corner)
    for i, (there, to) in enumerate(((region_s, (north, lon)), (region_e, (lat, west)), (region_se, (north, west)))):
        halo.append(remote(regions, there, halo_send, halo_recv, 12 + i, to))
    started.extend(halo[3:])

    l_dm.wait()
    for s in range(8):
        part = dm_raw[:, s * 24:(s + 1) * 24, :].astype(F32)
        dm_send[s] = part.reshape(CELLS, 128).astype(BF)
    def window_rows(half, first, last, full, to_side, to_corner, wide):
        low_row, high_row = first * 72 // 16 * 16, -(-last * 72 // 16) * 16
        moved = nn(to_win[low_row:high_row, :], full[half + 1])
        for wc in range(first, last):
            at = ((half // 2) * 4 + wc) * WIN + (half % 2) * 72
            part = moved[wc * 72 - low_row:(wc + 1) * 72 - low_row, :]
            if wc == 3:
                if half == 3:
                    part = part + nn(edge_in[3, :, 0:PACK], to_corner[...])[0:72]
                else:
                    part = part + nn(edge_in[half], to_side[...])[0:72]
            wide[at:at + 72, :] = part

    diagonal = lax.broadcasted_iota(jnp.int32, (48, 48), 0) == lax.broadcasted_iota(jnp.int32, (48, 48), 1)

    def key_rows(source, first, extra):
        rows = []
        for row in range(first, first + 3):
            column = jnp.sum(jnp.where(diagonal, source[row:row + 1, :].astype(F32), 0.0), 1, keepdims=True)
            rows.append(jnp.broadcast_to(column + extra, (48, 128)))
        return jnp.concatenate(rows * LEV, 0).astype(BF)

    def norm_window(w, _):
        rows = pl.ds(pl.multiple_of(w * WIN, WIN), WIN)
        centred, inverse = stats(xw[rows, :])
        normed[rows, :] = (centred * inverse).astype(BF)
        return 0

    def project(rows):
        block = normed[rows, :]
        q[rows, :] = (nn(block, wq[:, 0:D]).astype(BF) * 0.125).astype(BF)
        k[rows, :] = nn(block, wq[:, D:2 * D]).astype(BF)
        v[rows, :] = nn(block, wq[:, 2 * D:3 * D]).astype(BF)

    def later_rows(i):
        return pl.ds(pl.multiple_of(3 * WIN + i * 240, 16), 240)

    def project_later(i, _):
        project(later_rows(i))
        return 0

    lane = lax.broadcasted_iota(jnp.int32, (WIN, 128), 1)
    low = lane < 64

    def spread(ref, rows, src, filler):
        blank = jnp.zeros((WIN, 128), BF)
        for head, first, last in SEGMENTS:
            chunk, at = first // 256, pl.ds(first, last - first)
            part = slice(first - head * WIN, last - head * WIN)
            own = src[rows, (head // 2) * 128:(head // 2 + 1) * 128]
            own = jnp.where(low if head % 2 == 0 else ~low, own, blank)
            block = head // 2 - CHUNK_LANE[chunk] // 128
            fill = blank if filler is None else filler
            if chunk == 0:
                ref[at, 0:128] = own[part]
                ref[at, 128:256] = fill[part]
            else:
                ref[at, 0:128] = (jnp.where(low, fill, own) if block == 0 else fill)[part]
                ref[at, 128:256] = (own if block == 1 else blank)[part]

    def by_heads(stage, left, right, chunk):
        out = tn(left, right[:, CHUNK_LANE[chunk]:CHUNK_LANE[chunk] + 256])
        for head, first, last in SEGMENTS:
            if first // 256 == chunk:
                block = head // 2 - CHUNK_LANE[chunk] // 128
                rows = slice(first - chunk * 256, last - chunk * 256)
                stage[first:last, :] = out[rows, block * 128:(block + 1) * 128]

    def joined(stage, pair):
        even, odd = 2 * pair * WIN, (2 * pair + 1) * WIN
        return jnp.where(low, stage[even:even + WIN, :], stage[odd:odd + WIN, :])

    def attend(w, q_b, stage):
        rows = pl.ds(pl.multiple_of(w * WIN, WIN), WIN)
        same = keyw[rows, :] == lane.astype(F32)
        differ = jnp.where(same | ~low, 0.0, 1.0).astype(BF)
        forbid = jnp.where(same, -1e30, 0.0).astype(BF)
        spread(q_b, rows, q, differ)
        k_b = [k[rows, i * 128:(i + 1) * 128] for i in range(4)]
        k_x = [jnp.concatenate([k_b[0], jnp.where(low, forbid, k_b[1])], 1)]
        k_x += [jnp.concatenate([jnp.where(low, forbid, k_b[i]), k_b[i + 1]], 1) for i in range(3)]
        values = v[rows, :]
        for chunk in range(5):
            cols = slice(chunk * 256, min(chunk * 256 + 256, 1152))
            raw = jnp.exp(nt(k_x[min(chunk, 3)], q_b[cols, :]))
            total_w = jnp.sum(raw, 0, keepdims=True)
            shrink = jnp.where(total_w > 1.0, 2.0 ** -32, 1.0)
            part = (raw * shrink) * (1.0 / (total_w * shrink))
            soft[w, :, cols] = part
            by_heads(stage, part.astype(BF), values, chunk)
        for pair in range(4):
            mixed[rows, pair * 128:(pair + 1) * 128] = joined(stage, pair).astype(BF)

    def attend_pair(i, _):
        attend(2 * i, block_q.at[0], staged.at[0])
        attend(2 * i + 1, block_q.at[1], staged.at[1])
        return 0

    l_to.wait()
    for half in range(2):
        window_rows(half, 0, 3, ext, side, corner, xw)
    lax.fori_loop(0, 3, norm_window, 0)
    for half in range(3):
        keys[half + 1] = key_rows(regions, 3 * half + 3, 0.0)
    for half in range(2):
        window_rows(half, 0, 3, keys, key_side, key_corner, keyw)
    l_wq.wait()
    project(slice(0, 3 * WIN))
    mine = pl.ds(pl.multiple_of(lon * 128, 128), 128)
    a2a_in = []

    def send_cotangents(steps):
        for by in steps:
            to = lax.rem(lon + by, 8)
            copy = remote(dm_send.at[to], dm_recv.at[:, mine], a2a_send, a2a_recv, by - 1, (lat, to))
            a2a_in.append(copy)
            started.append(copy)

    send_cotangents((2, 4, 6))
    dm_recv[:, mine] = dm_send[lon]
    attend_pair(0, 0)
    attend(2, block_q.at[0], staged.at[0])

    for copy in halo:
        copy.wait_recv()
    send_cotangents((1, 3, 5, 7))
    l_edge.wait()
    edge_key = jnp.where(lat == 15, 4.0, 0.0)
    keys[4] = key_rows(region_s, 0, edge_key)
    for half in range(4):
        near = key_rows(region_e, 3 * half + 3, 0.0) if half < 3 else key_rows(region_se, 0, edge_key)
        key_loose[half * EDGE:(half + 1) * EDGE, :] = nn(pack[...], near)[0:EDGE]
    key_side[...] = key_loose[0:SIDE, :].astype(BF)
    key_corner[...] = key_loose[96:, :].astype(BF)
    for half in range(4):
        first = 3 if half < 2 else 0
        window_rows(half, first, 4, ext, side, corner, xw)
        window_rows(half, first, 4, keys, key_side, key_corner, keyw)
    lax.fori_loop(3, 8, norm_window, 0)
    lax.fori_loop(0, 3, project_later, 0)
    lax.fori_loop(2, 4, attend_pair, 0)

    l_wp.wait()
    l_from.wait()
    l_un.wait()
    l_corner.wait()

    def to_grid(half, number, lat_send, lat_recv, diag_send, to_side, to_corner, keep):
        first = (half // 2) * 4
        block = jnp.concatenate([tmp[(first + wc) * WIN + (half % 2) * 72:(first + wc) * WIN + (half % 2) * 72 + 72, :] for wc in range(4)], 0)
        moved = nn(from_win[...], block.astype(BF))
        out = []
        if half == 3:
            loose[3 * EDGE:, :] = jnp.zeros((EDGE, D), F32)
            diag_send[...] = moved[HALF:, :].astype(BF)
            lat_send[...] = moved[:HALF, :].astype(BF)
            out.append((lat_send, lat_recv, number * 3, (south, lon)))
            out.append((diag_send, to_corner, number * 3 + 2, (south, east)))
        else:
            put(keep, slice((half + 1) * HALF, (half + 2) * HALF), moved[:HALF, :])
            loose[half * EDGE:(half + 1) * EDGE, :] = moved[HALF:HALF + EDGE, :]
        if half == 0:
            packed[number] = loose[...].astype(BF)
            sides = packed.at[number, pl.ds(0, SIDE)]
            out.append((sides, to_side, number * 3 + 1, (lat, east)))
        return out

    def launch(parts):
        out = [remote(src, dst, halo_send, halo_recv, i, to) for src, dst, i, to in parts]
        started.extend(out)
        return out

    def from_edges(hb, to_side, to_corner):
        return nn(uncorner[...], to_corner[...]) if hb == 0 else nn(unpack[hb - 1], to_side[...])

    branch_halo = []
    for band in (1, 0):
        if band == 0:
            attend(3, block_q.at[0], staged.at[0])
        rows = slice(band * 576, (band + 1) * 576)
        tmp[rows, :] = nn(mixed[rows, :], wp[...])
        for half in (band * 2 + 1, band * 2):
            branch_halo += launch(to_grid(half, 1, b_send, b_lat, b_diag, b_side, b_corner, grid_s))

    l_wm.wait()
    for copy in a2a_in:
        copy.wait_recv()

    def d_in_part(p, _):
        d_in[p] = nt(dm_recv[...], wm[pl.ds(pl.multiple_of(p * D, D), D), :])
        return 0

    lax.fori_loop(0, 4, d_in_part, 0)
    for i in range(9):
        rows = slice(i * 128, (i + 1) * 128)
        normed_t[:, rows] = normed[rows, :].T
        mixed_t[:, rows] = mixed[rows, :].T

    for copy in branch_halo:
        copy.wait_recv()
    for hb in range(4):
        at = slice(hb * HALF, (hb + 1) * HALF)
        own = b_lat[...].astype(F32) if hb == 0 else take(grid_s, at)
        full = own + from_edges(hb, b_side, b_corner)
        put(grid_s, at, (ext[hb].astype(F32) + full).astype(BF).astype(F32))

    def cell_rows(p, lev, i):
        row = 2 * i + p % 2
        return ((row // 3 * 2 + lev) * 3 + row % 3) * 48 + p // 2

    for p in range(4):
        for lev in range(LEV):
            for i in range(6):
                at = (lev * 6 + i) * 24
                g[p, at:at + 24, :] = take(grid_s, pl.ds(cell_rows(p, lev, i), 24, stride=2))

    average = sum(jnp.sum(g[p], -1, keepdims=True) for p in range(4)) / (4 * D)
    variance = 0.0
    for p in range(4):
        centred = g[p] - average
        variance = variance + jnp.sum(centred * centred, -1, keepdims=True)
    inverse = lax.rsqrt(variance / (4 * D) + EPS)
    mean_d = sum(jnp.sum(d_in[p], -1, keepdims=True) for p in range(4)) / (4 * D)
    mean_dh = sum(jnp.sum(d_in[p] * ((g[p] - average) * inverse), -1, keepdims=True) for p in range(4)) / (4 * D)
    for p in range(4):
        hat = (g[p] - average) * inverse
        d_part = inverse * (d_in[p] - mean_d - hat * mean_dh)
        g[p] = hat
        for lev in range(LEV):
            for i in range(6):
                at = (lev * 6 + i) * 24
                put(d_str, pl.ds(cell_rows(p, lev, i), 24, stride=2), d_part[at:at + 24, :])

    for hb in range(4):
        d_ext[hb] = take(d_str, slice(hb * HALF, (hb + 1) * HALF)).astype(BF)
    gather_edges(2, d_ext)
    d_halo = send_halo(2, d_ext, d_side, d_corner)

    for n in range(2):
        cols = slice(n * 512, (n + 1) * 512)
        sums = nn(g[0].astype(BF), wm[0:D, cols])
        for p in range(1, 4):
            sums = sums + nn(g[p].astype(BF), wm[p * D:(p + 1) * D, cols])
        for s in range(4):
            merged[n * 4 + s] = sums[:, s * 128:(s + 1) * 128].astype(BF)
    merged_out = []

    def send_merged(steps):
        for by in steps:
            to = lax.rem(lon + by, 8)
            copy = remote(merged.at[to], merged_in.at[lon], a2a_send, a2a_recv, 6 + by, (lat, to))
            merged_out.append(copy)
            started.append(copy)

    send_merged((2, 4, 6))
    merged_in[lon] = merged[lon]

    def back(rows):
        block = tmp[rows, :].astype(BF)
        d_win[rows, :] = block
        d_mix[rows, :] = nt(block, wp[...]).astype(BF)

    def back_later(i, _):
        back(later_rows(i))
        return 0

    def attend_back(w, q_b, d_b, stage):
        rows = pl.ds(pl.multiple_of(w * WIN, WIN), WIN)
        spread(q_b, rows, q, None)
        spread(d_b, rows, d_mix, None)
        keys, values = k[rows, :], v[rows, :]
        d_k, d_v = [], []
        for chunk in range(5):
            cols = slice(chunk * 256, min(chunk * 256 + 256, 1152))
            part = soft[w, :, cols]
            d_soft = nt(values[:, CHUNK_LANE[chunk]:CHUNK_LANE[chunk] + 256], d_b[cols, :])
            delta = jnp.sum(part * d_soft, 0, keepdims=True)
            d_s = (part * (d_soft - delta)).astype(BF)
            d_v.append(nn(part.astype(BF), d_b[cols, :]))
            d_k.append(nn(d_s, q_b[cols, :]))
            by_heads(stage, d_s, keys, chunk)
        for which, d in ((1, d_k), (2, d_v)):
            both = [d[0][:, 0:128] + d[1][:, 0:128], d[1][:, 128:256] + d[2][:, 0:128],
                    d[2][:, 128:256] + d[3][:, 0:128] + d[4][:, 0:128], d[3][:, 128:256] + d[4][:, 128:256]]
            for pair in range(4):
                d_qkv[rows, which * D + pair * 128:which * D + (pair + 1) * 128] = both[pair].astype(BF)
        for pair in range(4):
            d_qkv[rows, pair * 128:(pair + 1) * 128] = (joined(stage, pair) * 0.125).astype(BF)

    def attend_back_pair(i, _):
        attend_back(2 * i, block_q.at[0], block_d.at[0], staged.at[0])
        attend_back(2 * i + 1, block_q.at[1], block_d.at[1], staged.at[1])
        return 0

    orders = (("z", "y", "x"), ("y", "x", "z"), ("x", "z", "y"), ("z", "x", "y"))
    along = {"z": (on_z, z_at), "y": (on_y, y_at), "x": (on_x, x_at)}
    acc1 = d_in
    other = (lat + 1 - 2 * core, lon)
    half_at = pl.multiple_of(core * 256, 256)
    away_at = pl.multiple_of((1 - core) * 256, 256)
    factor = float(LEV * 192 * 384) ** -0.5
    outs = []

    def summed(m):
        (move1, at1), (_, at2), (_, at3) = [along[axis] for axis in orders[m]]

        def send(i, src, dst, to):
            copy = remote(src, dst, ar_send, ar_recv, m * 38 + i, to)
            started.append(copy)
            return copy

        core_send[m] = grads[m, pl.ds(away_at, 256), :].astype(BF)
        flying = [send(0, core_send.at[m], core_recv.at[m], other)]
        yield
        flying[0].wait_recv()
        acc1[m, 0:256, :] = grads[m, pl.ds(half_at, 256), :] + core_recv[m].astype(F32)
        send1[m] = acc1[m, 0:256, :].astype(BF)
        flying = []
        for by in range(1, 4):
            rows = pl.ds(pl.multiple_of(lax.rem(at1 + by, 4) * 64, 64), 64)
            flying.append(send(by, send1.at[m, rows], recv1.at[m, by - 1], move1(by)))
        yield
        for copy in flying:
            copy.wait_recv()
        own = acc1[m, pl.ds(pl.multiple_of(at1 * 64, 64), 64), :]
        for j in range(3):
            own = own + recv1[m, j].astype(F32)
        send2[m] = own.astype(BF)
        acc1[m, 0:64, :] = own
        rest = [(b2, b3) for b2 in range(4) for b3 in range(4) if (b2, b3) != (0, 0)]
        flying = []
        for i, (b2, b3) in enumerate(rest):
            rows = pl.ds(pl.multiple_of(lax.rem(at2 + b2, 4) * 16, 16), 16)
            cols = pl.ds(pl.multiple_of(lax.rem(at3 + b3, 4) * 128, 128), 128)
            flying.append(send(4 + i, send2.at[m, rows, cols], recv2.at[m, i], on_plane(orders[m], b2, b3)))
        yield
        for copy in flying:
            copy.wait_recv()
        row1 = core * 256
        row2 = row1 + at1 * 64
        row3 = row2 + at2 * 16
        rows1, rows2, rows3 = [pl.ds(pl.multiple_of(r, n), n) for r, n in ((row1, 256), (row2, 64), (row3, 16))]
        cols = pl.ds(pl.multiple_of(at3 * 128, 128), 128)
        own = acc1[m, pl.ds(pl.multiple_of(at2 * 16, 16), 16), cols]
        for j in range(15):
            own = own + recv2[m, j].astype(F32)
        total[m, rows3, cols] = (own * factor).astype(BF)
        piece = total.at[m, rows3, cols]
        flying = [send(19 + i, piece, piece, on_plane(orders[m], b2, b3)) for i, (b2, b3) in enumerate(rest)]
        yield
        for copy in flying:
            copy.wait_recv()
        flying = [send(33 + by, total.at[m, rows2], total.at[m, rows2], move1(by)) for by in range(1, 4)]
        yield
        for copy in flying:
            copy.wait_recv()
        flying = [send(37, total.at[m, rows1], total.at[m, rows1], other)]
        yield
        flying[0].wait_recv()
        outs.append(local(m, total.at[m], gw_out.at[:, pl.ds(m * D, D)]))
        yield

    for half in range(2):
        window_rows(half, 0, 3, d_ext, d_side, d_corner, tmp)
    back(slice(0, 3 * WIN))
    attend_back_pair(0, 0)
    attend_back(2, block_q.at[0], block_d.at[0], staged.at[0])
    for copy in d_halo:
        copy.wait_recv()
    send_merged((1, 3, 5, 7))
    for half in range(4):
        window_rows(half, 3 if half < 2 else 0, 4, d_ext, d_side, d_corner, tmp)
    lax.fori_loop(0, 3, back_later, 0)
    grads[0] = nn(mixed_t[...], d_win[...])
    sums = [summed(0)]
    next(sums[0])
    attend_back_pair(2, 0)
    next(sums[0])
    attend_back_pair(3, 0)
    attend_back(3, block_q.at[0], block_d.at[0], staged.at[0])

    for m in range(3):
        grads[m + 1] = nn(normed_t[...], d_qkv[:, m * D:(m + 1) * D])
        sums.append(summed(m + 1))
        next(sums[m + 1])

    def norm_back_band(band, _):
        rows = pl.ds(pl.multiple_of(band * 576, 576), 576)
        d_norm = nt(d_qkv[rows, :], wq[...])
        centred, inverse = stats(xw[rows, :])
        hat = centred * inverse
        tmp[rows, :] = inverse * (
            d_norm - jnp.mean(d_norm, -1, keepdims=True) - hat * jnp.mean(d_norm * hat, -1, keepdims=True)
        )
        return 0

    roll_parts = []
    for band in (1, 0):
        norm_back_band(band, 0)
        if band == 1:
            for step in sums:
                next(step)
        for half in (band * 2 + 1, band * 2):
            roll_parts += to_grid(half, 3, r_send, r_lat, r_diag, r_side, r_corner, grid_s)
    for step in sums:
        next(step)
    roll_halo = launch(roll_parts)

    for copy in merged_out:
        copy.wait_recv()
    for s in range(8):
        merged_all[:, s * 24:(s + 1) * 24, :] = merged_in[s].astype(F32).reshape(12, 24, 128)
    dm_raw[...] = merged_all[...].astype(BF)
    outs.append(local(4, dm_raw, m_out))
    for _ in range(2):
        for step in sums:
            next(step)

    for copy in roll_halo:
        copy.wait_recv()
    for hb in range(4):
        at = slice(hb * HALF, (hb + 1) * HALF)
        own = r_lat[...].astype(F32) if hb == 0 else take(grid_s, at)
        gx_all[hb] = (take(d_str, at) + own + from_edges(hb, r_side, r_corner)).astype(BF)
        for lev in range(LEV):
            src = gx_all.at[hb, pl.ds(lev * 144, 144)]
            outs.append(local(5 + hb * 2 + lev, src, gx_out.at[lev, pl.ds(hb * 144, 144)]))
    for _ in range(8):
        for step in sums:
            next(step, None)

    for copy in started:
        copy.wait_send()
    for copy in outs:
        copy.wait()


def finish(m_in, gx_in, gw_in, m_out, gx_out, gq_out, gp_out, m_v, gx_v, gx_wide, gw_v, wide, in_sem, out_sem):
    ins, outs = [], []

    def start(sems, held, src, dst):
        copy = pltpu.make_async_copy(src, dst, sems.at[len(held)])
        copy.start()
        held.append(copy)

    quarters = [pl.ds(i * 128, 128) for i in range(4)]
    halves = [(lev, pl.ds(i * 288, 288)) for lev in range(LEV) for i in range(2)]
    for rows in quarters:
        start(in_sem, ins, gw_in.at[rows], gw_v.at[rows])
    for at in halves:
        start(in_sem, ins, gx_in.at[at], gx_v.at[at])
    start(in_sem, ins, m_in, m_v)
    for i, rows in enumerate(quarters):
        ins[i].wait()
        wide[rows, :] = gw_v[rows, :].astype(F32)
        start(out_sem, outs, wide.at[rows, pl.ds(D, 3 * D)], gq_out.at[rows])
        start(out_sem, outs, wide.at[rows, pl.ds(0, D)], gp_out.at[rows])
    for i, at in enumerate(halves):
        ins[4 + i].wait()
        gx_wide[at] = gx_v[at].astype(F32)
        start(out_sem, outs, gx_wide.at[at], gx_out.at[at])
    ins[8].wait()
    start(out_sem, outs, m_v, m_out)
    for copy in outs:
        copy.wait()


def vmem(*shape, dtype=BF):
    return pltpu.VMEM(shape, dtype)


SCRATCH = [
    vmem(5, HALF, D), vmem(SIDE, D), vmem(PACK, D)] + [vmem(12, 48, dtype=jnp.int32)] * 4 + [
    vmem(5, HALF, 128), vmem(SIDE, 128), vmem(PACK, 128), vmem(4 * EDGE, 128, dtype=F32), vmem(D, 3 * D), vmem(D, D), vmem(4 * D, D2),
    vmem(12, 192, 128), vmem(8, CELLS, 128), vmem(CELLS, D2), vmem(HALF, HALF), vmem(HALF + PACK, HALF), vmem(4, 80, SIDE),
    vmem(PACK, HALF), vmem(3, HALF, SIDE), vmem(HALF, PACK), vmem(4 * EDGE, D, dtype=F32), vmem(4, 4 * EDGE, D),
    vmem(TOK, D, dtype=F32), vmem(TOK, 128, dtype=F32), vmem(TOK, D), vmem(TOK, D), vmem(TOK, D), vmem(TOK, D),
    vmem(2, 1152, 256), vmem(2, 1152, 256), vmem(2, 1152, 128, dtype=F32), vmem(8, WIN, 1152, dtype=F32), vmem(D, TOK), vmem(D, TOK), vmem(TOK, D), vmem(TOK, D, dtype=F32),
    vmem(HALF, D), vmem(PACK, D), vmem(HALF, D), vmem(SIDE, D), vmem(PACK, D),
    vmem(4, TOK, 128, dtype=F32), vmem(4, CELLS, D, dtype=F32), vmem(4, CELLS, D, dtype=F32), vmem(4, TOK, 128, dtype=F32),
    vmem(5, HALF, D), vmem(SIDE, D), vmem(PACK, D), vmem(TOK, D), vmem(TOK, D), vmem(TOK, 3 * D), vmem(8, CELLS, 128), vmem(8, CELLS, 128), vmem(12, 192, 128, dtype=F32),
    vmem(HALF, D), vmem(PACK, D), vmem(HALF, D), vmem(SIDE, D), vmem(PACK, D), vmem(4, HALF, D),
    vmem(4, D, D, dtype=F32), vmem(4, 256, D), vmem(4, 256, D), vmem(4, 256, D),
    vmem(4, 3, 64, D), vmem(4, 64, D), vmem(4, 15, 16, 128), vmem(4, D, D),
    pltpu.SemaphoreType.DMA((38,)), pltpu.SemaphoreType.DMA((15,)), pltpu.SemaphoreType.DMA((15,)),
    pltpu.SemaphoreType.DMA((14,)), pltpu.SemaphoreType.DMA((14,)),
    pltpu.SemaphoreType.DMA((152,)), pltpu.SemaphoreType.DMA((152,)),
]


def per_device(tokens, region, w_qkv, w_proj, w_merge, d_merged):
    levels, lat_rows, lon_cols, feature = tokens.shape
    consts = [jnp.asarray(a, BF) for a in one_hots()]
    anywhere = pl.BlockSpec(memory_space=pl.ANY)
    m_out, gx_out, gw_out = pl.pallas_call(
        kernel,
        out_shape=(
            jax.ShapeDtypeStruct((12, 192, 128), BF),
            jax.ShapeDtypeStruct((levels, 576, feature), BF),
            jax.ShapeDtypeStruct((D, 4 * D), BF),
        ),
        in_specs=[anywhere] * 12,
        out_specs=(anywhere,) * 3,
        scratch_shapes=SCRATCH,
        compiler_params=pltpu.CompilerParams(
            collective_id=0, has_side_effects=True, vmem_limit_bytes=64 * 1024 * 1024
        ),
    )(
        tokens.reshape(levels, 576, feature), region, w_qkv, w_proj, w_merge,
        d_merged.reshape(12, 192, 128), *consts,
    )
    merged, grad_x, grad_qkv, grad_proj = pl.pallas_call(
        finish,
        out_shape=(
            jax.ShapeDtypeStruct((12, 192, 128), BF),
            jax.ShapeDtypeStruct((levels, 576, feature), F32),
            jax.ShapeDtypeStruct((D, 3 * D), F32),
            jax.ShapeDtypeStruct((D, D), F32),
        ),
        in_specs=[anywhere] * 3,
        out_specs=(anywhere,) * 4,
        scratch_shapes=[
            vmem(12, 192, 128), vmem(LEV, 576, D), vmem(LEV, 576, D, dtype=F32), vmem(D, 4 * D), vmem(D, 4 * D, dtype=F32),
            pltpu.SemaphoreType.DMA((9,)), pltpu.SemaphoreType.DMA((13,)),
        ],
        compiler_params=pltpu.CompilerParams(vmem_limit_bytes=64 * 1024 * 1024),
    )(m_out, gx_out, gw_out)
    return (
        merged.reshape(levels, 6, 192, 128), grad_x.reshape(levels, lat_rows, lon_cols, feature), grad_qkv, grad_proj
    )


def solution(mesh):
    in_specs = (
        P(None, "lat", "lon", None),
        P("lat", "lon"),
        P(),
        P(),
        P(),
        P(None, "lat", None, "lon"),
    )
    out_specs = (P(None, "lat", None, "lon"), P(None, "lat", "lon", None), P(), P())
    return jax.shard_map(
        per_device, mesh=mesh, in_specs=in_specs, out_specs=out_specs, check_vma=False
    )
```

```python
import functools

import jax
import jax.numpy as jnp
import numpy as np
from jax import lax
from jax.experimental import pallas as pl
from jax.experimental.pallas import tpu as pltpu
from jax.sharding import PartitionSpec as P

D = 512
D2 = 1024
HEADS = 8
LEV = 2
WIN_LAT = 6
WIN_LON = 12
EPS = 1e-05

HALF = 288
EDGE = 36
PACK = 48
SIDE = 112
WIN = 144
TOK = 1152
CELLS = 288
BF = jnp.bfloat16
F32 = jnp.float32
MESH = pl.DeviceIdType.MESH


CHUNK_LANE = (0, 0, 128, 256, 256)
SEGMENTS = []
for _head in range(HEADS):
    _at = _head * WIN
    while _at < (_head + 1) * WIN:
        _end = min((_at // 256 + 1) * 256, (_head + 1) * WIN)
        SEGMENTS.append((_head, _at, _end))
        _at = _end


def one_hots():
    to_win = np.zeros((HALF, HALF), np.float32)
    from_win = np.zeros((HALF + PACK, HALF), np.float32)
    edge_in = np.zeros((4, 80, SIDE), np.float32)
    pack = np.zeros((PACK, HALF), np.float32)
    unpack = np.zeros((3, HALF, SIDE), np.float32)
    for lr in range(6):
        for wc in range(4):
            for cw in range(WIN_LON):
                u = wc * 72 + lr * WIN_LON + cw
                col = WIN_LON * wc + WIN_LON // 2 + cw
                if col < 48:
                    to_win[u, lr * 48 + col] = from_win[lr * 48 + col, u] = 1.0
                else:
                    at = lr * 6 + col - 48
                    from_win[HALF + at, u] = 1.0
                    for half in range(4):
                        edge_in[half, u - 216, half * EDGE + at if half < 3 else 12 + at] = 1.0
        for c in range(6):
            pack[lr * 6 + c, lr * 48 + c] = 1.0
            for half in range(3):
                unpack[half, lr * 48 + c, half * EDGE + lr * 6 + c] = 1.0
    return to_win, from_win, edge_in, pack, unpack, pack.T


def nn(a, b):
    return lax.dot_general(a, b, (((1,), (0,)), ((), ())), preferred_element_type=F32)


def nt(a, b):
    return lax.dot_general(a, b, (((1,), (1,)), ((), ())), preferred_element_type=F32)


def tn(a, b):
    return lax.dot_general(a, b, (((0,), (0,)), ((), ())), preferred_element_type=F32)


def take(ref, rows):
    return jnp.concatenate([ref[c, rows, :] for c in range(4)], 1)


def put(ref, rows, value):
    for c in range(4):
        ref[c, rows, :] = value[:, c * 128:(c + 1) * 128]


def stats(x):
    average = jnp.mean(x, -1, keepdims=True)
    centred = x - average
    variance = jnp.mean(centred * centred, -1, keepdims=True)
    return centred, lax.rsqrt(variance + EPS)


def kernel(
    tokens, region, w_qkv_h, w_proj_h, w_merge_h, d_merged, to_win_h, from_win_h, edge_in_h, pack_h, unpack_h, corner_h,
    m_out, gx_out, gw_out,
    ext, side, corner, regions, region_s, region_e, region_se, keys, key_side, key_corner, key_loose, wq, wp, wm, dm_raw, dm_send, dm_recv, to_win, from_win, edge_in, pack, unpack, uncorner, loose, packed,
    xw, keyw, normed, q, k, v, block_q, block_d, staged, soft, mixed_t, normed_t, mixed, tmp, b_send, b_diag, b_lat, b_side, b_corner,
    grid_s, g, d_in, d_str, d_ext, d_side, d_corner, d_win, d_mix, d_qkv, merged, merged_in, merged_all,
    r_send, r_diag, r_lat, r_side, r_corner, gx_all,
    grads, core_send, core_recv, send1, recv1, send2, recv2, total,
    local_sem, halo_send, halo_recv, a2a_send, a2a_recv, ar_send, ar_recv,
):
    lat = lax.axis_index("lat")
    lon = lax.axis_index("lon")
    core = lax.rem(lat, 2)
    z_at = lax.rem(lax.div(lat, 2), 4)
    y_lo = lax.div(lat, 8)
    x_at = lax.div(lon, 2)
    y_at = lax.rem(lon, 2) * 2 + y_lo

    south = lax.rem(lat + 1, 16)
    north = lax.rem(lat + 15, 16)
    east = lax.rem(lon + 1, 8)
    west = lax.rem(lon + 7, 8)

    places = {"x": x_at, "y": y_at, "z": z_at}

    def moved_by(steps):
        x, y, z = [lax.rem(places[axis] + steps[axis], 4) if steps.get(axis) else places[axis] for axis in "xyz"]
        return (lax.rem(y, 2) * 8 + z * 2 + core, x * 2 + lax.div(y, 2))

    def on_z(by):
        return moved_by({"z": by})

    def on_y(by):
        return moved_by({"y": by})

    def on_x(by):
        return moved_by({"x": by})

    def on_plane(order, b2, b3):
        return moved_by({order[1]: b2, order[2]: b3})

    def local(i, src, dst):
        copy = pltpu.make_async_copy(src, dst, local_sem.at[i])
        copy.start()
        return copy

    def remote(src, dst, sends, recvs, i, to):
        copy = pltpu.make_async_remote_copy(
            src_ref=src, dst_ref=dst, send_sem=sends.at[i], recv_sem=recvs.at[i], device_id=to, device_id_type=MESH
        )
        copy.start()
        return copy

    started = []

    loads = []
    for hb in range(4):
        for lev in range(LEV):
            rows, place = pl.ds(hb * 144, 144), pl.ds(lev * 144, 144)
            loads.append(local(len(loads), tokens.at[lev, rows], ext.at[hb, place]))
    l_reg = local(8, region, regions)
    l_pack = local(9, pack_h, pack)

    barrier = pltpu.get_barrier_semaphore()
    peers = [(south, lon), (north, lon), (south, east), (north, west)]
    peers += [(lat, lax.rem(lon + by, 8)) for by in range(1, 8)]
    peers += [on_z(by) for by in (1, 2, 3)] + [on_y(by) for by in (1, 3)]
    for first, second in ("xy", "yz", "xz"):
        for b2 in range(1, 4):
            for b3 in range(1, 4):
                if (first, second, b3) != ("x", "y", 2):
                    peers.append(moved_by({first: b2, second: b3}))
    for peer in peers:
        pl.semaphore_signal(barrier, inc=1, device_id=peer, device_id_type=MESH)

    for copy in loads:
        copy.wait()
    later = ((to_win_h, to_win), (w_qkv_h, wq), (d_merged, dm_raw), (edge_in_h, edge_in), (w_proj_h, wp),
             (from_win_h, from_win), (unpack_h, unpack), (corner_h, uncorner), (w_merge_h, wm))
    l_to, l_wq, l_dm, l_edge, l_wp, l_from, l_un, l_corner, l_wm = [
        local(10 + i, src, dst) for i, (src, dst) in enumerate(later)
    ]
    l_reg.wait()
    l_pack.wait()

    def gather_edges(number, full):
        for i, hb in enumerate((1, 2, 3, 0)):
            loose[i * EDGE:(i + 1) * EDGE, :] = nn(pack[...], full[hb])[0:EDGE]
        packed[number] = loose[...].astype(BF)

    def send_halo(number, full, to_side, to_corner):
        out = [
            remote(full.at[0], full.at[4], halo_send, halo_recv, number * 3, (north, lon)),
            remote(packed.at[number, pl.ds(0, SIDE)], to_side, halo_send, halo_recv, number * 3 + 1, (lat, west)),
            remote(packed.at[number, pl.ds(96, PACK)], to_corner, halo_send, halo_recv, number * 3 + 2, (north, west)),
        ]
        started.extend(out)
        return out

    gather_edges(0, ext)
    pl.semaphore_wait(barrier, len(peers))
    halo = send_halo(0, ext, side, corner)
    for i, (there, to) in enumerate(((region_s, (north, lon)), (region_e, (lat, west)), (region_se, (north, west)))):
        halo.append(remote(regions, there, halo_send, halo_recv, 12 + i, to))
    started.extend(halo[3:])

    l_dm.wait()
    for s in range(8):
        part = dm_raw[:, s * 24:(s + 1) * 24, :].astype(F32)
        dm_send[s] = part.reshape(CELLS, 128).astype(BF)
    def window_rows(half, first, last, full, to_side, to_corner, wide):
        low_row, high_row = first * 72 // 16 * 16, -(-last * 72 // 16) * 16
        moved = nn(to_win[low_row:high_row, :], full[half + 1])
        for wc in range(first, last):
            at = ((half // 2) * 4 + wc) * WIN + (half % 2) * 72
            part = moved[wc * 72 - low_row:(wc + 1) * 72 - low_row, :]
            if wc == 3:
                if half == 3:
                    part = part + nn(edge_in[3, :, 0:PACK], to_corner[...])[0:72]
                else:
                    part = part + nn(edge_in[half], to_side[...])[0:72]
            wide[at:at + 72, :] = part

    diagonal = lax.broadcasted_iota(jnp.int32, (48, 48), 0) == lax.broadcasted_iota(jnp.int32, (48, 48), 1)

    def key_rows(source, first, extra):
        rows = []
        for row in range(first, first + 3):
            column = jnp.sum(jnp.where(diagonal, source[row:row + 1, :].astype(F32), 0.0), 1, keepdims=True)
            rows.append(jnp.broadcast_to(column + extra, (48, 128)))
        return jnp.concatenate(rows * LEV, 0).astype(BF)

    def norm_window(w, _):
        rows = pl.ds(pl.multiple_of(w * WIN, WIN), WIN)
        centred, inverse = stats(xw[rows, :])
        normed[rows, :] = (centred * inverse).astype(BF)
        return 0

    def project(rows):
        block = normed[rows, :]
        q[rows, :] = (nn(block, wq[:, 0:D]).astype(BF) * 0.125).astype(BF)
        k[rows, :] = nn(block, wq[:, D:2 * D]).astype(BF)
        v[rows, :] = nn(block, wq[:, 2 * D:3 * D]).astype(BF)

    def later_rows(i):
        return pl.ds(pl.multiple_of(3 * WIN + i * 240, 16), 240)

    def project_later(i, _):
        project(later_rows(i))
        return 0

    lane = lax.broadcasted_iota(jnp.int32, (WIN, 128), 1)
    low = lane < 64

    def spread(ref, rows, src, filler):
        blank = jnp.zeros((WIN, 128), BF)
        for head, first, last in SEGMENTS:
            chunk, at = first // 256, pl.ds(first, last - first)
            part = slice(first - head * WIN, last - head * WIN)
            own = src[rows, (head // 2) * 128:(head // 2 + 1) * 128]
            own = jnp.where(low if head % 2 == 0 else ~low, own, blank)
            block = head // 2 - CHUNK_LANE[chunk] // 128
            fill = blank if filler is None else filler
            if chunk == 0:
                ref[at, 0:128] = own[part]
                ref[at, 128:256] = fill[part]
            else:
                ref[at, 0:128] = (jnp.where(low, fill, own) if block == 0 else fill)[part]
                ref[at, 128:256] = (own if block == 1 else blank)[part]

    def by_heads(stage, left, right, chunk):
        out = tn(left, right[:, CHUNK_LANE[chunk]:CHUNK_LANE[chunk] + 256])
        for head, first, last in SEGMENTS:
            if first // 256 == chunk:
                block = head // 2 - CHUNK_LANE[chunk] // 128
                rows = slice(first - chunk * 256, last - chunk * 256)
                stage[first:last, :] = out[rows, block * 128:(block + 1) * 128]

    def joined(stage, pair):
        even, odd = 2 * pair * WIN, (2 * pair + 1) * WIN
        return jnp.where(low, stage[even:even + WIN, :], stage[odd:odd + WIN, :])

    def attend(w, q_b, stage):
        rows = pl.ds(pl.multiple_of(w * WIN, WIN), WIN)
        same = keyw[rows, :] == lane.astype(F32)
        differ = jnp.where(same | ~low, 0.0, 1.0).astype(BF)
        forbid = jnp.where(same, -1e30, 0.0).astype(BF)
        spread(q_b, rows, q, differ)
        k_b = [k[rows, i * 128:(i + 1) * 128] for i in range(4)]
        k_x = [jnp.concatenate([k_b[0], jnp.where(low, forbid, k_b[1])], 1)]
        k_x += [jnp.concatenate([jnp.where(low, forbid, k_b[i]), k_b[i + 1]], 1) for i in range(3)]
        values = v[rows, :]
        for chunk in range(5):
            cols = slice(chunk * 256, min(chunk * 256 + 256, 1152))
            raw = jnp.exp(nt(k_x[min(chunk, 3)], q_b[cols, :]))
            total_w = jnp.sum(raw, 0, keepdims=True)
            shrink = jnp.where(total_w > 1.0, 2.0 ** -32, 1.0)
            part = (raw * shrink) * (1.0 / (total_w * shrink))
            soft[w, :, cols] = part
            by_heads(stage, part.astype(BF), values, chunk)
        for pair in range(4):
            mixed[rows, pair * 128:(pair + 1) * 128] = joined(stage, pair).astype(BF)

    def attend_pair(i, _):
        attend(2 * i, block_q.at[0], staged.at[0])
        attend(2 * i + 1, block_q.at[1], staged.at[1])
        return 0

    l_to.wait()
    for half in range(2):
        window_rows(half, 0, 3, ext, side, corner, xw)
    lax.fori_loop(0, 3, norm_window, 0)
    for half in range(3):
        keys[half + 1] = key_rows(regions, 3 * half + 3, 0.0)
    for half in range(2):
        window_rows(half, 0, 3, keys, key_side, key_corner, keyw)
    l_wq.wait()
    project(slice(0, 3 * WIN))
    mine = pl.ds(pl.multiple_of(lon * 128, 128), 128)
    a2a_in = []

    def send_cotangents(steps):
        for by in steps:
            to = lax.rem(lon + by, 8)
            copy = remote(dm_send.at[to], dm_recv.at[:, mine], a2a_send, a2a_recv, by - 1, (lat, to))
            a2a_in.append(copy)
            started.append(copy)

    send_cotangents((2, 4, 6))
    dm_recv[:, mine] = dm_send[lon]
    attend_pair(0, 0)
    attend(2, block_q.at[0], staged.at[0])

    for copy in halo:
        copy.wait_recv()
    send_cotangents((1, 3, 5, 7))
    l_edge.wait()
    edge_key = jnp.where(lat == 15, 4.0, 0.0)
    keys[4] = key_rows(region_s, 0, edge_key)
    for half in range(4):
        near = key_rows(region_e, 3 * half + 3, 0.0) if half < 3 else key_rows(region_se, 0, edge_key)
        key_loose[half * EDGE:(half + 1) * EDGE, :] = nn(pack[...], near)[0:EDGE]
    key_side[...] = key_loose[0:SIDE, :].astype(BF)
    key_corner[...] = key_loose[96:, :].astype(BF)
    for half in range(4):
        first = 3 if half < 2 else 0
        window_rows(half, first, 4, ext, side, corner, xw)
        window_rows(half, first, 4, keys, key_side, key_corner, keyw)
    lax.fori_loop(3, 8, norm_window, 0)
    lax.fori_loop(0, 3, project_later, 0)
    lax.fori_loop(2, 4, attend_pair, 0)

    l_wp.wait()
    l_from.wait()
    l_un.wait()
    l_corner.wait()

    def to_grid(half, number, lat_send, lat_recv, diag_send, to_side, to_corner, keep):
        first = (half // 2) * 4
        block = jnp.concatenate([tmp[(first + wc) * WIN + (half % 2) * 72:(first + wc) * WIN + (half % 2) * 72 + 72, :] for wc in range(4)], 0)
        moved = nn(from_win[...], block.astype(BF))
        out = []
        if half == 3:
            loose[3 * EDGE:, :] = jnp.zeros((EDGE, D), F32)
            diag_send[...] = moved[HALF:, :].astype(BF)
            lat_send[...] = moved[:HALF, :].astype(BF)
            out.append((lat_send, lat_recv, number * 3, (south, lon)))
            out.append((diag_send, to_corner, number * 3 + 2, (south, east)))
        else:
            put(keep, slice((half + 1) * HALF, (half + 2) * HALF), moved[:HALF, :])
            loose[half * EDGE:(half + 1) * EDGE, :] = moved[HALF:HALF + EDGE, :]
        if half == 0:
            packed[number] = loose[...].astype(BF)
            sides = packed.at[number, pl.ds(0, SIDE)]
            out.append((sides, to_side, number * 3 + 1, (lat, east)))
        return out

    def launch(parts):
        out = [remote(src, dst, halo_send, halo_recv, i, to) for src, dst, i, to in parts]
        started.extend(out)
        return out

    def from_edges(hb, to_side, to_corner):
        return nn(uncorner[...], to_corner[...]) if hb == 0 else nn(unpack[hb - 1], to_side[...])

    branch_halo = []
    for band in (1, 0):
        if band == 0:
            attend(3, block_q.at[0], staged.at[0])
        rows = slice(band * 576, (band + 1) * 576)
        tmp[rows, :] = nn(mixed[rows, :], wp[...])
        for half in (band * 2 + 1, band * 2):
            branch_halo += launch(to_grid(half, 1, b_send, b_lat, b_diag, b_side, b_corner, grid_s))

    l_wm.wait()
    for copy in a2a_in:
        copy.wait_recv()

    def d_in_part(p, _):
        d_in[p] = nt(dm_recv[...], wm[pl.ds(pl.multiple_of(p * D, D), D), :])
        return 0

    lax.fori_loop(0, 4, d_in_part, 0)
    for i in range(9):
        rows = slice(i * 128, (i + 1) * 128)
        normed_t[:, rows] = normed[rows, :].T
        mixed_t[:, rows] = mixed[rows, :].T

    for copy in branch_halo:
        copy.wait_recv()
    for hb in range(4):
        at = slice(hb * HALF, (hb + 1) * HALF)
        own = b_lat[...].astype(F32) if hb == 0 else take(grid_s, at)
        full = own + from_edges(hb, b_side, b_corner)
        put(grid_s, at, (ext[hb].astype(F32) + full).astype(BF).astype(F32))

    def cell_rows(p, lev, i):
        row = 2 * i + p % 2
        return ((row // 3 * 2 + lev) * 3 + row % 3) * 48 + p // 2

    for p in range(4):
        for lev in range(LEV):
            for i in range(6):
                at = (lev * 6 + i) * 24
                g[p, at:at + 24, :] = take(grid_s, pl.ds(cell_rows(p, lev, i), 24, stride=2))

    average = sum(jnp.sum(g[p], -1, keepdims=True) for p in range(4)) / (4 * D)
    variance = 0.0
    for p in range(4):
        centred = g[p] - average
        variance = variance + jnp.sum(centred * centred, -1, keepdims=True)
    inverse = lax.rsqrt(variance / (4 * D) + EPS)
    mean_d = sum(jnp.sum(d_in[p], -1, keepdims=True) for p in range(4)) / (4 * D)
    mean_dh = sum(jnp.sum(d_in[p] * ((g[p] - average) * inverse), -1, keepdims=True) for p in range(4)) / (4 * D)
    for p in range(4):
        hat = (g[p] - average) * inverse
        d_part = inverse * (d_in[p] - mean_d - hat * mean_dh)
        g[p] = hat
        for lev in range(LEV):
            for i in range(6):
                at = (lev * 6 + i) * 24
                put(d_str, pl.ds(cell_rows(p, lev, i), 24, stride=2), d_part[at:at + 24, :])

    for hb in range(4):
        d_ext[hb] = take(d_str, slice(hb * HALF, (hb + 1) * HALF)).astype(BF)
    gather_edges(2, d_ext)
    d_halo = send_halo(2, d_ext, d_side, d_corner)

    for n in range(2):
        cols = slice(n * 512, (n + 1) * 512)
        sums = nn(g[0].astype(BF), wm[0:D, cols])
        for p in range(1, 4):
            sums = sums + nn(g[p].astype(BF), wm[p * D:(p + 1) * D, cols])
        for s in range(4):
            merged[n * 4 + s] = sums[:, s * 128:(s + 1) * 128].astype(BF)
    merged_out = []

    def send_merged(steps):
        for by in steps:
            to = lax.rem(lon + by, 8)
            copy = remote(merged.at[to], merged_in.at[lon], a2a_send, a2a_recv, 6 + by, (lat, to))
            merged_out.append(copy)
            started.append(copy)

    send_merged((2, 4, 6))
    merged_in[lon] = merged[lon]

    def back(rows):
        block = tmp[rows, :].astype(BF)
        d_win[rows, :] = block
        d_mix[rows, :] = nt(block, wp[...]).astype(BF)

    def back_later(i, _):
        back(later_rows(i))
        return 0

    def attend_back(w, q_b, d_b, stage):
        rows = pl.ds(pl.multiple_of(w * WIN, WIN), WIN)
        spread(q_b, rows, q, None)
        spread(d_b, rows, d_mix, None)
        keys, values = k[rows, :], v[rows, :]
        d_k, d_v = [], []
        for chunk in range(5):
            cols = slice(chunk * 256, min(chunk * 256 + 256, 1152))
            part = soft[w, :, cols]
            d_soft = nt(values[:, CHUNK_LANE[chunk]:CHUNK_LANE[chunk] + 256], d_b[cols, :])
            delta = jnp.sum(part * d_soft, 0, keepdims=True)
            d_s = (part * (d_soft - delta)).astype(BF)
            d_v.append(nn(part.astype(BF), d_b[cols, :]))
            d_k.append(nn(d_s, q_b[cols, :]))
            by_heads(stage, d_s, keys, chunk)
        for which, d in ((1, d_k), (2, d_v)):
            both = [d[0][:, 0:128] + d[1][:, 0:128], d[1][:, 128:256] + d[2][:, 0:128],
                    d[2][:, 128:256] + d[3][:, 0:128] + d[4][:, 0:128], d[3][:, 128:256] + d[4][:, 128:256]]
            for pair in range(4):
                d_qkv[rows, which * D + pair * 128:which * D + (pair + 1) * 128] = both[pair].astype(BF)
        for pair in range(4):
            d_qkv[rows, pair * 128:(pair + 1) * 128] = (joined(stage, pair) * 0.125).astype(BF)

    def attend_back_pair(i, _):
        attend_back(2 * i, block_q.at[0], block_d.at[0], staged.at[0])
        attend_back(2 * i + 1, block_q.at[1], block_d.at[1], staged.at[1])
        return 0

    orders = (("z", "y", "x"), ("y", "x", "z"), ("x", "z", "y"), ("z", "x", "y"))
    along = {"z": (on_z, z_at), "y": (on_y, y_at), "x": (on_x, x_at)}
    acc1 = d_in
    other = (lat + 1 - 2 * core, lon)
    half_at = pl.multiple_of(core * 256, 256)
    away_at = pl.multiple_of((1 - core) * 256, 256)
    factor = float(LEV * 192 * 384) ** -0.5
    outs = []

    def summed(m):
        (move1, at1), (_, at2), (_, at3) = [along[axis] for axis in orders[m]]

        def send(i, src, dst, to):
            copy = remote(src, dst, ar_send, ar_recv, m * 41 + i, to)
            started.append(copy)
            return copy

        core_send[m] = grads[m, pl.ds(away_at, 256), :].astype(BF)
        flying = [send(0, core_send.at[m], core_recv.at[m], other)]
        yield
        flying[0].wait_recv()
        acc1[m, 0:256, :] = grads[m, pl.ds(half_at, 256), :] + core_recv[m].astype(F32)
        send1[m] = acc1[m, 0:256, :].astype(BF)
        flying = []
        for by in range(1, 4):
            rows = pl.ds(pl.multiple_of(lax.rem(at1 + by, 4) * 64, 64), 64)
            flying.append(send(by, send1.at[m, rows], recv1.at[m, by - 1], move1(by)))
        yield
        for copy in flying:
            copy.wait_recv()
        own = acc1[m, pl.ds(pl.multiple_of(at1 * 64, 64), 64), :]
        for j in range(3):
            own = own + recv1[m, j].astype(F32)
        send2[m] = own.astype(BF)
        acc1[m, 0:64, :] = own
        rest = [(b2, b3) for b2 in range(4) for b3 in range(4) if (b2, b3) != (0, 0)]
        flying = []
        for i, (b2, b3) in enumerate(rest):
            rows = pl.ds(pl.multiple_of(lax.rem(at2 + b2, 4) * 16, 16), 16)
            cols = pl.ds(pl.multiple_of(lax.rem(at3 + b3, 4) * 128, 128), 128)
            flying.append(send(4 + i, send2.at[m, rows, cols], recv2.at[m, i], on_plane(orders[m], b2, b3)))
        yield
        for copy in flying:
            copy.wait_recv()
        row1 = core * 256
        row2 = row1 + at1 * 64
        row3 = row2 + at2 * 16
        rows2, rows3 = [pl.ds(pl.multiple_of(r, n), n) for r, n in ((row2, 64), (row3, 16))]
        cols = pl.ds(pl.multiple_of(at3 * 128, 128), 128)
        own = acc1[m, pl.ds(pl.multiple_of(at2 * 16, 16), 16), cols]
        for j in range(15):
            own = own + recv2[m, j].astype(F32)
        total[m, rows3, cols] = (own * factor).astype(BF)
        piece = total.at[m, rows3, cols]
        flying = [send(19 + i, piece, piece, on_plane(orders[m], b2, b3)) for i, (b2, b3) in enumerate(rest)]
        yield
        for copy in flying:
            copy.wait_recv()
        flying = [send(33 + by, total.at[m, rows2], total.at[m, rows2], move1(by)) for by in range(1, 4)]
        crossing = [send(37, total.at[m, rows2], total.at[m, rows2], other)]
        yield
        for by, copy in enumerate(flying, 1):
            copy.wait_recv()
            rows = pl.ds(pl.multiple_of(row1 + lax.rem(at1 + 4 - by, 4) * 64, 64), 64)
            crossing.append(send(37 + by, total.at[m, rows], total.at[m, rows], other))
        yield
        for copy in crossing:
            copy.wait_recv()
        outs.append(local(m, total.at[m], gw_out.at[:, pl.ds(m * D, D)]))
        yield

    for half in range(2):
        window_rows(half, 0, 3, d_ext, d_side, d_corner, tmp)
    back(slice(0, 3 * WIN))
    attend_back_pair(0, 0)
    attend_back(2, block_q.at[0], block_d.at[0], staged.at[0])
    for copy in d_halo:
        copy.wait_recv()
    send_merged((1, 3, 5, 7))
    for half in range(4):
        window_rows(half, 3 if half < 2 else 0, 4, d_ext, d_side, d_corner, tmp)
    lax.fori_loop(0, 3, back_later, 0)
    grads[0] = nn(mixed_t[...], d_win[...])
    sums = [summed(0)]
    next(sums[0])
    attend_back_pair(2, 0)
    next(sums[0])
    attend_back_pair(3, 0)
    attend_back(3, block_q.at[0], block_d.at[0], staged.at[0])

    proj_sum = sums.pop()
    for m in range(3):
        grads[m + 1] = nn(normed_t[...], d_qkv[:, m * D:(m + 1) * D])
        sums.append(summed(m + 1))
        next(sums[m])
    sums.append(proj_sum)

    def norm_back_band(band, _):
        rows = pl.ds(pl.multiple_of(band * 576, 576), 576)
        d_norm = nt(d_qkv[rows, :], wq[...])
        centred, inverse = stats(xw[rows, :])
        hat = centred * inverse
        tmp[rows, :] = inverse * (
            d_norm - jnp.mean(d_norm, -1, keepdims=True) - hat * jnp.mean(d_norm * hat, -1, keepdims=True)
        )
        return 0

    roll_parts = []
    for band in (1, 0):
        norm_back_band(band, 0)
        if band == 1:
            for step in sums:
                next(step)
        for half in (band * 2 + 1, band * 2):
            roll_parts += to_grid(half, 3, r_send, r_lat, r_diag, r_side, r_corner, grid_s)
    for step in sums:
        next(step)
    roll_halo = launch(roll_parts)

    for copy in merged_out:
        copy.wait_recv()
    for s in range(8):
        merged_all[:, s * 24:(s + 1) * 24, :] = merged_in[s].astype(F32).reshape(12, 24, 128)
    dm_raw[...] = merged_all[...].astype(BF)
    outs.append(local(4, dm_raw, m_out))
    for _ in range(2):
        for step in sums:
            next(step)

    for copy in roll_halo:
        copy.wait_recv()
    for hb in range(4):
        at = slice(hb * HALF, (hb + 1) * HALF)
        own = r_lat[...].astype(F32) if hb == 0 else take(grid_s, at)
        gx_all[hb] = (take(d_str, at) + own + from_edges(hb, r_side, r_corner)).astype(BF)
        for lev in range(LEV):
            src = gx_all.at[hb, pl.ds(lev * 144, 144)]
            outs.append(local(5 + hb * 2 + lev, src, gx_out.at[lev, pl.ds(hb * 144, 144)]))
    for _ in range(8):
        for step in sums:
            next(step, None)

    for copy in started:
        copy.wait_send()
    for copy in outs:
        copy.wait()


def finish(m_in, gx_in, gw_in, m_out, gx_out, gq_out, gp_out, m_v, gx_v, gx_wide, gw_v, wide, in_sem, out_sem):
    ins, outs = [], []

    def start(sems, held, src, dst):
        copy = pltpu.make_async_copy(src, dst, sems.at[len(held)])
        copy.start()
        held.append(copy)

    quarters = [pl.ds(i * 128, 128) for i in range(4)]
    halves = [(lev, pl.ds(i * 288, 288)) for lev in range(LEV) for i in range(2)]
    for rows in quarters:
        start(in_sem, ins, gw_in.at[rows], gw_v.at[rows])
    for at in halves:
        start(in_sem, ins, gx_in.at[at], gx_v.at[at])
    start(in_sem, ins, m_in, m_v)
    for i, rows in enumerate(quarters):
        ins[i].wait()
        wide[rows, :] = gw_v[rows, :].astype(F32)
        start(out_sem, outs, wide.at[rows, pl.ds(D, 3 * D)], gq_out.at[rows])
        start(out_sem, outs, wide.at[rows, pl.ds(0, D)], gp_out.at[rows])
    for i, at in enumerate(halves):
        ins[4 + i].wait()
        gx_wide[at] = gx_v[at].astype(F32)
        start(out_sem, outs, gx_wide.at[at], gx_out.at[at])
    ins[8].wait()
    start(out_sem, outs, m_v, m_out)
    for copy in outs:
        copy.wait()


def vmem(*shape, dtype=BF):
    return pltpu.VMEM(shape, dtype)


SCRATCH = [
    vmem(5, HALF, D), vmem(SIDE, D), vmem(PACK, D)] + [vmem(12, 48, dtype=jnp.int32)] * 4 + [
    vmem(5, HALF, 128), vmem(SIDE, 128), vmem(PACK, 128), vmem(4 * EDGE, 128, dtype=F32), vmem(D, 3 * D), vmem(D, D), vmem(4 * D, D2),
    vmem(12, 192, 128), vmem(8, CELLS, 128), vmem(CELLS, D2), vmem(HALF, HALF), vmem(HALF + PACK, HALF), vmem(4, 80, SIDE),
    vmem(PACK, HALF), vmem(3, HALF, SIDE), vmem(HALF, PACK), vmem(4 * EDGE, D, dtype=F32), vmem(4, 4 * EDGE, D),
    vmem(TOK, D, dtype=F32), vmem(TOK, 128, dtype=F32), vmem(TOK, D), vmem(TOK, D), vmem(TOK, D), vmem(TOK, D),
    vmem(2, 1152, 256), vmem(2, 1152, 256), vmem(2, 1152, 128, dtype=F32), vmem(8, WIN, 1152, dtype=F32), vmem(D, TOK), vmem(D, TOK), vmem(TOK, D), vmem(TOK, D, dtype=F32),
    vmem(HALF, D), vmem(PACK, D), vmem(HALF, D), vmem(SIDE, D), vmem(PACK, D),
    vmem(4, TOK, 128, dtype=F32), vmem(4, CELLS, D, dtype=F32), vmem(4, CELLS, D, dtype=F32), vmem(4, TOK, 128, dtype=F32),
    vmem(5, HALF, D), vmem(SIDE, D), vmem(PACK, D), vmem(TOK, D), vmem(TOK, D), vmem(TOK, 3 * D), vmem(8, CELLS, 128), vmem(8, CELLS, 128), vmem(12, 192, 128, dtype=F32),
    vmem(HALF, D), vmem(PACK, D), vmem(HALF, D), vmem(SIDE, D), vmem(PACK, D), vmem(4, HALF, D),
    vmem(4, D, D, dtype=F32), vmem(4, 256, D), vmem(4, 256, D), vmem(4, 256, D),
    vmem(4, 3, 64, D), vmem(4, 64, D), vmem(4, 15, 16, 128), vmem(4, D, D),
    pltpu.SemaphoreType.DMA((38,)), pltpu.SemaphoreType.DMA((15,)), pltpu.SemaphoreType.DMA((15,)),
    pltpu.SemaphoreType.DMA((14,)), pltpu.SemaphoreType.DMA((14,)),
    pltpu.SemaphoreType.DMA((164,)), pltpu.SemaphoreType.DMA((164,)),
]


def per_device(tokens, region, w_qkv, w_proj, w_merge, d_merged):
    levels, lat_rows, lon_cols, feature = tokens.shape
    consts = [jnp.asarray(a, BF) for a in one_hots()]
    anywhere = pl.BlockSpec(memory_space=pl.ANY)
    m_out, gx_out, gw_out = pl.pallas_call(
        kernel,
        out_shape=(
            jax.ShapeDtypeStruct((12, 192, 128), BF),
            jax.ShapeDtypeStruct((levels, 576, feature), BF),
            jax.ShapeDtypeStruct((D, 4 * D), BF),
        ),
        in_specs=[anywhere] * 12,
        out_specs=(anywhere,) * 3,
        scratch_shapes=SCRATCH,
        compiler_params=pltpu.CompilerParams(
            collective_id=0, has_side_effects=True, vmem_limit_bytes=64 * 1024 * 1024
        ),
    )(
        tokens.reshape(levels, 576, feature), region, w_qkv, w_proj, w_merge,
        d_merged.reshape(12, 192, 128), *consts,
    )
    merged, grad_x, grad_qkv, grad_proj = pl.pallas_call(
        finish,
        out_shape=(
            jax.ShapeDtypeStruct((12, 192, 128), BF),
            jax.ShapeDtypeStruct((levels, 576, feature), F32),
            jax.ShapeDtypeStruct((D, 3 * D), F32),
            jax.ShapeDtypeStruct((D, D), F32),
        ),
        in_specs=[anywhere] * 3,
        out_specs=(anywhere,) * 4,
        scratch_shapes=[
            vmem(12, 192, 128), vmem(LEV, 576, D), vmem(LEV, 576, D, dtype=F32), vmem(D, 4 * D), vmem(D, 4 * D, dtype=F32),
            pltpu.SemaphoreType.DMA((9,)), pltpu.SemaphoreType.DMA((13,)),
        ],
        compiler_params=pltpu.CompilerParams(vmem_limit_bytes=64 * 1024 * 1024),
    )(m_out, gx_out, gw_out)
    return (
        merged.reshape(levels, 6, 192, 128), grad_x.reshape(levels, lat_rows, lon_cols, feature), grad_qkv, grad_proj
    )


def solution(mesh):
    in_specs = (
        P(None, "lat", "lon", None),
        P("lat", "lon"),
        P(),
        P(),
        P(),
        P(None, "lat", None, "lon"),
    )
    out_specs = (P(None, "lat", None, "lon"), P(None, "lat", "lon", None), P(), P())
    return jax.shard_map(
        per_device, mesh=mesh, in_specs=in_specs, out_specs=out_specs, check_vma=False
    )
```
